32 devices in a mesh: dp: 8 (over y, x, core), tensor: 4 (over z).
Axes of the slice: x: 2, y: 2, z: 4, core: 2. Of those that a mesh axis runs over, the one named last changes fastest.
Arguments:
- train_hidden: bfloat16 [64, 128, 14336], P('dp', None, 'tensor')
- train_grads: bfloat16 [64, 128, 4096], P('dp', None, 'tensor'), may hold values from -6 to 6
- train_ids: int32 [64, 128], P('dp'), may hold values from 0 to 128004, as said below
- query_hidden: bfloat16 [16, 128, 14336], P(None, 'dp', 'tensor')
- query_grads: bfloat16 [16, 128, 4096], P(None, 'dp', 'tensor'), may hold values from -6 to 6
- query_ids: int32 [16, 128], P(None, 'dp'), may hold values from 0 to 128004, as said below
- proj_in: bfloat16 [14336, 64], P('tensor'), may hold values from -0.046875 to 0.046875
- proj_out: bfloat16 [4096, 64], P('tensor'), may hold values from -0.09375 to 0.09375
Outputs:
- scores: float32 [16, 64], P(None, ('dp', 'tensor'))
The draws below stay inside these ranges and needn't reach their ends.
Inputs may be any that keep to these rules, and one draw needn't show every extreme that they name: `train_ids`: id 128004 marks padding and appears only at the end of a sequence; the first 32 tokens of every training sequence are not padding; other ids lie below 128000. `query_ids`: id 128004 marks padding and appears only at the end of a query; the first 32 tokens of every query are not padding; other ids lie below 128000.
All inputs are finite; a program needn't handle non-finite values.
Results may differ from the reference program's by a relative error of at most 0.0003.
Values sent between devices are 32-bit elements; how exact they have to be, the bound alone decides.
No kernel may reach another device: no remote copies, remote signals or barrier semaphores. Data moves between devices by JAX's collectives and lax.ppermute only.
A program may use at most 128 MiB of HBM per device.

```python
import math
import jax
import jax.numpy as jnp
from jax import lax

D = 4096
FF = 14336
RANK = 64
LEN = 128
QUERIES = 16
ITERS = 3
TRAIN = 64
QLEN = 128
FEAT = 4096


def padded_ids(key, count, length):
    first, second = jax.random.split(key)
    lengths = jax.random.randint(first, (count, 1), length // 4, length + 1)
    tokens = jax.random.randint(second, (count, length), 0, 128000)
    places = jnp.arange(length)[None, :]
    return jnp.where(places < lengths, tokens, 128004).astype(jnp.int32)


def draw_train_ids(key, part):
    key = jax.random.fold_in(key, 11)
    return padded_ids(key, TRAIN, LEN)


def draw_query_ids(key, part):
    key = jax.random.fold_in(key, 12)
    return padded_ids(key, QUERIES, QLEN)


def draw_train_hidden(key, part):
    key = jax.random.fold_in(key, 21)
    first, second, third = jax.random.split(key, 3)
    rising = 3.0 ** (jnp.arange(TRAIN, dtype=jnp.float32) / TRAIN)
    rows = rising * jnp.exp(jax.random.uniform(first, (TRAIN,), jnp.float32, 0.0, math.log(3.4)))
    columns = jnp.exp(jax.random.uniform(second, (FF,), jnp.float32, math.log(0.5), math.log(2.0)))
    base = jax.random.normal(third, (TRAIN, LEN, FF), jnp.float32)
    return (base * rows[:, None, None] * columns[None, None, :]).astype(jnp.bfloat16)


def draw_query_hidden(key, part):
    key = jax.random.fold_in(key, 22)
    first, second, third = jax.random.split(key, 3)
    rising = 3.0 ** (jnp.arange(QLEN, dtype=jnp.float32) / QLEN)
    places = rising * jnp.exp(jax.random.uniform(first, (QLEN,), jnp.float32, 0.0, math.log(3.4)))
    columns = jnp.exp(jax.random.uniform(second, (FF,), jnp.float32, math.log(0.5), math.log(2.0)))
    base = jax.random.normal(third, (QUERIES, QLEN, FF), jnp.float32)
    return (base * places[None, :, None] * columns[None, None, :]).astype(jnp.bfloat16)


def steps_of(stream_key, shape, shards, smallest, largest):
    level, own = 1.0, jax.random.fold_in(stream_key, 6)
    for axis_at, parts in shards:
        heights = jnp.exp(jax.random.uniform(jax.random.fold_in(own, axis_at), (parts,), jnp.float32, smallest / len(shards), largest / len(shards)))
        level = level * jnp.repeat(heights, shape[axis_at] // parts).reshape([-1 if axis == axis_at else 1 for axis in range(len(shape))])
    return level


def scatter_about(rng, dims, width, most, cuts=(), kind=jnp.bfloat16):
    level = steps_of(rng, dims, cuts, -0.22, 0.18) if cuts else 1.0
    array = jax.random.normal(rng, dims, jnp.float32) * width * level
    return jnp.minimum(jnp.maximum(array, -most), most).astype(kind)


def setup_inputs(seed: int = 0) -> dict:
    keys = jax.random.split(jax.random.key(seed), 9)
    train_hidden = draw_train_hidden(jax.random.fold_in(keys[8], 71), 0)
    train_grads = scatter_about(keys[1], (TRAIN, LEN, D), 1.0, 6.0, ((0, 8), (2, 4)))
    train_ids = draw_train_ids(jax.random.fold_in(keys[8], 71), 0)
    query_hidden = draw_query_hidden(jax.random.fold_in(keys[8], 71), 0)
    query_grads = scatter_about(keys[4], (QUERIES, QLEN, D), 1.0, 6.0, ((1, 8), (2, 4)))
    query_ids = draw_query_ids(jax.random.fold_in(keys[8], 71), 0)
    proj_in = scatter_about(keys[6], (FF, RANK), FF ** -0.5, 0.046875, ((0, 4),))
    proj_out = scatter_about(keys[7], (D, RANK), D ** -0.5, 0.09375, ((0, 4),))
    return {"train_hidden": train_hidden, "train_grads": train_grads, "train_ids": train_ids, "query_hidden": query_hidden, "query_grads": query_grads, "query_ids": query_ids, "proj_in": proj_in, "proj_out": proj_out}


PAD_ID = 128004
DAMP = 0.1


def one_gradient(hidden, grads, ids, proj_in, proj_out):
    mask = (ids != PAD_ID).astype(jnp.float32)
    side_in = jnp.dot(hidden, proj_in, preferred_element_type=jnp.float32)
    side_out = jnp.dot(grads, proj_out, preferred_element_type=jnp.float32)
    outer = jnp.dot((side_in * mask[:, None]).T, side_out, precision=lax.Precision.HIGHEST)
    return outer.reshape(-1) / jnp.sum(mask)


def reference(train_hidden, train_grads, train_ids, query_hidden, query_grads, query_ids, proj_in, proj_out):
    def per_train(item):
        return one_gradient(item[0], item[1], item[2], proj_in, proj_out)

    examples = lax.map(per_train, (train_hidden, train_grads, train_ids))
    queries = lax.map(per_train, (query_hidden, query_grads, query_ids))
    trace = jnp.sum(examples * examples) / TRAIN
    damping = DAMP * trace / FEAT

    def apply(direction):
        inner = jnp.dot(direction, examples.T, precision=lax.Precision.HIGHEST)
        term = jnp.dot(inner, examples, precision=lax.Precision.HIGHEST)
        return direction + term / (TRAIN * damping)

    solved = jnp.zeros_like(queries)
    residual = queries
    direction = queries
    norm_now = jnp.sum(residual * residual, axis=1)
    for step in range(ITERS):
        image = apply(direction)
        alpha = norm_now / jnp.sum(direction * image, axis=1)
        solved = solved + alpha[:, None] * direction
        residual = residual - alpha[:, None] * image
        fresh = jnp.sum(residual * residual, axis=1)
        direction = residual + (fresh / norm_now)[:, None] * direction
        norm_now = fresh
    return jnp.dot(solved, examples.T, precision=lax.Precision.HIGHEST)
```

```python
import functools

import jax
import jax.numpy as jnp
from jax import lax
from jax.experimental import pallas as pl
from jax.experimental.pallas import tpu as pltpu
from jax.sharding import PartitionSpec as P

ITERS = 3
PAD_ID = 128004
DAMP = 0.1
HIGHEST = lax.Precision.HIGHEST
F32 = jnp.float32
VMEM_LIMIT = 32 * 1024 * 1024
NT = (((1,), (1,)), ((), ()))
SMEM_SPEC = pl.BlockSpec(memory_space=pltpu.SMEM)
VMEM_SPEC = pl.BlockSpec(memory_space=pltpu.VMEM)
HBM_SPEC = pl.BlockSpec(memory_space=pltpu.HBM)


def call(kernel, out_shape, name, **kwargs):
    return pl.pallas_call(
        kernel,
        out_shape=out_shape,
        name=name,
        compiler_params=pltpu.CompilerParams(vmem_limit_bytes=VMEM_LIMIT),
        **kwargs,
    )


def swap(value, dp_flip, tensor_flip):
    groups, parts = lax.axis_size("dp"), lax.axis_size("tensor")
    flip = dp_flip * parts + tensor_flip
    return lax.ppermute(value, ("dp", "tensor"), [(i, i ^ flip) for i in range(groups * parts)])


def project_kernel(mesh, parts, hops, tile, at_ref, th_ref, tg_ref, qh_ref, qg_ref, pin_ref, pout_ref, *refs):
    out_refs = refs[: len(hops)]
    hid, grad, pin, pout, sems = refs[len(hops) :]
    at = at_ref[0]
    trows = th_ref.shape[0] // parts
    qrows = qh_ref.shape[0] // parts
    rows = trows + qrows
    rank = pin_ref.shape[0]
    sides = ((th_ref, qh_ref, hid, pin_ref, pin), (tg_ref, qg_ref, grad, pout_ref, pout))
    chunks = []
    for side, (_, _, buf, _, _) in enumerate(sides):
        start = 0
        while start < buf.shape[1]:
            size = min(2 * tile if not chunks else 4 * tile, buf.shape[1] - start)
            chunks.append((side, start, size))
            start += size
    copies = []
    for chunk, (side, start, size) in enumerate(chunks):
        train, query, buf, weight, held = sides[side]
        cols = pl.ds(start, size)
        pairs = [(weight.at[:, cols], held.at[:, cols])]
        for slot, hop in enumerate(hops):
            to = at ^ hop
            tsrc = pl.ds(pl.multiple_of(to * trows, trows), trows)
            qsrc = pl.ds(pl.multiple_of(to * qrows, qrows), qrows)
            pairs.append((train.at[tsrc, cols], buf.at[pl.ds(slot * rows, trows), cols]))
            pairs.append((query.at[qsrc, cols], buf.at[pl.ds(slot * rows + trows, qrows), cols]))
        copies.append(
            [pltpu.make_async_copy(src, dst, sems.at[chunk, k]) for k, (src, dst) in enumerate(pairs)]
        )
        for copy in copies[-1]:
            copy.start()

    def multiply(*sums):
        count = 0
        for (side, start, size), waits in zip(chunks, copies):
            _, _, buf, _, held = sides[side]
            for copy in waits:
                copy.wait()
            for col in range(start, start + size, tile):
                unit, turn = count % len(sums), count // len(sums)
                count += 1
                weight = [held[:, col : col + tile]]
                if side:
                    weight.insert(0, jnp.zeros((side * rank, tile), held.dtype))
                weight.append(jnp.zeros((tile - (side + 1) * rank, tile), held.dtype))
                weight = jnp.concatenate(weight, axis=0)
                pltpu.matmul_push_rhs(weight, turn % 2, unit, transpose=True)
                pltpu.matmul_acc_lhs(sums[unit], buf[:, col : col + tile], load_staged_rhs=turn % 2)
        total = pltpu.matmul_pop(sums[0])[:, : 2 * rank]
        for unit in sums[1:]:
            total = total + pltpu.matmul_pop(unit)[:, : 2 * rank]
        for slot, ref in enumerate(out_refs):
            ref[...] = total[slot * rows : (slot + 1) * rows]

    with jax.sharding.use_abstract_mesh(mesh.abstract_mesh):
        sums = [pltpu.ACC(unit)((hid.shape[0], tile), F32) for unit in range(2)]
        pl.run_scoped(multiply, *sums)


def project(mesh, at, arrays, parts, hops):
    train, _, query, _, pin, pout = arrays
    rank, ff = pin.shape
    width = pout.shape[1]
    rows = (train.shape[0] + query.shape[0]) // parts
    held = rows * len(hops)
    bf16 = jnp.bfloat16
    tile = 256
    return call(
        functools.partial(project_kernel, mesh, parts, hops, tile),
        [jax.ShapeDtypeStruct((rows, 2 * rank), F32)] * len(hops),
        "project_" + "_".join(str(hop) for hop in hops),
        in_specs=[SMEM_SPEC] + [HBM_SPEC] * 6,
        out_specs=[VMEM_SPEC] * len(hops),
        scratch_shapes=[
            pltpu.VMEM((held, ff), bf16),
            pltpu.VMEM((held, width), bf16),
            pltpu.VMEM((rank, ff), bf16),
            pltpu.VMEM((rank, width), bf16),
            pltpu.SemaphoreType.DMA((8, 1 + 2 * len(hops))),
        ],
        cost_estimate=pl.CostEstimate(
            flops=2 * held * (ff + width) * rank,
            bytes_accessed=2 * (held + rank) * (ff + width),
            transcendentals=0,
        ),
    )(at, *[pltpu.with_memory_space_constraint(array, pltpu.HBM) for array in arrays])


def fold(outer, start, half):
    return jnp.concatenate([outer[start : start + half], outer[start + half : start + 2 * half]], axis=1)


def outer_kernel(share, qshare, at_ref, quarter_ref, ids_ref, qids_ref, *refs):
    tok_refs, (keep_ref, send_ref, scratch) = refs[:-3], refs[-3:]
    at, mine = at_ref[0], quarter_ref[0]
    seq_len = ids_ref.shape[1]
    rank = tok_refs[0].shape[1] // 2
    qtok = qids_ref.shape[1]
    half = rank // 8

    def product(tokens, left):
        return jnp.dot(left, tokens[:, rank:], precision=HIGHEST, preferred_element_type=F32)

    def total(start, rows):
        value = tok_refs[0][start : start + rows, :]
        for ref in tok_refs[1:]:
            value = value + ref[start : start + rows, :]
        return value

    def store(slot, outer):
        for quarter in range(4):
            scratch[quarter, slot] = fold(outer, quarter * 2 * half, half)

    for seq in range(share):
        tokens = total(seq * seq_len, seq_len)
        mask = (ids_ref[pl.ds(at * share + seq, 1), :] != PAD_ID).astype(F32)
        outer = product(tokens, tokens.T[:rank] * mask)
        store(seq, outer / jnp.sum(mask, axis=1, keepdims=True))
    for quarter in range(4):
        scratch[quarter, share + qshare] = jnp.ones((half, 2 * rank), F32)
    for query in range(qshare):
        tokens = total(share * seq_len + query * qtok, qtok)
        mask = (qids_ref[pl.ds(at * qshare + query, 1), :] != PAD_ID).astype(F32)
        store(share + query, product(tokens, tokens.T[:rank] * mask))
        count = jnp.broadcast_to(jnp.sum(mask, axis=1, keepdims=True), (1, 2 * rank))
        for quarter in range(4):
            scratch[quarter, share + qshare, query : query + 1, :] = count
    for flip in range(2):
        keep_ref[flip] = scratch[mine ^ flip]
        send_ref[flip] = scratch[mine ^ 2 ^ flip]


def gram_kernel(qshare, at_ref, *refs):
    piece_refs, (out_ref, scratch) = refs[:-2], refs[-2:]
    at = at_ref[0]
    rows, half, lanes = piece_refs[0].shape
    nex = rows - qshare - 1
    ntrain = nex * len(piece_refs)
    nquery = scratch.shape[0]
    for hop, ref in enumerate(piece_refs):
        counts = ref[nex + qshare]
        for query in range(qshare):
            scratch[(at ^ hop) * qshare + query] = ref[nex + query] / counts[query : query + 1, :]
    total = None
    for row in range(half):
        both = jnp.concatenate(
            [ref[:nex, row, :] for ref in piece_refs] + [scratch[:, row, :]], axis=0
        )
        high = both.astype(jnp.bfloat16)
        low = (both - high.astype(F32)).astype(jnp.bfloat16)
        left = jnp.concatenate([high, low], axis=0)
        product = lax.dot_general(left, high, NT, preferred_element_type=F32)
        product = product + lax.dot_general(left, low, NT, preferred_element_type=F32)
        total = product if total is None else total + product
    size = ntrain + nquery
    total = total[:size] + total[size:]
    if folds(ntrain):
        half = ntrain // 2
        out_ref[:half, :] = jnp.concatenate([total[:half, :ntrain], total[half:ntrain, :ntrain]], axis=1)
        out_ref[half:, :size] = total[ntrain:]
        out_ref[half:, size:] = jnp.zeros((nquery, 2 * ntrain - size), F32)
    else:
        out_ref[...] = total


def folds(ntrain):
    return 2 * ntrain <= 128


def solve_kernel(ntrain, feat, share, low_ref, one_ref, two_ref, out_ref):
    nquery = out_ref.shape[0]
    whole = one_ref[...] + two_ref[...]
    if folds(ntrain):
        half = ntrain // 2
        gram = jnp.concatenate([whole[:half, :ntrain], whole[:half, ntrain:]], axis=0)
        rest = whole[half:]
    else:
        gram = whole[:ntrain, :ntrain]
        rest = whole[ntrain:]
    cross = rest[:, :ntrain]
    square = rest[:, ntrain : ntrain + nquery]

    def rowsum(v):
        return jnp.sum(v, axis=1, keepdims=True)

    def diagonal(v):
        rows = lax.broadcasted_iota(jnp.int32, v.shape, 0)
        cols = lax.broadcasted_iota(jnp.int32, v.shape, 1)
        return jnp.where(rows == cols, v, 0.0)

    norm = rowsum(diagonal(square))
    trace = jnp.sum(diagonal(gram)) / ntrain
    scale = 1.0 / (ntrain * (DAMP * trace / feat))

    res_a, res_x, res_p = jnp.ones_like(norm), jnp.zeros_like(cross), cross
    dir_a, dir_x, dir_p = res_a, res_x, res_p
    solved = jnp.zeros_like(cross)
    now = norm
    for step in range(ITERS):
        square = dir_a * dir_a * norm + dir_a * rowsum(dir_x * cross) + rowsum(dir_x * dir_p)
        alpha = now / (square + rowsum(dir_p * dir_p) * scale)
        solved = solved + alpha * dir_p
        if step == ITERS - 1:
            break
        res_a = res_a - alpha * dir_a
        res_x = res_x - alpha * (dir_x + dir_p * scale)
        res_p = res_a * cross + jnp.dot(
            res_x, gram, precision=HIGHEST, preferred_element_type=F32
        )
        fresh = res_a * res_a * norm + res_a * rowsum(res_x * cross) + rowsum(res_x * res_p)
        beta = fresh / now
        dir_a = res_a + beta * dir_a
        dir_x = res_x + beta * dir_x
        dir_p = res_p + beta * dir_p
        now = fresh
    low = low_ref[0]
    cols = lax.broadcasted_iota(jnp.int32, solved.shape, 1)
    mine = [rowsum(jnp.where(cols == low * share + seq, solved, 0.0)) for seq in range(share)]
    out_ref[...] = jnp.concatenate(mine, axis=1)


def per_device(
    mesh, train_hidden, train_grads, train_ids, query_hidden, query_grads, query_ids, proj_in, proj_out
):
    parts = lax.axis_size("tensor")
    groups = lax.axis_size("dp")
    at = lax.axis_index("tensor").astype(jnp.int32).reshape(1)
    group = lax.axis_index("dp").astype(jnp.int32)
    low = (group & 3).reshape(1)
    steady = at[0] >> 1
    for bit in range((groups - 1).bit_length()):
        steady = steady ^ (group >> bit)
    quarter = ((steady & 1) * 2 + (low >> 1)).reshape(1)
    nseq, seq_len, ff = train_hidden.shape
    width = train_grads.shape[2]
    rank = proj_in.shape[1]
    nquery, qtok, _ = query_hidden.shape
    ntrain = nseq * groups
    share = nseq // parts
    qshare = nquery // parts
    half = rank // 8

    arrays = (
        train_hidden.reshape(nseq * seq_len, ff),
        train_grads.reshape(nseq * seq_len, width),
        query_hidden.reshape(nquery * qtok, ff),
        query_grads.reshape(nquery * qtok, width),
        proj_in.T,
        proj_out.T,
    )
    pieces = {}
    turn = at
    for hops in ((3,), (2, 1, 0)):
        values = project(mesh, turn, arrays, parts, hops)
        turn, *values = lax.optimization_barrier((turn, *values))
        for hop, value in zip(hops, values):
            pieces[hop] = swap(value, 0, hop) if hop else value

    early = pieces[3] + pieces[0]
    rows = share + qshare + 1
    keep, send = call(
        functools.partial(outer_kernel, share, qshare),
        [jax.ShapeDtypeStruct((2, rows, half, 2 * rank), F32)] * 2,
        "outer",
        in_specs=[SMEM_SPEC] * 2 + [VMEM_SPEC] * 5,
        scratch_shapes=[pltpu.VMEM((4, rows, half, 2 * rank), F32)],
    )(at, quarter, train_ids, query_ids, early, pieces[2], pieces[1])

    def ordered(bit, mine, other):
        nex = mine.shape[-3] - qshare - 1
        first = jnp.where(bit == 0, mine, other)[..., :nex, :, :]
        second = jnp.where(bit == 0, other, mine)[..., :nex, :, :]
        return jnp.concatenate([first, second, (mine + other)[..., nex:, :, :]], axis=-3)

    both = ordered(low[0] & 1, keep, swap(send, 1, 0))
    block = ordered(low[0] >> 1, both[0], swap(both[1], 3, 0))
    flip = 4
    while flip < groups:
        block = ordered(0, block, swap(block, flip | 1, 0))
        flip *= 2
    blocks = [block] + [swap(block, hop >> 1, hop) for hop in range(1, parts)]
    size = ntrain + nquery
    shape = (ntrain // 2 + nquery, 2 * ntrain) if folds(ntrain) else (size, size)
    gram = call(
        functools.partial(gram_kernel, qshare),
        jax.ShapeDtypeStruct(shape, F32),
        "gram",
        in_specs=[SMEM_SPEC] + [VMEM_SPEC] * parts,
        scratch_shapes=[pltpu.VMEM((nquery, half, 2 * rank), F32)],
    )(at, *blocks)
    gram = gram + swap(gram, 3, 0)
    return call(
        functools.partial(solve_kernel, ntrain, rank * rank, share),
        jax.ShapeDtypeStruct((nquery, share), F32),
        "solve",
        in_specs=[SMEM_SPEC] + [VMEM_SPEC] * 2,
    )(low, gram, swap(gram, 1, 0))


def solution(mesh):
    return jax.shard_map(
        functools.partial(per_device, mesh),
        mesh=mesh,
        in_specs=(
            P("dp", None, "tensor"),
            P("dp", None, "tensor"),
            P("dp", None),
            P(None, "dp", "tensor"),
            P(None, "dp", "tensor"),
            P(None, "dp"),
            P("tensor", None),
            P("tensor", None),
        ),
        out_specs=P(None, ("dp", "tensor")),
        check_vma=False,
    )
```

```python
import functools

import jax
import jax.numpy as jnp
from jax import lax
from jax.experimental import pallas as pl
from jax.experimental.pallas import tpu as pltpu
from jax.sharding import PartitionSpec as P

ITERS = 3
PAD_ID = 128004
DAMP = 0.1
HIGHEST = lax.Precision.HIGHEST
F32 = jnp.float32
VMEM_LIMIT = 32 * 1024 * 1024
NT = (((1,), (1,)), ((), ()))
SMEM_SPEC = pl.BlockSpec(memory_space=pltpu.SMEM)
VMEM_SPEC = pl.BlockSpec(memory_space=pltpu.VMEM)
HBM_SPEC = pl.BlockSpec(memory_space=pltpu.HBM)


def call(kernel, out_shape, name, **kwargs):
    return pl.pallas_call(
        kernel,
        out_shape=out_shape,
        name=name,
        compiler_params=pltpu.CompilerParams(vmem_limit_bytes=VMEM_LIMIT),
        **kwargs,
    )


def swap(value, dp_flip, tensor_flip):
    groups, parts = lax.axis_size("dp"), lax.axis_size("tensor")
    flip = dp_flip * parts + tensor_flip
    return lax.ppermute(value, ("dp", "tensor"), [(i, i ^ flip) for i in range(groups * parts)])


def project_kernel(mesh, parts, hops, tile, at_ref, th_ref, tg_ref, qh_ref, qg_ref, pin_ref, pout_ref, *refs):
    out_refs = refs[: len(hops)]
    hid, grad, pin, pout, sems = refs[len(hops) :]
    at = at_ref[0]
    trows = th_ref.shape[0] // parts
    qrows = qh_ref.shape[0] // parts
    rows = trows + qrows
    rank = pin_ref.shape[0]
    sides = ((th_ref, qh_ref, hid, pin_ref, pin), (tg_ref, qg_ref, grad, pout_ref, pout))
    chunks = []
    started = 0
    for side, (train, query, buf, weight, held) in enumerate(sides):
        first = 4 * tile if side == 0 else buf.shape[1]
        for start, size in ((0, first), (first, buf.shape[1] - first)):
            if not size:
                continue
            cols = pl.ds(start, size)
            pairs = [] if start else [(weight, held)]
            for slot, hop in enumerate(hops):
                to = at ^ hop
                tsrc = pl.ds(pl.multiple_of(to * trows, trows), trows)
                pairs.append((train.at[tsrc, cols], buf.at[pl.ds(slot * rows, trows), cols]))
            for slot, hop in enumerate(() if start else hops):
                to = at ^ hop
                qsrc = pl.ds(pl.multiple_of(to * qrows, qrows), qrows)
                pairs.append((query.at[qsrc, :], buf.at[pl.ds(slot * rows + trows, qrows), :]))
            copies = []
            for src, dst in pairs:
                copies.append(pltpu.make_async_copy(src, dst, sems.at[started]))
                copies[-1].start()
                started += 1
            chunks.append((side, start, size, copies))

    def multiply(*sums):
        count = 0
        for side, start, size, copies in chunks:
            _, _, buf, _, held = sides[side]
            for copy in copies:
                copy.wait()
            for col in range(start, start + size, tile):
                unit, turn = count % len(sums), count // len(sums)
                count += 1
                weight = [held[:, col : col + tile]]
                if side:
                    weight.insert(0, jnp.zeros((side * rank, tile), held.dtype))
                weight.append(jnp.zeros((tile - (side + 1) * rank, tile), held.dtype))
                weight = jnp.concatenate(weight, axis=0)
                pltpu.matmul_push_rhs(weight, turn % 2, unit, transpose=True)
                pltpu.matmul_acc_lhs(sums[unit], buf[:, col : col + tile], load_staged_rhs=turn % 2)
        total = pltpu.matmul_pop(sums[0])[:, : 2 * rank]
        for unit in sums[1:]:
            total = total + pltpu.matmul_pop(unit)[:, : 2 * rank]
        for slot, ref in enumerate(out_refs):
            ref[...] = total[slot * rows : (slot + 1) * rows]

    with jax.sharding.use_abstract_mesh(mesh.abstract_mesh):
        sums = [pltpu.ACC(unit)((hid.shape[0], tile), F32) for unit in range(2)]
        pl.run_scoped(multiply, *sums)


def project(mesh, at, arrays, parts, hops):
    train, _, query, _, pin, pout = arrays
    rank, ff = pin.shape
    width = pout.shape[1]
    rows = (train.shape[0] + query.shape[0]) // parts
    held = rows * len(hops)
    bf16 = jnp.bfloat16
    tile = 256
    return call(
        functools.partial(project_kernel, mesh, parts, hops, tile),
        [jax.ShapeDtypeStruct((rows, 2 * rank), F32)] * len(hops),
        "project_" + "_".join(str(hop) for hop in hops),
        in_specs=[SMEM_SPEC] + [HBM_SPEC] * 6,
        out_specs=[VMEM_SPEC] * len(hops),
        scratch_shapes=[
            pltpu.VMEM((held, ff), bf16),
            pltpu.VMEM((held, width), bf16),
            pltpu.VMEM((rank, ff), bf16),
            pltpu.VMEM((rank, width), bf16),
            pltpu.SemaphoreType.DMA((2 + 5 * len(hops),)),
        ],
        cost_estimate=pl.CostEstimate(
            flops=2 * held * (ff + width) * rank,
            bytes_accessed=2 * (held + rank) * (ff + width),
            transcendentals=0,
        ),
    )(at, *[pltpu.with_memory_space_constraint(array, pltpu.HBM) for array in arrays])


def halves(value):
    high = value.astype(jnp.bfloat16)
    return high, (value - high.astype(F32)).astype(jnp.bfloat16)


def outer_kernel(share, qshare, at_ref, quarter_ref, ids_ref, qids_ref, *refs):
    tok_refs, (keep_ref, send_ref, scratch) = refs[:-3], refs[-3:]
    at, mine = at_ref[0], quarter_ref[0]
    seq_len = ids_ref.shape[1]
    rank = tok_refs[0].shape[1] // 2
    qtok = qids_ref.shape[1]
    half = rank // 8

    def total(start, rows):
        value = tok_refs[0][start : start + rows, :]
        for ref in tok_refs[1:]:
            value = value + ref[start : start + rows, :]
        return value

    def product(lefts, tokens):
        left = jnp.concatenate([part for value in lefts for part in halves(value)], axis=0)
        right = jnp.concatenate(halves(tokens), axis=1)
        out = jnp.dot(left, right, preferred_element_type=F32)
        out = out[:, : 2 * rank] + out[:, 2 * rank :]
        sums = []
        for index in range(len(lefts)):
            start = 2 * rank * index
            sums.append(out[start : start + rank] + out[start + rank : start + 2 * rank])
        return sums

    def store(slot, outer):
        for quarter in range(4):
            start = quarter * 2 * half
            scratch[quarter, slot] = jnp.concatenate(
                [outer[start : start + half, rank:], outer[start + half : start + 2 * half, rank:]],
                axis=1,
            )

    for seq in range(share):
        tokens = total(seq * seq_len, seq_len)
        mask = (ids_ref[pl.ds(at * share + seq, 1), :] != PAD_ID).astype(F32)
        (outer,) = product([tokens.T[:rank] * mask], tokens)
        store(seq, outer / jnp.sum(mask, axis=1, keepdims=True))

    for quarter in range(4):
        scratch[quarter, share + qshare] = jnp.ones((half, 2 * rank), F32)
    tokens = total(share * seq_len, qshare * qtok)
    left = tokens.T[:rank]
    owner = lax.broadcasted_iota(jnp.int32, (1, qshare * qtok), 1) // qtok
    lefts = []
    for query in range(qshare):
        mask = (qids_ref[pl.ds(at * qshare + query, 1), :] != PAD_ID).astype(F32)
        lefts.append(left * jnp.where(owner == query, jnp.concatenate([mask] * qshare, axis=1), 0.0))
        count = jnp.broadcast_to(jnp.sum(mask, axis=1, keepdims=True), (1, 2 * rank))
        for quarter in range(4):
            scratch[quarter, share + qshare, query : query + 1, :] = count
    for query, outer in enumerate(product(lefts, tokens)):
        store(share + query, outer)
    for flip in range(2):
        keep_ref[flip] = scratch[mine ^ flip]
        send_ref[flip] = scratch[mine ^ 2 ^ flip]


def gram_kernel(qshare, hops, at_ref, *refs):
    piece_refs, (out_ref, scratch) = refs[:-2], refs[-2:]
    at = at_ref[0]
    _, half, lanes = piece_refs[0].shape
    nquery = scratch.shape[0]
    examples = []
    for hop, pieces in hops:
        for piece in pieces[:-1]:
            examples.append((piece_refs[piece], piece_refs[piece].shape[0]))
        last = piece_refs[pieces[-1]]
        nex = last.shape[0] - qshare
        examples.append((last, nex))
        scratch[pl.ds((at ^ hop) * qshare, qshare)] = last[nex:]
    ntrain = sum(nex for _, nex in examples)
    both = jnp.concatenate(
        [
            jnp.concatenate(
                [ref[:nex, row, :] for ref, nex in examples] + [scratch[:, row, :]], axis=0
            )
            for row in range(half)
        ],
        axis=1,
    )
    size = ntrain + nquery
    high, low = halves(both)
    gap = jnp.zeros((-size % 128, half * lanes), high.dtype)
    left = jnp.concatenate([high, low], axis=0)
    right = jnp.concatenate([high, gap, low], axis=0)
    total = lax.dot_general(left, right, NT, preferred_element_type=F32)
    total = total[:size] + total[size:]
    total = total[:, :size] + total[:, size + gap.shape[0] :]
    if folds(ntrain):
        half = ntrain // 2
        out_ref[:half, :] = jnp.concatenate([total[:half, :ntrain], total[half:ntrain, :ntrain]], axis=1)
        out_ref[half:, :size] = total[ntrain:]
        out_ref[half:, size:] = jnp.zeros((nquery, 2 * ntrain - size), F32)
    else:
        out_ref[...] = total


def folds(ntrain):
    return 2 * ntrain <= 128


def solve_kernel(ntrain, feat, share, low_ref, one_ref, two_ref, out_ref, columns):
    nquery = out_ref.shape[1]
    whole = one_ref[...] + two_ref[...]
    if folds(ntrain):
        half = ntrain // 2
        gram = jnp.concatenate([whole[:half, :ntrain], whole[:half, ntrain:]], axis=0)
        rest = whole[half:]
    else:
        gram = whole[:ntrain, :ntrain]
        rest = whole[ntrain:]
    cross = rest[:, :ntrain]
    square = rest[:, ntrain : ntrain + nquery]

    def rowsum(v):
        return jnp.sum(v, axis=1, keepdims=True)

    def diagonal(v):
        rows = lax.broadcasted_iota(jnp.int32, v.shape, 0)
        cols = lax.broadcasted_iota(jnp.int32, v.shape, 1)
        return jnp.where(rows == cols, v, 0.0)

    norm = rowsum(diagonal(square))
    trace = jnp.sum(diagonal(gram)) / ntrain
    scale = 1.0 / (ntrain * (DAMP * trace / feat))

    def thirds(value):
        high, rest = halves(value)
        low = value - high.astype(F32) - rest.astype(F32)
        return high, rest, low.astype(jnp.bfloat16)

    gram_parts = thirds(gram)

    def times_gram(value):
        left = jnp.concatenate(thirds(value), axis=0)
        out = sum(jnp.dot(left, part, preferred_element_type=F32) for part in gram_parts[::-1])
        return out[2 * nquery :] + out[nquery : 2 * nquery] + out[:nquery]

    res_a, res_x, res_p = jnp.ones_like(norm), jnp.zeros_like(cross), cross
    dir_a, dir_x, dir_p = res_a, res_x, res_p
    solved = jnp.zeros_like(cross)
    now = norm
    for step in range(ITERS):
        inner = dir_p * dir_p * scale
        if step:
            inner = inner + dir_x * (dir_a * cross + dir_p)
        alpha = now / (dir_a * dir_a * norm + rowsum(inner))
        solved = solved + alpha * dir_p
        if step == ITERS - 1:
            break
        res_a = res_a - alpha * dir_a
        res_x = res_x - alpha * (dir_x + dir_p * scale)
        res_p = res_a * cross + times_gram(res_x)
        fresh = res_a * res_a * norm + rowsum(res_x * (res_a * cross + res_p))
        beta = fresh / now
        dir_a = res_a + beta * dir_a
        dir_x = res_x + beta * dir_x
        dir_p = res_p + beta * dir_p
        now = fresh
    columns[...] = solved.T
    out_ref[...] = columns[pl.ds(low_ref[0] * share, share), :]


def per_device(
    mesh, train_hidden, train_grads, train_ids, query_hidden, query_grads, query_ids, proj_in, proj_out
):
    parts = lax.axis_size("tensor")
    groups = lax.axis_size("dp")
    at = lax.axis_index("tensor").astype(jnp.int32).reshape(1)
    group = lax.axis_index("dp").astype(jnp.int32)
    low = (group & 3).reshape(1)
    steady = group
    for bit in range(1, (groups - 1).bit_length()):
        steady = steady ^ (group >> bit)
    quarter = ((steady & 1) * 2 + (low >> 1)).reshape(1)
    nseq, seq_len, ff = train_hidden.shape
    width = train_grads.shape[2]
    rank = proj_in.shape[1]
    nquery, qtok, _ = query_hidden.shape
    ntrain = nseq * groups
    share = nseq // parts
    qshare = nquery // parts
    half = rank // 8

    arrays = (
        train_hidden.reshape(nseq * seq_len, ff),
        train_grads.reshape(nseq * seq_len, width),
        query_hidden.reshape(nquery * qtok, ff),
        query_grads.reshape(nquery * qtok, width),
        proj_in.T,
        proj_out.T,
    )
    pieces = {}
    turn = at
    for hops in ((3,), (2, 1), (0,)):
        values = project(mesh, turn, arrays, parts, hops)
        turn, *values = lax.optimization_barrier((turn, *values))
        for hop, value in zip(hops, values):
            pieces[hop] = swap(value, 0, hop) if hop else value

    early = pieces[3] + pieces[0]
    rows = share + qshare + 1
    keep, send = call(
        functools.partial(outer_kernel, share, qshare),
        [jax.ShapeDtypeStruct((2, rows, half, 2 * rank), F32)] * 2,
        "outer",
        in_specs=[SMEM_SPEC] * 2 + [VMEM_SPEC] * 5,
        scratch_shapes=[pltpu.VMEM((4, rows, half, 2 * rank), F32)],
    )(at, quarter, train_ids, query_ids, early, pieces[2], pieces[1])

    def ordered(bit, mine, other):
        nex = mine.shape[-3] - qshare - 1
        first = jnp.where(bit == 0, mine, other)[..., :nex, :, :]
        second = jnp.where(bit == 0, other, mine)[..., :nex, :, :]
        return jnp.concatenate([first, second, (mine + other)[..., nex:, :, :]], axis=-3)

    both = ordered(low[0] & 1, keep, swap(send, 1, 0))
    block = ordered(low[0] >> 1, both[0], swap(both[1], 3, 0))
    flip = 4
    while 2 * flip < groups:
        block = ordered(0, block, swap(block, flip | 1, 0))
        flip *= 2
    nex = block.shape[0] - qshare - 1
    own = block[:nex]
    other = swap(block, flip | 1, 0)
    early = swap(own, 0, 3)
    rest = (block + other)[nex:]
    after = jnp.concatenate([other[:nex], rest[:qshare] / rest[qshare, :qshare, None, :]], axis=0)
    whole = jnp.concatenate([own, after], axis=0)
    far = swap(whole, 0, 2)
    late = swap(lax.optimization_barrier((after, early))[0], 0, 3)
    near = swap(whole, 0, 1)
    blocks = [whole, early, late, far, near]
    hops = ((0, (0,)), (3, (1, 2)), (2, (3,)), (1, (4,)))
    size = ntrain + nquery
    shape = (ntrain // 2 + nquery, 2 * ntrain) if folds(ntrain) else (size, size)
    gram = call(
        functools.partial(gram_kernel, qshare, hops),
        jax.ShapeDtypeStruct(shape, F32),
        "gram",
        in_specs=[SMEM_SPEC] + [VMEM_SPEC] * len(blocks),
        scratch_shapes=[pltpu.VMEM((nquery, half, 2 * rank), F32)],
    )(at, *blocks)
    gram = gram + swap(gram, 3, 0)
    return call(
        functools.partial(solve_kernel, ntrain, rank * rank, share),
        jax.ShapeDtypeStruct((share, nquery), F32),
        "solve",
        in_specs=[SMEM_SPEC] + [VMEM_SPEC] * 2,
        scratch_shapes=[pltpu.VMEM((ntrain, nquery), F32)],
    )(low, gram, swap(gram, 1, 0)).T


def solution(mesh):
    return jax.shard_map(
        functools.partial(per_device, mesh),
        mesh=mesh,
        in_specs=(
            P("dp", None, "tensor"),
            P("dp", None, "tensor"),
            P("dp", None),
            P(None, "dp", "tensor"),
            P(None, "dp", "tensor"),
            P(None, "dp"),
            P("tensor", None),
            P("tensor", None),
        ),
        out_specs=P(None, ("dp", "tensor")),
        check_vma=False,
    )
```

```python
import functools

import jax
import jax.numpy as jnp
from jax import lax
from jax.experimental import pallas as pl
from jax.experimental.pallas import tpu as pltpu
from jax.sharding import PartitionSpec as P

ITERS = 3
PAD_ID = 128004
DAMP = 0.1
HIGHEST = lax.Precision.HIGHEST
F32 = jnp.float32
VMEM_LIMIT = 32 * 1024 * 1024
NT = (((1,), (1,)), ((), ()))
SMEM_SPEC = pl.BlockSpec(memory_space=pltpu.SMEM)
VMEM_SPEC = pl.BlockSpec(memory_space=pltpu.VMEM)
HBM_SPEC = pl.BlockSpec(memory_space=pltpu.HBM)


def call(kernel, out_shape, name, **kwargs):
    return pl.pallas_call(
        kernel,
        out_shape=out_shape,
        name=name,
        compiler_params=pltpu.CompilerParams(vmem_limit_bytes=VMEM_LIMIT),
        **kwargs,
    )


def swap(value, dp_flip, tensor_flip):
    groups, parts = lax.axis_size("dp"), lax.axis_size("tensor")
    flip = dp_flip * parts + tensor_flip
    return lax.ppermute(value, ("dp", "tensor"), [(i, i ^ flip) for i in range(groups * parts)])


def project_kernel(mesh, parts, hops, tile, at_ref, th_ref, tg_ref, qh_ref, qg_ref, pin_ref, pout_ref, *refs):
    out_refs = refs[: len(hops)]
    hid, grad, pin, pout, sems = refs[len(hops) :]
    at = at_ref[0]
    trows = th_ref.shape[0] // parts
    qrows = qh_ref.shape[0] // parts
    rows = trows + qrows
    rank = pin_ref.shape[0]
    sides = ((th_ref, qh_ref, hid, pin_ref, pin), (tg_ref, qg_ref, grad, pout_ref, pout))
    chunks = []
    started = 0
    for side in (1, 0):
        train, query, buf, weight, held = sides[side]
        wide = buf.shape[1]
        first = wide if side else 4 * tile
        second = (wide - first + tile) // (2 * tile) * tile
        for start, size in ((0, first), (first, second), (first + second, wide - first - second)):
            if not size:
                continue
            cols = pl.ds(start, size)
            pairs = [] if start else [(weight, held)]
            for slot, hop in enumerate(hops):
                to = at ^ hop
                tsrc = pl.ds(pl.multiple_of(to * trows, trows), trows)
                pairs.append((train.at[tsrc, cols], buf.at[pl.ds(slot * rows, trows), cols]))
            for slot, hop in enumerate(() if start else hops):
                to = at ^ hop
                qsrc = pl.ds(pl.multiple_of(to * qrows, qrows), qrows)
                pairs.append((query.at[qsrc, :], buf.at[pl.ds(slot * rows + trows, qrows), :]))
            copies = []
            for src, dst in pairs:
                copies.append(pltpu.make_async_copy(src, dst, sems.at[started]))
                copies[-1].start()
                started += 1
            chunks.append((side, start, size, copies))

    def multiply(*sums):
        count = 0
        for side, start, size, copies in chunks:
            _, _, buf, _, held = sides[side]
            for copy in copies:
                copy.wait()
            for col in range(start, start + size, tile):
                unit, turn = count % len(sums), count // len(sums)
                count += 1
                weight = [held[:, col : col + tile]]
                if side:
                    weight.insert(0, jnp.zeros((side * rank, tile), held.dtype))
                weight.append(jnp.zeros((tile - (side + 1) * rank, tile), held.dtype))
                weight = jnp.concatenate(weight, axis=0)
                pltpu.matmul_push_rhs(weight, turn % 2, unit, transpose=True)
                pltpu.matmul_acc_lhs(sums[unit], buf[:, col : col + tile], load_staged_rhs=turn % 2)
        total = pltpu.matmul_pop(sums[0])[:, : 2 * rank]
        for unit in sums[1:]:
            total = total + pltpu.matmul_pop(unit)[:, : 2 * rank]
        for slot, ref in enumerate(out_refs):
            ref[...] = total[slot * rows : (slot + 1) * rows]

    with jax.sharding.use_abstract_mesh(mesh.abstract_mesh):
        sums = [pltpu.ACC(unit)((hid.shape[0], tile), F32) for unit in range(2)]
        pl.run_scoped(multiply, *sums)


def project(mesh, at, arrays, parts, hops):
    train, _, query, _, pin, pout = arrays
    rank, ff = pin.shape
    width = pout.shape[1]
    rows = (train.shape[0] + query.shape[0]) // parts
    held = rows * len(hops)
    bf16 = jnp.bfloat16
    tile = 256
    return call(
        functools.partial(project_kernel, mesh, parts, hops, tile),
        [jax.ShapeDtypeStruct((rows, 2 * rank), F32)] * len(hops),
        "project_" + "_".join(str(hop) for hop in hops),
        in_specs=[SMEM_SPEC] + [HBM_SPEC] * 6,
        out_specs=[VMEM_SPEC] * len(hops),
        scratch_shapes=[
            pltpu.VMEM((held, ff), bf16),
            pltpu.VMEM((held, width), bf16),
            pltpu.VMEM((rank, ff), bf16),
            pltpu.VMEM((rank, width), bf16),
            pltpu.SemaphoreType.DMA((2 + 6 * len(hops),)),
        ],
        cost_estimate=pl.CostEstimate(
            flops=2 * held * (ff + width) * rank,
            bytes_accessed=2 * (held + rank) * (ff + width),
            transcendentals=0,
        ),
    )(at, *[pltpu.with_memory_space_constraint(array, pltpu.HBM) for array in arrays])


def halves(value):
    high = value.astype(jnp.bfloat16)
    return high, (value - high.astype(F32)).astype(jnp.bfloat16)


def outer_kernel(share, qshare, at_ref, quarter_ref, ids_ref, qids_ref, *refs):
    tok_refs, (keep_ref, send_ref, scratch) = refs[:-3], refs[-3:]
    at, mine = at_ref[0], quarter_ref[0]
    seq_len = ids_ref.shape[1]
    rank = tok_refs[0].shape[1] // 2
    qtok = qids_ref.shape[1]
    half = rank // 8

    def total(start, rows):
        value = tok_refs[0][start : start + rows, :]
        for ref in tok_refs[1:]:
            value = value + ref[start : start + rows, :]
        return value

    def product(lefts, tokens):
        left = jnp.concatenate([part for value in lefts for part in halves(value)], axis=0)
        right = jnp.concatenate(halves(tokens), axis=1)
        out = jnp.dot(left, right, preferred_element_type=F32)
        out = out[:, : 2 * rank] + out[:, 2 * rank :]
        sums = []
        for index in range(len(lefts)):
            start = 2 * rank * index
            sums.append(out[start : start + rank] + out[start + rank : start + 2 * rank])
        return sums

    def store(slot, outer):
        for quarter in range(4):
            start = quarter * 2 * half
            scratch[quarter, slot] = jnp.concatenate(
                [outer[start : start + half, rank:], outer[start + half : start + 2 * half, rank:]],
                axis=1,
            )

    for seq in range(share):
        tokens = total(seq * seq_len, seq_len)
        mask = (ids_ref[pl.ds(at * share + seq, 1), :] != PAD_ID).astype(F32)
        (outer,) = product([tokens.T[:rank] * mask], tokens)
        store(seq, outer / jnp.sum(mask, axis=1, keepdims=True))

    for quarter in range(4):
        scratch[quarter, share + qshare] = jnp.ones((half, 2 * rank), F32)
    tokens = total(share * seq_len, qshare * qtok)
    left = tokens.T[:rank]
    owner = lax.broadcasted_iota(jnp.int32, (1, qshare * qtok), 1) // qtok
    lefts = []
    for query in range(qshare):
        mask = (qids_ref[pl.ds(at * qshare + query, 1), :] != PAD_ID).astype(F32)
        lefts.append(left * jnp.where(owner == query, jnp.concatenate([mask] * qshare, axis=1), 0.0))
        count = jnp.broadcast_to(jnp.sum(mask, axis=1, keepdims=True), (1, 2 * rank))
        for quarter in range(4):
            scratch[quarter, share + qshare, query : query + 1, :] = count
    for query, outer in enumerate(product(lefts, tokens)):
        store(share + query, outer)
    for flip in range(2):
        keep_ref[flip] = scratch[mine ^ flip]
        send_ref[flip] = scratch[mine ^ 2 ^ flip]


def gram_kernel(qshare, hops, at_ref, *refs):
    piece_refs, (out_ref, scratch) = refs[:-2], refs[-2:]
    at = at_ref[0]
    _, half, lanes = piece_refs[0].shape
    nquery = scratch.shape[0]
    examples = []
    for hop, pieces in hops:
        for piece in pieces[:-1]:
            examples.append((piece_refs[piece], piece_refs[piece].shape[0]))
        last = piece_refs[pieces[-1]]
        nex = last.shape[0] - qshare
        examples.append((last, nex))
        scratch[pl.ds((at ^ hop) * qshare, qshare)] = last[nex:]
    ntrain = sum(nex for _, nex in examples)
    both = jnp.concatenate(
        [
            jnp.concatenate(
                [ref[:nex, row, :] for ref, nex in examples] + [scratch[:, row, :]], axis=0
            )
            for row in range(half)
        ],
        axis=1,
    )
    size = ntrain + nquery
    high, low = halves(both)
    gap = jnp.zeros((-size % 128, half * lanes), high.dtype)
    left = jnp.concatenate([high, low], axis=0)
    right = jnp.concatenate([high, gap, low], axis=0)
    total = lax.dot_general(left, right, NT, preferred_element_type=F32)
    total = total[:size] + total[size:]
    total = total[:, :size] + total[:, size + gap.shape[0] :]
    if folds(ntrain):
        half = ntrain // 2
        out_ref[:half, :] = jnp.concatenate([total[:half, :ntrain], total[half:ntrain, :ntrain]], axis=1)
        rest = [total[start : start + nquery, ntrain:] for start in range(0, size, nquery)]
        rest.append(jnp.zeros((nquery, 2 * ntrain - size), F32))
        out_ref[half:, :] = jnp.concatenate(rest, axis=1)
    else:
        out_ref[...] = total


def folds(ntrain):
    return 2 * ntrain <= 128


def solve_kernel(ntrain, feat, share, low_ref, one_ref, two_ref, out_ref, columns):
    nquery = out_ref.shape[1]
    whole = one_ref[...] + two_ref[...]
    if folds(ntrain):
        half = ntrain // 2
        gram = jnp.concatenate([whole[:half, :ntrain], whole[:half, ntrain:]], axis=0)
        rest = whole[half:]
        cross = [rest[:, start : start + nquery] for start in range(0, ntrain, nquery)]
        cross = jnp.concatenate(cross, axis=0)
        square = rest[:, ntrain : ntrain + nquery]
    else:
        gram = whole[:ntrain, :ntrain]
        cross = whole[:ntrain, ntrain:]
        square = whole[ntrain:, ntrain:]

    def colsum(v):
        return jnp.sum(v, axis=0, keepdims=True)

    def diagonal(v):
        rows = lax.broadcasted_iota(jnp.int32, v.shape, 0)
        cols = lax.broadcasted_iota(jnp.int32, v.shape, 1)
        return jnp.where(rows == cols, v, 0.0)

    norm = colsum(diagonal(square))
    trace = jnp.sum(colsum(diagonal(gram)), axis=1, keepdims=True) / ntrain
    scale = 1.0 / (ntrain * (DAMP * trace / feat))

    def thirds(value):
        high, rest = halves(value)
        low = value - high.astype(F32) - rest.astype(F32)
        return high, rest, low.astype(jnp.bfloat16)

    gram_parts = jnp.concatenate(thirds(gram), axis=0)

    def times_gram(value):
        out = sum(
            jnp.dot(gram_parts, part, preferred_element_type=F32) for part in thirds(value)[::-1]
        )
        return out[2 * ntrain :] + out[ntrain : 2 * ntrain] + out[:ntrain]

    res_a, res_x, res_p = jnp.ones_like(norm), jnp.zeros_like(cross), cross
    dir_a, dir_x, dir_p = res_a, res_x, res_p
    solved = jnp.zeros_like(cross)
    now = norm
    for step in range(ITERS):
        inner = dir_p * dir_p * scale
        if step:
            inner = inner + dir_x * (dir_a * cross + dir_p)
        alpha = now / (dir_a * dir_a * norm + colsum(inner))
        solved = solved + alpha * dir_p
        if step == ITERS - 1:
            break
        res_a = res_a - alpha * dir_a
        res_x = res_x - alpha * (dir_x + dir_p * scale)
        res_p = res_a * cross + times_gram(res_x)
        fresh = res_a * res_a * norm + colsum(res_x * (res_a * cross + res_p))
        beta = fresh / now
        dir_a = res_a + beta * dir_a
        dir_x = res_x + beta * dir_x
        dir_p = res_p + beta * dir_p
        now = fresh
    columns[...] = solved
    out_ref[...] = columns[pl.ds(low_ref[0] * share, share), :]


def per_device(
    mesh, train_hidden, train_grads, train_ids, query_hidden, query_grads, query_ids, proj_in, proj_out
):
    parts = lax.axis_size("tensor")
    groups = lax.axis_size("dp")
    at = lax.axis_index("tensor").astype(jnp.int32).reshape(1)
    group = lax.axis_index("dp").astype(jnp.int32)
    low = (group & 3).reshape(1)
    steady = group
    for bit in range(1, (groups - 1).bit_length()):
        steady = steady ^ (group >> bit)
    quarter = ((steady & 1) * 2 + (low >> 1)).reshape(1)
    nseq, seq_len, ff = train_hidden.shape
    width = train_grads.shape[2]
    rank = proj_in.shape[1]
    nquery, qtok, _ = query_hidden.shape
    ntrain = nseq * groups
    share = nseq // parts
    qshare = nquery // parts
    half = rank // 8

    arrays = (
        train_hidden.reshape(nseq * seq_len, ff),
        train_grads.reshape(nseq * seq_len, width),
        query_hidden.reshape(nquery * qtok, ff),
        query_grads.reshape(nquery * qtok, width),
        proj_in.T,
        proj_out.T,
    )
    pieces = {}
    turn = at
    for hops in ((3,), (2, 1), (0,)):
        values = project(mesh, turn, arrays, parts, hops)
        turn, *values = lax.optimization_barrier((turn, *values))
        for hop, value in zip(hops, values):
            pieces[hop] = swap(value, 0, hop) if hop else value

    early = pieces[3] + pieces[0]
    rows = share + qshare + 1
    keep, send = call(
        functools.partial(outer_kernel, share, qshare),
        [jax.ShapeDtypeStruct((2, rows, half, 2 * rank), F32)] * 2,
        "outer",
        in_specs=[SMEM_SPEC] * 2 + [VMEM_SPEC] * 5,
        scratch_shapes=[pltpu.VMEM((4, rows, half, 2 * rank), F32)],
    )(at, quarter, train_ids, query_ids, early, pieces[2], pieces[1])

    def ordered(bit, mine, other):
        nex = mine.shape[-3] - qshare - 1
        first = jnp.where(bit == 0, mine, other)[..., :nex, :, :]
        second = jnp.where(bit == 0, other, mine)[..., :nex, :, :]
        return jnp.concatenate([first, second, (mine + other)[..., nex:, :, :]], axis=-3)

    both = ordered(low[0] & 1, keep, swap(send, 1, 0))
    block = ordered(low[0] >> 1, both[0], swap(both[1], 3, 0))
    flip = 4
    while 2 * flip < groups:
        block = ordered(0, block, swap(block, flip | 1, 0))
        flip *= 2
    nex = block.shape[0] - qshare - 1
    own = block[:nex]
    other = swap(block, flip | 1, 0)
    early = swap(own, 0, 2)
    rest = (block + other)[nex:]
    after = jnp.concatenate([other[:nex], rest[:qshare] / rest[qshare, :qshare, None, :]], axis=0)
    whole = jnp.concatenate([own, after], axis=0)
    far = swap(whole, 0, 3)
    late = swap(lax.optimization_barrier((after, early))[0], 0, 2)
    near = swap(whole, 0, 1)
    blocks = [whole, early, late, far, near]
    hops = ((0, (0,)), (2, (1, 2)), (3, (3,)), (1, (4,)))
    size = ntrain + nquery
    shape = (ntrain // 2 + nquery, 2 * ntrain) if folds(ntrain) else (size, size)
    gram = call(
        functools.partial(gram_kernel, qshare, hops),
        jax.ShapeDtypeStruct(shape, F32),
        "gram",
        in_specs=[SMEM_SPEC] + [VMEM_SPEC] * len(blocks),
        scratch_shapes=[pltpu.VMEM((nquery, half, 2 * rank), F32)],
    )(at, *blocks)
    gram = gram + swap(gram, 3, 0)
    return call(
        functools.partial(solve_kernel, ntrain, rank * rank, share),
        jax.ShapeDtypeStruct((share, nquery), F32),
        "solve",
        in_specs=[SMEM_SPEC] + [VMEM_SPEC] * 2,
        scratch_shapes=[pltpu.VMEM((ntrain, nquery), F32)],
    )(low, gram, swap(gram, 1, 0)).T


def solution(mesh):
    return jax.shard_map(
        functools.partial(per_device, mesh),
        mesh=mesh,
        in_specs=(
            P("dp", None, "tensor"),
            P("dp", None, "tensor"),
            P("dp", None),
            P(None, "dp", "tensor"),
            P(None, "dp", "tensor"),
            P(None, "dp"),
            P("tensor", None),
            P("tensor", None),
        ),
        out_specs=P(None, ("dp", "tensor")),
        check_vma=False,
    )
```

```python
import functools

import jax
import jax.numpy as jnp
from jax import lax
from jax.experimental import pallas as pl
from jax.experimental.pallas import tpu as pltpu
from jax.sharding import PartitionSpec as P

ITERS = 3
PAD_ID = 128004
DAMP = 0.1
HIGHEST = lax.Precision.HIGHEST
F32 = jnp.float32
VMEM_LIMIT = 32 * 1024 * 1024
NT = (((1,), (1,)), ((), ()))
SMEM_SPEC = pl.BlockSpec(memory_space=pltpu.SMEM)
VMEM_SPEC = pl.BlockSpec(memory_space=pltpu.VMEM)
HBM_SPEC = pl.BlockSpec(memory_space=pltpu.HBM)


def call(kernel, out_shape, name, **kwargs):
    return pl.pallas_call(
        kernel,
        out_shape=out_shape,
        name=name,
        compiler_params=pltpu.CompilerParams(vmem_limit_bytes=VMEM_LIMIT),
        **kwargs,
    )


def swap(value, dp_flip, tensor_flip):
    groups, parts = lax.axis_size("dp"), lax.axis_size("tensor")
    flip = dp_flip * parts + tensor_flip
    return lax.ppermute(value, ("dp", "tensor"), [(i, i ^ flip) for i in range(groups * parts)])


def project_kernel(mesh, parts, hops, tile, at_ref, th_ref, tg_ref, qh_ref, qg_ref, pin_ref, pout_ref, *refs):
    out_refs = refs[: len(hops)]
    hid, grad, pin, pout, sems = refs[len(hops) :]
    at = at_ref[0]
    trows = th_ref.shape[0] // parts
    qrows = qh_ref.shape[0] // parts
    rows = trows + qrows
    rank = pin_ref.shape[0]
    sides = ((th_ref, qh_ref, hid, pin_ref, pin), (tg_ref, qg_ref, grad, pout_ref, pout))
    chunks = []
    started = 0
    for side in (1, 0):
        train, query, buf, weight, held = sides[side]
        wide = buf.shape[1]
        first = wide if side else 4 * tile
        second = (wide - first + tile) // (2 * tile) * tile
        for start, size in ((0, first), (first, second), (first + second, wide - first - second)):
            if not size:
                continue
            cols = pl.ds(start, size)
            pairs = [] if start else [(weight, held)]
            for slot, hop in enumerate(hops):
                to = at ^ hop
                tsrc = pl.ds(pl.multiple_of(to * trows, trows), trows)
                pairs.append((train.at[tsrc, cols], buf.at[pl.ds(slot * rows, trows), cols]))
            for slot, hop in enumerate(() if start else hops):
                to = at ^ hop
                qsrc = pl.ds(pl.multiple_of(to * qrows, qrows), qrows)
                pairs.append((query.at[qsrc, :], buf.at[pl.ds(slot * rows + trows, qrows), :]))
            copies = []
            for src, dst in pairs:
                copies.append(pltpu.make_async_copy(src, dst, sems.at[started]))
                copies[-1].start()
                started += 1
            chunks.append((side, start, size, copies))

    def multiply(*sums):
        pair = len(sums) // 2
        count = 0
        for side, start, size, copies in chunks:
            _, _, buf, _, held = sides[side]
            for copy in copies:
                copy.wait()
            for col in range(start, start + size, tile * pair):
                unit, turn = count % 2, count // 2
                count += 1
                cols = [c for c in range(col, col + tile * pair, tile) if c < start + size]
                weight = [held[:, c : c + tile] for c in cols]
                if side:
                    weight.insert(0, jnp.zeros((pair * side * rank, tile), held.dtype))
                filled = sum(part.shape[0] for part in weight)
                if filled < tile:
                    weight.append(jnp.zeros((tile - filled, tile), held.dtype))
                weight = jnp.concatenate(weight, axis=0)
                pltpu.matmul_push_rhs(weight, turn % 2, unit, transpose=True)
                for index, c in enumerate(cols):
                    load = {} if index else {"load_staged_rhs": turn % 2}
                    pltpu.matmul_acc_lhs(sums[unit * pair + index], buf[:, c : c + tile], **load)
        totals = [
            pltpu.matmul_pop(sums[index]) + pltpu.matmul_pop(sums[pair + index])
            for index in range(pair)
        ]
        parts_of = []
        for side in range(2):
            value = None
            for index, total in enumerate(totals):
                at_col = (pair * side + index) * rank
                piece = total[:, at_col : at_col + rank]
                value = piece if value is None else value + piece
            parts_of.append(value)
        value = jnp.concatenate(parts_of, axis=1)
        for slot, ref in enumerate(out_refs):
            ref[...] = value[slot * rows : (slot + 1) * rows]

    with jax.sharding.use_abstract_mesh(mesh.abstract_mesh):
        pair = 2 if 2 * hid.shape[0] <= 1024 else 1
        sums = [pltpu.ACC(unit)((hid.shape[0], tile), F32) for unit in range(2) for _ in range(pair)]
        pl.run_scoped(multiply, *sums)


def project(mesh, at, arrays, parts, hops):
    train, _, query, _, pin, pout = arrays
    rank, ff = pin.shape
    width = pout.shape[1]
    rows = (train.shape[0] + query.shape[0]) // parts
    held = rows * len(hops)
    bf16 = jnp.bfloat16
    tile = 256
    return call(
        functools.partial(project_kernel, mesh, parts, hops, tile),
        [jax.ShapeDtypeStruct((rows, 2 * rank), F32)] * len(hops),
        "project_" + "_".join(str(hop) for hop in hops),
        in_specs=[SMEM_SPEC] + [HBM_SPEC] * 6,
        out_specs=[VMEM_SPEC] * len(hops),
        scratch_shapes=[
            pltpu.VMEM((held, ff), bf16),
            pltpu.VMEM((held, width), bf16),
            pltpu.VMEM((rank, ff), bf16),
            pltpu.VMEM((rank, width), bf16),
            pltpu.SemaphoreType.DMA((2 + 6 * len(hops),)),
        ],
        cost_estimate=pl.CostEstimate(
            flops=2 * held * (ff + width) * rank,
            bytes_accessed=2 * (held + rank) * (ff + width),
            transcendentals=0,
        ),
    )(at, *[pltpu.with_memory_space_constraint(array, pltpu.HBM) for array in arrays])


def halves(value):
    high = value.astype(jnp.bfloat16)
    return high, (value - high.astype(F32)).astype(jnp.bfloat16)


def outer_kernel(share, qshare, at_ref, quarter_ref, ids_ref, qids_ref, *refs):
    tok_refs, (keep_ref, send_ref, scratch) = refs[:-3], refs[-3:]
    at, mine = at_ref[0], quarter_ref[0]
    seq_len = ids_ref.shape[1]
    rank = tok_refs[0].shape[1] // 2
    qtok = qids_ref.shape[1]
    half = rank // 8

    def total(start, rows):
        value = tok_refs[0][start : start + rows, :]
        for ref in tok_refs[1:]:
            value = value + ref[start : start + rows, :]
        return value

    def product(lefts, tokens):
        left = jnp.concatenate([part for value in lefts for part in halves(value)], axis=0)
        right = jnp.concatenate(halves(tokens), axis=1)
        out = jnp.dot(left, right, preferred_element_type=F32)
        out = out[:, : 2 * rank] + out[:, 2 * rank :]
        sums = []
        for index in range(len(lefts)):
            start = 2 * rank * index
            sums.append(out[start : start + rank] + out[start + rank : start + 2 * rank])
        return sums

    def store(slot, outer):
        for quarter in range(4):
            start = quarter * 2 * half
            scratch[quarter, slot] = jnp.concatenate(
                [outer[start : start + half, rank:], outer[start + half : start + 2 * half, rank:]],
                axis=1,
            )

    for seq in range(share):
        tokens = total(seq * seq_len, seq_len)
        mask = (ids_ref[pl.ds(at * share + seq, 1), :] != PAD_ID).astype(F32)
        (outer,) = product([tokens.T[:rank] * mask], tokens)
        store(seq, outer / jnp.sum(mask, axis=1, keepdims=True))

    for quarter in range(4):
        scratch[quarter, share + qshare] = jnp.ones((half, 2 * rank), F32)
    tokens = total(share * seq_len, qshare * qtok)
    left = tokens.T[:rank]
    owner = lax.broadcasted_iota(jnp.int32, (1, qshare * qtok), 1) // qtok
    lefts = []
    for query in range(qshare):
        mask = (qids_ref[pl.ds(at * qshare + query, 1), :] != PAD_ID).astype(F32)
        lefts.append(left * jnp.where(owner == query, jnp.concatenate([mask] * qshare, axis=1), 0.0))
        count = jnp.broadcast_to(jnp.sum(mask, axis=1, keepdims=True), (1, 2 * rank))
        for quarter in range(4):
            scratch[quarter, share + qshare, query : query + 1, :] = count
    for query, outer in enumerate(product(lefts, tokens)):
        store(share + query, outer)
    for flip in range(2):
        keep_ref[flip] = scratch[mine ^ flip]
        send_ref[flip] = scratch[mine ^ 2 ^ flip]


def gram_kernel(qshare, hops, at_ref, *refs):
    piece_refs, (out_ref, scratch) = refs[:-2], refs[-2:]
    at = at_ref[0]
    _, half, lanes = piece_refs[0].shape
    nquery = scratch.shape[0]
    examples = []
    for hop, pieces in hops:
        for piece in pieces[:-1]:
            examples.append((piece_refs[piece], piece_refs[piece].shape[0]))
        last = piece_refs[pieces[-1]]
        nex = last.shape[0] - qshare
        examples.append((last, nex))
        scratch[pl.ds((at ^ hop) * qshare, qshare)] = last[nex:]
    ntrain = sum(nex for _, nex in examples)
    both = jnp.concatenate(
        [
            jnp.concatenate(
                [ref[:nex, row, :] for ref, nex in examples] + [scratch[:, row, :]], axis=0
            )
            for row in range(half)
        ],
        axis=1,
    )
    size = ntrain + nquery
    high, low = halves(both)
    gap = jnp.zeros((-size % 128, half * lanes), high.dtype)
    left = jnp.concatenate([high, low], axis=0)
    right = jnp.concatenate([high, gap, low], axis=0)
    total = lax.dot_general(left, right, NT, preferred_element_type=F32)
    total = total[:size] + total[size:]
    total = total[:, :size] + total[:, size + gap.shape[0] :]
    if folds(ntrain):
        half = ntrain // 2
        out_ref[:half, :] = jnp.concatenate([total[:half, :ntrain], total[half:ntrain, :ntrain]], axis=1)
        rest = [total[start : start + nquery, ntrain:] for start in range(0, size, nquery)]
        rest.append(jnp.zeros((nquery, 2 * ntrain - size), F32))
        out_ref[half:, :] = jnp.concatenate(rest, axis=1)
    else:
        out_ref[...] = total


def folds(ntrain):
    return 2 * ntrain <= 128


def solve_kernel(ntrain, feat, share, low_ref, one_ref, two_ref, out_ref, columns):
    nquery = out_ref.shape[1]
    whole = one_ref[...] + two_ref[...]
    if folds(ntrain):
        half = ntrain // 2
        gram = jnp.concatenate([whole[:half, :ntrain], whole[:half, ntrain:]], axis=0)
        rest = whole[half:]
        cross = [rest[:, start : start + nquery] for start in range(0, ntrain, nquery)]
        cross = jnp.concatenate(cross, axis=0)
        square = rest[:, ntrain : ntrain + nquery]
    else:
        gram = whole[:ntrain, :ntrain]
        cross = whole[:ntrain, ntrain:]
        square = whole[ntrain:, ntrain:]

    def colsum(v):
        return jnp.sum(v, axis=0, keepdims=True)

    def diagonal(v):
        rows = lax.broadcasted_iota(jnp.int32, v.shape, 0)
        cols = lax.broadcasted_iota(jnp.int32, v.shape, 1)
        return jnp.where(rows == cols, v, 0.0)

    norm = colsum(diagonal(square))
    trace = jnp.sum(colsum(diagonal(gram)), axis=1, keepdims=True) / ntrain
    scale = 1.0 / (ntrain * (DAMP * trace / feat))

    def thirds(value):
        high, rest = halves(value)
        low = value - high.astype(F32) - rest.astype(F32)
        return high, rest, low.astype(jnp.bfloat16)

    gram_parts = jnp.concatenate(thirds(gram), axis=0)

    def times_gram(value):
        out = sum(
            jnp.dot(gram_parts, part, preferred_element_type=F32) for part in thirds(value)[::-1]
        )
        return out[2 * ntrain :] + out[ntrain : 2 * ntrain] + out[:ntrain]

    res_a, res_x, res_p = jnp.ones_like(norm), jnp.zeros_like(cross), cross
    dir_a, dir_x, dir_p = res_a, res_x, res_p
    solved = jnp.zeros_like(cross)
    now = norm
    for step in range(ITERS):
        inner = dir_p * dir_p * scale
        if step:
            inner = inner + dir_x * (dir_a * cross + dir_p)
        alpha = now / (dir_a * dir_a * norm + colsum(inner))
        solved = solved + alpha * dir_p
        if step == ITERS - 1:
            break
        res_a = res_a - alpha * dir_a
        res_x = res_x - alpha * (dir_x + dir_p * scale)
        res_p = res_a * cross + times_gram(res_x)
        fresh = res_a * res_a * norm + colsum(res_x * (res_a * cross + res_p))
        beta = fresh / now
        dir_a = res_a + beta * dir_a
        dir_x = res_x + beta * dir_x
        dir_p = res_p + beta * dir_p
        now = fresh
    columns[...] = solved
    out_ref[...] = columns[pl.ds(low_ref[0] * share, share), :]


def per_device(
    mesh, train_hidden, train_grads, train_ids, query_hidden, query_grads, query_ids, proj_in, proj_out
):
    parts = lax.axis_size("tensor")
    groups = lax.axis_size("dp")
    at = lax.axis_index("tensor").astype(jnp.int32).reshape(1)
    group = lax.axis_index("dp").astype(jnp.int32)
    low = (group & 3).reshape(1)
    steady = group
    for bit in range(1, (groups - 1).bit_length()):
        steady = steady ^ (group >> bit)
    quarter = ((steady & 1) * 2 + (low >> 1)).reshape(1)
    nseq, seq_len, ff = train_hidden.shape
    width = train_grads.shape[2]
    rank = proj_in.shape[1]
    nquery, qtok, _ = query_hidden.shape
    ntrain = nseq * groups
    share = nseq // parts
    qshare = nquery // parts
    half = rank // 8

    arrays = (
        train_hidden.reshape(nseq * seq_len, ff),
        train_grads.reshape(nseq * seq_len, width),
        query_hidden.reshape(nquery * qtok, ff),
        query_grads.reshape(nquery * qtok, width),
        proj_in.T,
        proj_out.T,
    )
    pieces = {}
    turn = at
    for hops in ((3,), (2, 1), (0,)):
        values = project(mesh, turn, arrays, parts, hops)
        turn, *values = lax.optimization_barrier((turn, *values))
        for hop, value in zip(hops, values):
            pieces[hop] = swap(value, 0, hop) if hop else value

    early = pieces[3] + pieces[0]
    rows = share + qshare + 1
    keep, send = call(
        functools.partial(outer_kernel, share, qshare),
        [jax.ShapeDtypeStruct((2, rows, half, 2 * rank), F32)] * 2,
        "outer",
        in_specs=[SMEM_SPEC] * 2 + [VMEM_SPEC] * 5,
        scratch_shapes=[pltpu.VMEM((4, rows, half, 2 * rank), F32)],
    )(at, quarter, train_ids, query_ids, early, pieces[2], pieces[1])

    def ordered(bit, mine, other):
        nex = mine.shape[-3] - qshare - 1
        first = jnp.where(bit == 0, mine, other)[..., :nex, :, :]
        second = jnp.where(bit == 0, other, mine)[..., :nex, :, :]
        return jnp.concatenate([first, second, (mine + other)[..., nex:, :, :]], axis=-3)

    both = ordered(low[0] & 1, keep, swap(send, 1, 0))
    block = ordered(low[0] >> 1, both[0], swap(both[1], 3, 0))
    flip = 4
    while 2 * flip < groups:
        block = ordered(0, block, swap(block, flip | 1, 0))
        flip *= 2
    nex = block.shape[0] - qshare - 1
    own = block[:nex]
    other = swap(block, flip | 1, 0)
    early = swap(own, 0, 2)
    rest = (block + other)[nex:]
    after = jnp.concatenate([other[:nex], rest[:qshare] / rest[qshare, :qshare, None, :]], axis=0)
    whole = jnp.concatenate([own, after], axis=0)
    far = swap(whole, 0, 3)
    late = swap(lax.optimization_barrier((after, early))[0], 0, 2)
    near = swap(whole, 0, 1)
    blocks = [whole, early, late, far, near]
    hops = ((0, (0,)), (2, (1, 2)), (3, (3,)), (1, (4,)))
    size = ntrain + nquery
    shape = (ntrain // 2 + nquery, 2 * ntrain) if folds(ntrain) else (size, size)
    gram = call(
        functools.partial(gram_kernel, qshare, hops),
        jax.ShapeDtypeStruct(shape, F32),
        "gram",
        in_specs=[SMEM_SPEC] + [VMEM_SPEC] * len(blocks),
        scratch_shapes=[pltpu.VMEM((nquery, half, 2 * rank), F32)],
    )(at, *blocks)
    gram = gram + swap(gram, 3, 0)
    return call(
        functools.partial(solve_kernel, ntrain, rank * rank, share),
        jax.ShapeDtypeStruct((share, nquery), F32),
        "solve",
        in_specs=[SMEM_SPEC] + [VMEM_SPEC] * 2,
        scratch_shapes=[pltpu.VMEM((ntrain, nquery), F32)],
    )(low, gram, swap(gram, 1, 0)).T


def solution(mesh):
    return jax.shard_map(
        functools.partial(per_device, mesh),
        mesh=mesh,
        in_specs=(
            P("dp", None, "tensor"),
            P("dp", None, "tensor"),
            P("dp", None),
            P(None, "dp", "tensor"),
            P(None, "dp", "tensor"),
            P(None, "dp"),
            P("tensor", None),
            P("tensor", None),
        ),
        out_specs=P(None, ("dp", "tensor")),
        check_vma=False,
    )
```

```python
import functools

import jax
import jax.numpy as jnp
from jax import lax
from jax.experimental import pallas as pl
from jax.experimental.pallas import tpu as pltpu
from jax.sharding import PartitionSpec as P

ITERS = 3
PAD_ID = 128004
DAMP = 0.1
HIGHEST = lax.Precision.HIGHEST
F32 = jnp.float32
VMEM_LIMIT = 32 * 1024 * 1024
NT = (((1,), (1,)), ((), ()))
SMEM_SPEC = pl.BlockSpec(memory_space=pltpu.SMEM)
VMEM_SPEC = pl.BlockSpec(memory_space=pltpu.VMEM)
HBM_SPEC = pl.BlockSpec(memory_space=pltpu.HBM)


def call(kernel, out_shape, name, **kwargs):
    return pl.pallas_call(
        kernel,
        out_shape=out_shape,
        name=name,
        compiler_params=pltpu.CompilerParams(vmem_limit_bytes=VMEM_LIMIT),
        **kwargs,
    )


def swap(value, dp_flip, tensor_flip):
    groups, parts = lax.axis_size("dp"), lax.axis_size("tensor")
    flip = dp_flip * parts + tensor_flip
    return lax.ppermute(value, ("dp", "tensor"), [(i, i ^ flip) for i in range(groups * parts)])


def project_kernel(mesh, parts, hops, tile, at_ref, th_ref, tg_ref, qh_ref, qg_ref, pin_ref, pout_ref, *refs):
    out_refs = refs[: len(hops)]
    hid, grad, pin, pout, sems = refs[len(hops) :]
    at = at_ref[0]
    trows = th_ref.shape[0] // parts
    qrows = qh_ref.shape[0] // parts
    rows = trows + qrows
    rank = pin_ref.shape[0]
    sides = ((th_ref, qh_ref, hid, pin_ref, pin), (tg_ref, qg_ref, grad, pout_ref, pout))
    chunks = []
    started = 0
    for side in (1, 0):
        train, query, buf, weight, held = sides[side]
        wide = buf.shape[1]
        first = wide if side else 4 * tile
        second = (wide - first + tile) // (2 * tile) * tile
        for start, size in ((0, first), (first, second), (first + second, wide - first - second)):
            if not size:
                continue
            cols = pl.ds(start, size)
            pairs = [] if start else [(weight, held)]
            for slot, hop in enumerate(hops):
                to = at ^ hop
                tsrc = pl.ds(pl.multiple_of(to * trows, trows), trows)
                pairs.append((train.at[tsrc, cols], buf.at[pl.ds(slot * rows, trows), cols]))
            for slot, hop in enumerate(() if start else hops):
                to = at ^ hop
                qsrc = pl.ds(pl.multiple_of(to * qrows, qrows), qrows)
                pairs.append((query.at[qsrc, :], buf.at[pl.ds(slot * rows + trows, qrows), :]))
            copies = []
            for src, dst in pairs:
                copies.append(pltpu.make_async_copy(src, dst, sems.at[started]))
                copies[-1].start()
                started += 1
            chunks.append((side, start, size, copies))

    def multiply(*sums):
        count = 0
        for side, start, size, copies in chunks:
            _, _, buf, _, held = sides[side]
            for copy in copies:
                copy.wait()
            for col in range(start, start + size, tile):
                unit, turn = count % len(sums), count // len(sums)
                count += 1
                weight = [held[:, col : col + tile]]
                if side:
                    weight.insert(0, jnp.zeros((side * rank, tile), held.dtype))
                weight.append(jnp.zeros((tile - (side + 1) * rank, tile), held.dtype))
                weight = jnp.concatenate(weight, axis=0)
                pltpu.matmul_push_rhs(weight, turn % 2, unit, transpose=True)
                pltpu.matmul_acc_lhs(sums[unit], buf[:, col : col + tile], load_staged_rhs=turn % 2)
        total = pltpu.matmul_pop(sums[0])[:, : 2 * rank]
        for unit in sums[1:]:
            total = total + pltpu.matmul_pop(unit)[:, : 2 * rank]
        for slot, ref in enumerate(out_refs):
            ref[...] = total[slot * rows : (slot + 1) * rows]

    with jax.sharding.use_abstract_mesh(mesh.abstract_mesh):
        sums = [pltpu.ACC(unit)((hid.shape[0], tile), F32) for unit in range(2)]
        pl.run_scoped(multiply, *sums)


def project(mesh, at, arrays, parts, hops):
    train, _, query, _, pin, pout = arrays
    rank, ff = pin.shape
    width = pout.shape[1]
    rows = (train.shape[0] + query.shape[0]) // parts
    held = rows * len(hops)
    bf16 = jnp.bfloat16
    tile = 256
    return call(
        functools.partial(project_kernel, mesh, parts, hops, tile),
        [jax.ShapeDtypeStruct((rows, 2 * rank), F32)] * len(hops),
        "project_" + "_".join(str(hop) for hop in hops),
        in_specs=[SMEM_SPEC] + [HBM_SPEC] * 6,
        out_specs=[VMEM_SPEC] * len(hops),
        scratch_shapes=[
            pltpu.VMEM((held, ff), bf16),
            pltpu.VMEM((held, width), bf16),
            pltpu.VMEM((rank, ff), bf16),
            pltpu.VMEM((rank, width), bf16),
            pltpu.SemaphoreType.DMA((2 + 6 * len(hops),)),
        ],
        cost_estimate=pl.CostEstimate(
            flops=2 * held * (ff + width) * rank,
            bytes_accessed=2 * (held + rank) * (ff + width),
            transcendentals=0,
        ),
    )(at, *[pltpu.with_memory_space_constraint(array, pltpu.HBM) for array in arrays])


def halves(value):
    high = value.astype(jnp.bfloat16)
    return high, (value - high.astype(F32)).astype(jnp.bfloat16)


def outer_kernel(share, qshare, at_ref, quarter_ref, ids_ref, qids_ref, *refs):
    tok_refs, (keep_ref, send_ref, scratch) = refs[:-3], refs[-3:]
    at, mine = at_ref[0], quarter_ref[0]
    seq_len = ids_ref.shape[1]
    rank = tok_refs[0].shape[1] // 2
    qtok = qids_ref.shape[1]
    half = rank // 8

    def total(start, rows):
        value = tok_refs[0][start : start + rows, :]
        for ref in tok_refs[1:]:
            value = value + ref[start : start + rows, :]
        return value

    def product(lefts, tokens):
        left = jnp.concatenate([part for value in lefts for part in halves(value)], axis=0)
        right = jnp.concatenate(halves(tokens), axis=1)
        out = jnp.dot(left, right, preferred_element_type=F32)
        out = out[:, : 2 * rank] + out[:, 2 * rank :]
        sums = []
        for index in range(len(lefts)):
            start = 2 * rank * index
            sums.append(out[start : start + rank] + out[start + rank : start + 2 * rank])
        return sums

    def store(slot, outer):
        for quarter in range(4):
            start = quarter * 2 * half
            scratch[quarter, slot] = jnp.concatenate(
                [outer[start : start + half, rank:], outer[start + half : start + 2 * half, rank:]],
                axis=1,
            )

    for seq in range(share):
        tokens = total(seq * seq_len, seq_len)
        mask = (ids_ref[pl.ds(at * share + seq, 1), :] != PAD_ID).astype(F32)
        (outer,) = product([tokens.T[:rank] * mask], tokens)
        store(seq, outer / jnp.sum(mask, axis=1, keepdims=True))

    for quarter in range(4):
        scratch[quarter, share + qshare] = jnp.ones((half, 2 * rank), F32)
    tokens = total(share * seq_len, qshare * qtok)
    left = tokens.T[:rank]
    owner = lax.broadcasted_iota(jnp.int32, (1, qshare * qtok), 1) // qtok
    lefts = []
    for query in range(qshare):
        mask = (qids_ref[pl.ds(at * qshare + query, 1), :] != PAD_ID).astype(F32)
        lefts.append(left * jnp.where(owner == query, jnp.concatenate([mask] * qshare, axis=1), 0.0))
        count = jnp.broadcast_to(jnp.sum(mask, axis=1, keepdims=True), (1, 2 * rank))
        for quarter in range(4):
            scratch[quarter, share + qshare, query : query + 1, :] = count
    for query, outer in enumerate(product(lefts, tokens)):
        store(share + query, outer)
    for flip in range(2):
        keep_ref[flip] = scratch[mine ^ flip]
        send_ref[flip] = scratch[mine ^ 2 ^ flip]


def gram_kernel(qshare, hops, at_ref, *refs):
    piece_refs, (out_ref, scratch) = refs[:-2], refs[-2:]
    at = at_ref[0]
    _, half, lanes = piece_refs[0].shape
    nquery = scratch.shape[0]
    examples = []
    for hop, pieces in hops:
        for piece in pieces[:-1]:
            examples.append((piece_refs[piece], piece_refs[piece].shape[0]))
        last = piece_refs[pieces[-1]]
        nex = last.shape[0] - qshare
        examples.append((last, nex))
        scratch[pl.ds((at ^ hop) * qshare, qshare)] = last[nex:]
    ntrain = sum(nex for _, nex in examples)
    both = jnp.concatenate(
        [
            jnp.concatenate(
                [ref[:nex, row, :] for ref, nex in examples] + [scratch[:, row, :]], axis=0
            )
            for row in range(half)
        ],
        axis=1,
    )
    size = ntrain + nquery
    high, low = halves(both)
    gap = jnp.zeros((-size % 128, half * lanes), high.dtype)
    left = jnp.concatenate([high, low], axis=0)
    right = jnp.concatenate([high, gap, low], axis=0)
    total = lax.dot_general(left, right, NT, preferred_element_type=F32)
    total = total[:size] + total[size:]
    total = total[:, :size] + total[:, size + gap.shape[0] :]
    if folds(ntrain):
        half = ntrain // 2
        out_ref[:half, :] = jnp.concatenate([total[:half, :ntrain], total[half:ntrain, :ntrain]], axis=1)
        rest = [total[start : start + nquery, ntrain:] for start in range(0, size, nquery)]
        rest.append(jnp.zeros((nquery, 2 * ntrain - size), F32))
        out_ref[half:, :] = jnp.concatenate(rest, axis=1)
    else:
        out_ref[...] = total


def folds(ntrain):
    return 2 * ntrain <= 128


def solve_kernel(ntrain, feat, share, low_ref, one_ref, two_ref, out_ref, columns):
    nquery = out_ref.shape[1]
    whole = one_ref[...] + two_ref[...]
    if folds(ntrain):
        half = ntrain // 2
        gram = jnp.concatenate([whole[:half, :ntrain], whole[:half, ntrain:]], axis=0)
        rest = whole[half:]
        cross = [rest[:, start : start + nquery] for start in range(0, ntrain, nquery)]
        cross = jnp.concatenate(cross, axis=0)
        square = rest[:, ntrain : ntrain + nquery]
    else:
        gram = whole[:ntrain, :ntrain]
        cross = whole[:ntrain, ntrain:]
        square = whole[ntrain:, ntrain:]

    def colsum(v):
        return jnp.sum(v, axis=0, keepdims=True)

    def diagonal(v):
        rows = lax.broadcasted_iota(jnp.int32, v.shape, 0)
        cols = lax.broadcasted_iota(jnp.int32, v.shape, 1)
        return jnp.where(rows == cols, v, 0.0)

    norm = colsum(diagonal(square))
    trace = jnp.sum(colsum(diagonal(gram)), axis=1, keepdims=True) / ntrain
    scale = 1.0 / (ntrain * (DAMP * trace / feat))

    def thirds(value):
        high, rest = halves(value)
        low = value - high.astype(F32) - rest.astype(F32)
        return high, rest, low.astype(jnp.bfloat16)

    gram_parts = jnp.concatenate(thirds(gram), axis=0)

    def times_gram(value):
        out = sum(
            jnp.dot(gram_parts, part, preferred_element_type=F32) for part in thirds(value)[::-1]
        )
        return out[2 * ntrain :] + out[ntrain : 2 * ntrain] + out[:ntrain]

    res_a, res_x, res_p = jnp.ones_like(norm), jnp.zeros_like(cross), cross
    dir_a, dir_x, dir_p = res_a, res_x, res_p
    solved = jnp.zeros_like(cross)
    now = norm
    for step in range(ITERS):
        inner = dir_p * dir_p * scale
        if step:
            inner = inner + dir_x * (dir_a * cross + dir_p)
        alpha = now / (dir_a * dir_a * norm + colsum(inner))
        solved = solved + alpha * dir_p
        if step == ITERS - 1:
            break
        res_a = res_a - alpha * dir_a
        res_x = res_x - alpha * (dir_x + dir_p * scale)
        res_p = res_a * cross + times_gram(res_x)
        fresh = res_a * res_a * norm + colsum(res_x * (res_a * cross + res_p))
        beta = fresh / now
        dir_a = res_a + beta * dir_a
        dir_x = res_x + beta * dir_x
        dir_p = res_p + beta * dir_p
        now = fresh
    columns[...] = solved
    out_ref[...] = columns[pl.ds(low_ref[0] * share, share), :]


def per_device(
    mesh, train_hidden, train_grads, train_ids, query_hidden, query_grads, query_ids, proj_in, proj_out
):
    parts = lax.axis_size("tensor")
    groups = lax.axis_size("dp")
    at = lax.axis_index("tensor").astype(jnp.int32).reshape(1)
    group = lax.axis_index("dp").astype(jnp.int32)
    low = (group & 3).reshape(1)
    steady = group
    for bit in range(1, (groups - 1).bit_length()):
        steady = steady ^ (group >> bit)
    quarter = ((steady & 1) * 2 + (low >> 1)).reshape(1)
    nseq, seq_len, ff = train_hidden.shape
    width = train_grads.shape[2]
    rank = proj_in.shape[1]
    nquery, qtok, _ = query_hidden.shape
    ntrain = nseq * groups
    share = nseq // parts
    qshare = nquery // parts
    half = rank // 8

    arrays = (
        train_hidden.reshape(nseq * seq_len, ff),
        train_grads.reshape(nseq * seq_len, width),
        query_hidden.reshape(nquery * qtok, ff),
        query_grads.reshape(nquery * qtok, width),
        proj_in.T,
        proj_out.T,
    )
    pieces = {}
    turn = at
    for hops in ((3,), (2, 1), (0,)):
        values = project(mesh, turn, arrays, parts, hops)
        turn, *values = lax.optimization_barrier((turn, *values))
        for hop, value in zip(hops, values):
            pieces[hop] = swap(value, 0, hop) if hop else value

    early = pieces[3] + pieces[0]
    rows = share + qshare + 1
    keep, send = call(
        functools.partial(outer_kernel, share, qshare),
        [jax.ShapeDtypeStruct((2, rows, half, 2 * rank), F32)] * 2,
        "outer",
        in_specs=[SMEM_SPEC] * 2 + [VMEM_SPEC] * 5,
        scratch_shapes=[pltpu.VMEM((4, rows, half, 2 * rank), F32)],
    )(at, quarter, train_ids, query_ids, early, pieces[2], pieces[1])

    def ordered(bit, mine, other):
        nex = mine.shape[-3] - qshare - 1
        first = jnp.where(bit == 0, mine, other)[..., :nex, :, :]
        second = jnp.where(bit == 0, other, mine)[..., :nex, :, :]
        return jnp.concatenate([first, second, (mine + other)[..., nex:, :, :]], axis=-3)

    both = ordered(low[0] & 1, keep, swap(send, 1, 0))
    block = ordered(low[0] >> 1, both[0], swap(both[1], 3, 0))
    flip = 4
    while 2 * flip < groups:
        block = ordered(0, block, swap(block, flip | 1, 0))
        flip *= 2
    nex = block.shape[0] - qshare - 1
    own = block[:nex]
    other = swap(block, flip | 1, 0)
    ahead = {hop: swap(own, 0, hop) for hop in (2, 1)}
    rest = (block + other)[nex:]
    after = jnp.concatenate([other[:nex], rest[:qshare] / rest[qshare, :qshare, None, :]], axis=0)
    whole = jnp.concatenate([own, after], axis=0)

    far = swap(whole, 0, 3)
    behind = {
        2: swap(lax.optimization_barrier((after, ahead[2], ahead[1]))[0], 0, 2),
        1: swap(after, 0, 1),
    }
    blocks = [whole, ahead[1], behind[1], far, ahead[2], behind[2]]
    hops = ((0, (0,)), (1, (1, 2)), (3, (3,)), (2, (4, 5)))
    size = ntrain + nquery
    shape = (ntrain // 2 + nquery, 2 * ntrain) if folds(ntrain) else (size, size)
    gram = call(
        functools.partial(gram_kernel, qshare, hops),
        jax.ShapeDtypeStruct(shape, F32),
        "gram",
        in_specs=[SMEM_SPEC] + [VMEM_SPEC] * len(blocks),
        scratch_shapes=[pltpu.VMEM((nquery, half, 2 * rank), F32)],
    )(at, *blocks)
    gram = gram + swap(gram, 3, 0)
    return call(
        functools.partial(solve_kernel, ntrain, rank * rank, share),
        jax.ShapeDtypeStruct((share, nquery), F32),
        "solve",
        in_specs=[SMEM_SPEC] + [VMEM_SPEC] * 2,
        scratch_shapes=[pltpu.VMEM((ntrain, nquery), F32)],
    )(low, gram, swap(gram, 1, 0)).T


def solution(mesh):
    return jax.shard_map(
        functools.partial(per_device, mesh),
        mesh=mesh,
        in_specs=(
            P("dp", None, "tensor"),
            P("dp", None, "tensor"),
            P("dp", None),
            P(None, "dp", "tensor"),
            P(None, "dp", "tensor"),
            P(None, "dp"),
            P("tensor", None),
            P("tensor", None),
        ),
        out_specs=P(None, ("dp", "tensor")),
        check_vma=False,
    )
```

```python
import functools

import jax
import jax.numpy as jnp
from jax import lax
from jax.experimental import pallas as pl
from jax.experimental.pallas import tpu as pltpu
from jax.sharding import PartitionSpec as P

ITERS = 3
PAD_ID = 128004
DAMP = 0.1
HIGHEST = lax.Precision.HIGHEST
F32 = jnp.float32
VMEM_LIMIT = 32 * 1024 * 1024
NT = (((1,), (1,)), ((), ()))
SMEM_SPEC = pl.BlockSpec(memory_space=pltpu.SMEM)
VMEM_SPEC = pl.BlockSpec(memory_space=pltpu.VMEM)
HBM_SPEC = pl.BlockSpec(memory_space=pltpu.HBM)


def call(kernel, out_shape, name, **kwargs):
    return pl.pallas_call(
        kernel,
        out_shape=out_shape,
        name=name,
        compiler_params=pltpu.CompilerParams(vmem_limit_bytes=VMEM_LIMIT),
        **kwargs,
    )


def swap(value, dp_flip, tensor_flip):
    groups, parts = lax.axis_size("dp"), lax.axis_size("tensor")
    flip = dp_flip * parts + tensor_flip
    return lax.ppermute(value, ("dp", "tensor"), [(i, i ^ flip) for i in range(groups * parts)])


def project_kernel(mesh, parts, hops, tile, at_ref, th_ref, tg_ref, qh_ref, qg_ref, pin_ref, pout_ref, *refs):
    out_refs = refs[: len(hops)]
    hid, grad, pin, pout, sems = refs[len(hops) :]
    at = at_ref[0]
    trows = th_ref.shape[0] // parts
    qrows = qh_ref.shape[0] // parts
    rows = trows + qrows
    rank = pin_ref.shape[0]
    sides = ((th_ref, qh_ref, hid, pin_ref, pin), (tg_ref, qg_ref, grad, pout_ref, pout))
    chunks = []
    started = 0
    for side in (1, 0):
        train, query, buf, weight, held = sides[side]
        wide = buf.shape[1]
        first = wide if side else 4 * tile
        second = (wide - first + tile) // (2 * tile) * tile
        for start, size in ((0, first), (first, second), (first + second, wide - first - second)):
            if not size:
                continue
            cols = pl.ds(start, size)
            pairs = [] if start else [(weight, held)]
            for slot, hop in enumerate(hops):
                to = at ^ hop
                tsrc = pl.ds(pl.multiple_of(to * trows, trows), trows)
                pairs.append((train.at[tsrc, cols], buf.at[pl.ds(slot * rows, trows), cols]))
            for slot, hop in enumerate(() if start else hops):
                to = at ^ hop
                qsrc = pl.ds(pl.multiple_of(to * qrows, qrows), qrows)
                pairs.append((query.at[qsrc, :], buf.at[pl.ds(slot * rows + trows, qrows), :]))
            copies = []
            for src, dst in pairs:
                copies.append(pltpu.make_async_copy(src, dst, sems.at[started]))
                copies[-1].start()
                started += 1
            chunks.append((side, start, size, copies))

    def multiply(*sums):
        count = 0
        half = hid.shape[0] // 2
        for side, start, size, copies in chunks:
            _, _, buf, _, held = sides[side]
            for copy in copies:
                copy.wait()
            for col in range(start, start + size, tile):
                turn = count % 2
                count += 1
                weight = [held[:, col : col + tile]]
                if side:
                    weight.insert(0, jnp.zeros((side * rank, tile), held.dtype))
                weight.append(jnp.zeros((tile - (side + 1) * rank, tile), held.dtype))
                weight = jnp.concatenate(weight, axis=0)
                for unit, acc in enumerate(sums):
                    pltpu.matmul_push_rhs(weight, turn, unit, transpose=True)
                    tokens = buf[unit * half : (unit + 1) * half, col : col + tile]
                    pltpu.matmul_acc_lhs(acc, tokens, load_staged_rhs=turn)
        total = jnp.concatenate([pltpu.matmul_pop(acc)[:, : 2 * rank] for acc in sums], axis=0)
        for slot, ref in enumerate(out_refs):
            ref[...] = total[slot * rows : (slot + 1) * rows]

    with jax.sharding.use_abstract_mesh(mesh.abstract_mesh):
        sums = [pltpu.ACC(unit)((hid.shape[0] // 2, tile), F32) for unit in range(2)]
        pl.run_scoped(multiply, *sums)


def project(mesh, at, arrays, parts, hops):
    train, _, query, _, pin, pout = arrays
    rank, ff = pin.shape
    width = pout.shape[1]
    rows = (train.shape[0] + query.shape[0]) // parts
    held = rows * len(hops)
    bf16 = jnp.bfloat16
    tile = 256
    return call(
        functools.partial(project_kernel, mesh, parts, hops, tile),
        [jax.ShapeDtypeStruct((rows, 2 * rank), F32)] * len(hops),
        "project_" + "_".join(str(hop) for hop in hops),
        in_specs=[SMEM_SPEC] + [HBM_SPEC] * 6,
        out_specs=[VMEM_SPEC] * len(hops),
        scratch_shapes=[
            pltpu.VMEM((held, ff), bf16),
            pltpu.VMEM((held, width), bf16),
            pltpu.VMEM((rank, ff), bf16),
            pltpu.VMEM((rank, width), bf16),
            pltpu.SemaphoreType.DMA((2 + 6 * len(hops),)),
        ],
        cost_estimate=pl.CostEstimate(
            flops=2 * held * (ff + width) * rank,
            bytes_accessed=2 * (held + rank) * (ff + width),
            transcendentals=0,
        ),
    )(at, *[pltpu.with_memory_space_constraint(array, pltpu.HBM) for array in arrays])


def halves(value):
    high = value.astype(jnp.bfloat16)
    return high, (value - high.astype(F32)).astype(jnp.bfloat16)


def outer_kernel(share, qshare, at_ref, quarter_ref, ids_ref, qids_ref, *refs):
    tok_refs, (keep_ref, send_ref, scratch) = refs[:-3], refs[-3:]
    at, mine = at_ref[0], quarter_ref[0]
    seq_len = ids_ref.shape[1]
    rank = tok_refs[0].shape[1] // 2
    qtok = qids_ref.shape[1]
    half = rank // 8

    def total(start, rows):
        value = tok_refs[0][start : start + rows, :]
        for ref in tok_refs[1:]:
            value = value + ref[start : start + rows, :]
        return value

    def product(lefts, tokens):
        left = jnp.concatenate([part for value in lefts for part in halves(value)], axis=0)
        right = jnp.concatenate(halves(tokens), axis=1)
        out = jnp.dot(left, right, preferred_element_type=F32)
        out = out[:, : 2 * rank] + out[:, 2 * rank :]
        sums = []
        for index in range(len(lefts)):
            start = 2 * rank * index
            sums.append(out[start : start + rank] + out[start + rank : start + 2 * rank])
        return sums

    def store(slot, outer):
        for quarter in range(4):
            start = quarter * 2 * half
            scratch[quarter, slot] = jnp.concatenate(
                [outer[start : start + half, rank:], outer[start + half : start + 2 * half, rank:]],
                axis=1,
            )

    for seq in range(share):
        tokens = total(seq * seq_len, seq_len)
        mask = (ids_ref[pl.ds(at * share + seq, 1), :] != PAD_ID).astype(F32)
        (outer,) = product([tokens.T[:rank] * mask], tokens)
        store(seq, outer / jnp.sum(mask, axis=1, keepdims=True))

    for quarter in range(4):
        scratch[quarter, share + qshare] = jnp.ones((half, 2 * rank), F32)
    tokens = total(share * seq_len, qshare * qtok)
    left = tokens.T[:rank]
    owner = lax.broadcasted_iota(jnp.int32, (1, qshare * qtok), 1) // qtok
    lefts = []
    for query in range(qshare):
        mask = (qids_ref[pl.ds(at * qshare + query, 1), :] != PAD_ID).astype(F32)
        lefts.append(left * jnp.where(owner == query, jnp.concatenate([mask] * qshare, axis=1), 0.0))
        count = jnp.broadcast_to(jnp.sum(mask, axis=1, keepdims=True), (1, 2 * rank))
        for quarter in range(4):
            scratch[quarter, share + qshare, query : query + 1, :] = count
    for query, outer in enumerate(product(lefts, tokens)):
        store(share + query, outer)
    for flip in range(2):
        keep_ref[flip] = scratch[mine ^ flip]
        send_ref[flip] = scratch[mine ^ 2 ^ flip]


def as_rows(values):
    half = values[0].shape[1]
    return jnp.concatenate(
        [
            jnp.concatenate([value[:, row, :] for value in values], axis=0) for row in range(half)
        ],
        axis=1,
    )


def rows_kernel(qshare, whole_ref, *refs):
    own = whole_ref.at[: whole_ref.shape[0] - qshare]
    refs[-1][...] = as_rows([own, *refs[:-1]])


def gram_kernel(qshare, hops, at_ref, first_ref, *refs):
    piece_refs, (out_ref, scratch) = refs[:-2], refs[-2:]
    nquery = scratch.shape[0]
    examples = []
    for hop, ref in zip(hops, piece_refs):
        nex = ref.shape[0] - qshare
        if hop:
            examples.append(ref.at[:nex])
        scratch[pl.ds((at_ref[0] ^ hop) * qshare, qshare)] = ref[nex:]
    both = jnp.concatenate([first_ref[...], as_rows([*examples, scratch])], axis=0)
    ntrain = both.shape[0] - nquery
    size = ntrain + nquery
    high, low = halves(both)
    gap = jnp.zeros((-size % 128, both.shape[1]), high.dtype)
    left = jnp.concatenate([high, low], axis=0)
    right = jnp.concatenate([high, gap, low], axis=0)
    total = lax.dot_general(left, right, NT, preferred_element_type=F32)
    total = total[:size] + total[size:]
    total = total[:, :size] + total[:, size + gap.shape[0] :]
    if folds(ntrain):
        half = ntrain // 2
        out_ref[:half, :] = jnp.concatenate([total[:half, :ntrain], total[half:ntrain, :ntrain]], axis=1)
        rest = [total[start : start + nquery, ntrain:] for start in range(0, size, nquery)]
        rest.append(jnp.zeros((nquery, 2 * ntrain - size), F32))
        out_ref[half:, :] = jnp.concatenate(rest, axis=1)
    else:
        out_ref[...] = total


def folds(ntrain):
    return 2 * ntrain <= 128


def solve_kernel(ntrain, feat, share, low_ref, one_ref, two_ref, out_ref, columns):
    nquery = out_ref.shape[1]
    whole = one_ref[...] + two_ref[...]
    if folds(ntrain):
        half = ntrain // 2
        gram = jnp.concatenate([whole[:half, :ntrain], whole[:half, ntrain:]], axis=0)
        rest = whole[half:]
        cross = [rest[:, start : start + nquery] for start in range(0, ntrain, nquery)]
        cross = jnp.concatenate(cross, axis=0)
        square = rest[:, ntrain : ntrain + nquery]
    else:
        gram = whole[:ntrain, :ntrain]
        cross = whole[:ntrain, ntrain:]
        square = whole[ntrain:, ntrain:]

    def colsum(v):
        return jnp.sum(v, axis=0, keepdims=True)

    def diagonal(v):
        rows = lax.broadcasted_iota(jnp.int32, v.shape, 0)
        cols = lax.broadcasted_iota(jnp.int32, v.shape, 1)
        return jnp.where(rows == cols, v, 0.0)

    norm = colsum(diagonal(square))
    trace = jnp.sum(colsum(diagonal(gram)), axis=1, keepdims=True) / ntrain
    scale = 1.0 / (ntrain * (DAMP * trace / feat))

    def thirds(value):
        high, rest = halves(value)
        low = value - high.astype(F32) - rest.astype(F32)
        return high, rest, low.astype(jnp.bfloat16)

    gram_parts = jnp.concatenate(thirds(gram), axis=0)

    def times_gram(value):
        out = sum(
            jnp.dot(gram_parts, part, preferred_element_type=F32) for part in thirds(value)[::-1]
        )
        return out[2 * ntrain :] + out[ntrain : 2 * ntrain] + out[:ntrain]

    res_a, res_x, res_p = jnp.ones_like(norm), jnp.zeros_like(cross), cross
    dir_a, dir_x, dir_p = res_a, res_x, res_p
    solved = jnp.zeros_like(cross)
    now = norm
    for step in range(ITERS):
        inner = dir_p * dir_p * scale
        if step:
            inner = inner + dir_x * (dir_a * cross + dir_p)
        alpha = now / (dir_a * dir_a * norm + colsum(inner))
        solved = solved + alpha * dir_p
        if step == ITERS - 1:
            break
        res_a = res_a - alpha * dir_a
        res_x = res_x - alpha * (dir_x + dir_p * scale)
        res_p = res_a * cross + times_gram(res_x)
        fresh = res_a * res_a * norm + colsum(res_x * (res_a * cross + res_p))
        beta = fresh / now
        dir_a = res_a + beta * dir_a
        dir_x = res_x + beta * dir_x
        dir_p = res_p + beta * dir_p
        now = fresh
    columns[...] = solved
    out_ref[...] = columns[pl.ds(low_ref[0] * share, share), :]


def per_device(
    mesh, train_hidden, train_grads, train_ids, query_hidden, query_grads, query_ids, proj_in, proj_out
):
    parts = lax.axis_size("tensor")
    groups = lax.axis_size("dp")
    at = lax.axis_index("tensor").astype(jnp.int32).reshape(1)
    group = lax.axis_index("dp").astype(jnp.int32)
    low = (group & 3).reshape(1)
    steady = group
    for bit in range(1, (groups - 1).bit_length()):
        steady = steady ^ (group >> bit)
    quarter = ((steady & 1) * 2 + (low >> 1)).reshape(1)
    nseq, seq_len, ff = train_hidden.shape
    width = train_grads.shape[2]
    rank = proj_in.shape[1]
    nquery, qtok, _ = query_hidden.shape
    ntrain = nseq * groups
    share = nseq // parts
    qshare = nquery // parts
    half = rank // 8

    arrays = (
        train_hidden.reshape(nseq * seq_len, ff),
        train_grads.reshape(nseq * seq_len, width),
        query_hidden.reshape(nquery * qtok, ff),
        query_grads.reshape(nquery * qtok, width),
        proj_in.T,
        proj_out.T,
    )
    pieces = {}
    turn = at
    for hops in ((3,), (2, 1), (0,)):
        values = project(mesh, turn, arrays, parts, hops)
        turn, *values = lax.optimization_barrier((turn, *values))
        for hop, value in zip(hops, values):
            pieces[hop] = swap(value, 0, hop) if hop else value

    early = pieces[3] + pieces[0]
    rows = share + qshare + 1
    keep, send = call(
        functools.partial(outer_kernel, share, qshare),
        [jax.ShapeDtypeStruct((2, rows, half, 2 * rank), F32)] * 2,
        "outer",
        in_specs=[SMEM_SPEC] * 2 + [VMEM_SPEC] * 5,
        scratch_shapes=[pltpu.VMEM((4, rows, half, 2 * rank), F32)],
    )(at, quarter, train_ids, query_ids, early, pieces[2], pieces[1])

    def ordered(bit, mine, other):
        nex = mine.shape[-3] - qshare - 1
        first = jnp.where(bit == 0, mine, other)[..., :nex, :, :]
        second = jnp.where(bit == 0, other, mine)[..., :nex, :, :]
        return jnp.concatenate([first, second, (mine + other)[..., nex:, :, :]], axis=-3)

    both = ordered(low[0] & 1, keep, swap(send, 1, 0))
    block = ordered(low[0] >> 1, both[0], swap(both[1], 3, 0))
    flip = 4
    while 2 * flip < groups:
        block = ordered(0, block, swap(block, flip | 1, 0))
        flip *= 2
    nex = block.shape[0] - qshare - 1
    own = block[:nex]
    other = swap(block, flip | 1, 0)
    ahead = {hop: swap(own, 0, hop) for hop in (2, 1)}
    rest = (block + other)[nex:]
    after = jnp.concatenate([other[:nex], rest[:qshare] / rest[qshare, :qshare, None, :]], axis=0)
    whole = jnp.concatenate([own, after], axis=0)

    far = swap(whole, 0, 3)
    behind = {
        2: swap(lax.optimization_barrier((after, ahead[2], ahead[1]))[0], 0, 2),
        1: swap(after, 0, 1),
    }
    first = call(
        functools.partial(rows_kernel, qshare),
        jax.ShapeDtypeStruct((4 * nex, half * 2 * rank), F32),
        "rows",
    )(whole, ahead[1], ahead[2])
    blocks = [whole, behind[1], far, behind[2]]
    hops = (0, 1, 3, 2)
    size = ntrain + nquery
    shape = (ntrain // 2 + nquery, 2 * ntrain) if folds(ntrain) else (size, size)
    gram = call(
        functools.partial(gram_kernel, qshare, hops),
        jax.ShapeDtypeStruct(shape, F32),
        "gram",
        in_specs=[SMEM_SPEC] + [VMEM_SPEC] * (1 + len(blocks)),
        scratch_shapes=[pltpu.VMEM((nquery, half, 2 * rank), F32)],
    )(at, first, *blocks)
    gram = gram + swap(gram, 3, 0)
    return call(
        functools.partial(solve_kernel, ntrain, rank * rank, share),
        jax.ShapeDtypeStruct((share, nquery), F32),
        "solve",
        in_specs=[SMEM_SPEC] + [VMEM_SPEC] * 2,
        scratch_shapes=[pltpu.VMEM((ntrain, nquery), F32)],
    )(low, gram, swap(gram, 1, 0)).T


def solution(mesh):
    return jax.shard_map(
        functools.partial(per_device, mesh),
        mesh=mesh,
        in_specs=(
            P("dp", None, "tensor"),
            P("dp", None, "tensor"),
            P("dp", None),
            P(None, "dp", "tensor"),
            P(None, "dp", "tensor"),
            P(None, "dp"),
            P("tensor", None),
            P("tensor", None),
        ),
        out_specs=P(None, ("dp", "tensor")),
        check_vma=False,
    )
```

```python
import functools

import jax
import jax.numpy as jnp
from jax import lax
from jax.experimental import pallas as pl
from jax.experimental.pallas import tpu as pltpu
from jax.sharding import PartitionSpec as P

ITERS = 3
PAD_ID = 128004
DAMP = 0.1
HIGHEST = lax.Precision.HIGHEST
F32 = jnp.float32
VMEM_LIMIT = 32 * 1024 * 1024
NT = (((1,), (1,)), ((), ()))
SMEM_SPEC = pl.BlockSpec(memory_space=pltpu.SMEM)
VMEM_SPEC = pl.BlockSpec(memory_space=pltpu.VMEM)
HBM_SPEC = pl.BlockSpec(memory_space=pltpu.HBM)


def call(kernel, out_shape, name, **kwargs):
    return pl.pallas_call(
        kernel,
        out_shape=out_shape,
        name=name,
        compiler_params=pltpu.CompilerParams(vmem_limit_bytes=VMEM_LIMIT),
        **kwargs,
    )


def swap(value, dp_flip, tensor_flip):
    groups, parts = lax.axis_size("dp"), lax.axis_size("tensor")
    flip = dp_flip * parts + tensor_flip
    return lax.ppermute(value, ("dp", "tensor"), [(i, i ^ flip) for i in range(groups * parts)])


def project_kernel(mesh, parts, hops, tile, at_ref, th_ref, tg_ref, qh_ref, qg_ref, pin_ref, pout_ref, *refs):
    out_refs = refs[: len(hops)]
    hid, grad, pin, pout, sems = refs[len(hops) :]
    at = at_ref[0]
    trows = th_ref.shape[0] // parts
    qrows = qh_ref.shape[0] // parts
    rows = trows + qrows
    rank = pin_ref.shape[0]
    sides = ((th_ref, qh_ref, hid, pin_ref, pin), (tg_ref, qg_ref, grad, pout_ref, pout))
    chunks = []
    started = 0
    for side in (1, 0):
        train, query, buf, weight, held = sides[side]
        wide = buf.shape[1]
        first = wide if side else 4 * tile
        second = (wide - first + tile) // (2 * tile) * tile
        for start, size in ((0, first), (first, second), (first + second, wide - first - second)):
            if not size:
                continue
            cols = pl.ds(start, size)
            pairs = [] if start else [(weight, held)]
            for slot, hop in enumerate(hops):
                to = at ^ hop
                tsrc = pl.ds(pl.multiple_of(to * trows, trows), trows)
                pairs.append((train.at[tsrc, cols], buf.at[pl.ds(slot * rows, trows), cols]))
            for slot, hop in enumerate(() if start else hops):
                to = at ^ hop
                qsrc = pl.ds(pl.multiple_of(to * qrows, qrows), qrows)
                pairs.append((query.at[qsrc, :], buf.at[pl.ds(slot * rows + trows, qrows), :]))
            copies = []
            for src, dst in pairs:
                copies.append(pltpu.make_async_copy(src, dst, sems.at[started]))
                started += 1
            chunks.append((side, start, size, copies))
    for *_, copies in chunks[:-1]:
        for copy in copies:
            copy.start()

    by_rows = len(hops) > 1
    held_rows = hid.shape[0] // 2 if by_rows else hid.shape[0]

    def multiply(*sums):
        count = 0
        for index, (side, start, size, copies) in enumerate(chunks):
            _, _, buf, _, held = sides[side]
            for copy in copies:
                copy.wait()
            if index == 0:
                for copy in chunks[-1][-1]:
                    copy.start()
            for col in range(start, start + size, tile):
                weight = [held[:, col : col + tile]]
                if side:
                    weight.insert(0, jnp.zeros((side * rank, tile), held.dtype))
                weight.append(jnp.zeros((tile - (side + 1) * rank, tile), held.dtype))
                weight = jnp.concatenate(weight, axis=0)
                units = range(len(sums)) if by_rows else (count % len(sums),)
                turn = (count if by_rows else count // len(sums)) % 2
                count += 1
                for unit in units:
                    first = unit * held_rows if by_rows else 0
                    pltpu.matmul_push_rhs(weight, turn, unit, transpose=True)
                    tokens = buf[first : first + held_rows, col : col + tile]
                    pltpu.matmul_acc_lhs(sums[unit], tokens, load_staged_rhs=turn)
        total = [pltpu.matmul_pop(acc)[:, : 2 * rank] for acc in sums]
        total = jnp.concatenate(total, axis=0) if by_rows else sum(total)
        for slot, ref in enumerate(out_refs):
            ref[...] = total[slot * rows : (slot + 1) * rows]

    with jax.sharding.use_abstract_mesh(mesh.abstract_mesh):
        sums = [pltpu.ACC(unit)((held_rows, tile), F32) for unit in range(2)]
        pl.run_scoped(multiply, *sums)


def project(mesh, at, arrays, parts, hops):
    train, _, query, _, pin, pout = arrays
    rank, ff = pin.shape
    width = pout.shape[1]
    rows = (train.shape[0] + query.shape[0]) // parts
    held = rows * len(hops)
    bf16 = jnp.bfloat16
    tile = 256
    return call(
        functools.partial(project_kernel, mesh, parts, hops, tile),
        [jax.ShapeDtypeStruct((rows, 2 * rank), F32)] * len(hops),
        "project_" + "_".join(str(hop) for hop in hops),
        in_specs=[SMEM_SPEC] + [HBM_SPEC] * 6,
        out_specs=[VMEM_SPEC] * len(hops),
        scratch_shapes=[
            pltpu.VMEM((held, ff), bf16),
            pltpu.VMEM((held, width), bf16),
            pltpu.VMEM((rank, ff), bf16),
            pltpu.VMEM((rank, width), bf16),
            pltpu.SemaphoreType.DMA((2 + 6 * len(hops),)),
        ],
        cost_estimate=pl.CostEstimate(
            flops=2 * held * (ff + width) * rank,
            bytes_accessed=2 * (held + rank) * (ff + width),
            transcendentals=0,
        ),
    )(at, *[pltpu.with_memory_space_constraint(array, pltpu.HBM) for array in arrays])


def halves(value):
    high = value.astype(jnp.bfloat16)
    return high, (value - high.astype(F32)).astype(jnp.bfloat16)


def outer_kernel(share, qshare, at_ref, quarter_ref, ids_ref, qids_ref, *refs):
    tok_refs, (keep_ref, send_ref, scratch) = refs[:-3], refs[-3:]
    at, mine = at_ref[0], quarter_ref[0]
    seq_len = ids_ref.shape[1]
    rank = tok_refs[0].shape[1] // 2
    qtok = qids_ref.shape[1]
    half = rank // 8

    def total(start, rows):
        value = tok_refs[0][start : start + rows, :]
        for ref in tok_refs[1:]:
            value = value + ref[start : start + rows, :]
        return value

    def product(lefts, tokens):
        left = jnp.concatenate([part for value in lefts for part in halves(value)], axis=0)
        right = jnp.concatenate(halves(tokens), axis=1)
        out = jnp.dot(left, right, preferred_element_type=F32)
        out = out[:, : 2 * rank] + out[:, 2 * rank :]
        sums = []
        for index in range(len(lefts)):
            start = 2 * rank * index
            sums.append(out[start : start + rank] + out[start + rank : start + 2 * rank])
        return sums

    def store(slot, outer):
        for quarter in range(4):
            start = quarter * 2 * half
            scratch[quarter, slot] = jnp.concatenate(
                [outer[start : start + half, rank:], outer[start + half : start + 2 * half, rank:]],
                axis=1,
            )

    for seq in range(share):
        tokens = total(seq * seq_len, seq_len)
        mask = (ids_ref[pl.ds(at * share + seq, 1), :] != PAD_ID).astype(F32)
        (outer,) = product([tokens.T[:rank] * mask], tokens)
        store(seq, outer / jnp.sum(mask, axis=1, keepdims=True))

    for quarter in range(4):
        scratch[quarter, share + qshare] = jnp.ones((half, 2 * rank), F32)
    tokens = total(share * seq_len, qshare * qtok)
    left = tokens.T[:rank]
    owner = lax.broadcasted_iota(jnp.int32, (1, qshare * qtok), 1) // qtok
    lefts = []
    for query in range(qshare):
        mask = (qids_ref[pl.ds(at * qshare + query, 1), :] != PAD_ID).astype(F32)
        lefts.append(left * jnp.where(owner == query, jnp.concatenate([mask] * qshare, axis=1), 0.0))
        count = jnp.broadcast_to(jnp.sum(mask, axis=1, keepdims=True), (1, 2 * rank))
        for quarter in range(4):
            scratch[quarter, share + qshare, query : query + 1, :] = count
    for query, outer in enumerate(product(lefts, tokens)):
        store(share + query, outer)
    for flip in range(2):
        keep_ref[flip] = scratch[mine ^ flip]
        send_ref[flip] = scratch[mine ^ 2 ^ flip]


def as_rows(values):
    half = values[0].shape[1]
    return jnp.concatenate(
        [
            jnp.concatenate([value[:, row, :] for value in values], axis=0) for row in range(half)
        ],
        axis=1,
    )


def rows_kernel(qshare, whole_ref, *refs):
    own = whole_ref.at[: whole_ref.shape[0] - qshare]
    refs[-1][...] = as_rows([own, *refs[:-1]])


def gram_kernel(qshare, hops, at_ref, first_ref, *refs):
    piece_refs, (out_ref, scratch) = refs[:-2], refs[-2:]
    nquery = scratch.shape[0]
    examples = []
    for hop, ref in zip(hops, piece_refs):
        nex = ref.shape[0] - qshare
        if hop:
            examples.append(ref.at[:nex])
        scratch[pl.ds((at_ref[0] ^ hop) * qshare, qshare)] = ref[nex:]
    both = jnp.concatenate([first_ref[...], as_rows([*examples, scratch])], axis=0)
    ntrain = both.shape[0] - nquery
    size = ntrain + nquery
    high, low = halves(both)
    gap = jnp.zeros((-size % 128, both.shape[1]), high.dtype)
    left = jnp.concatenate([high, low], axis=0)
    right = jnp.concatenate([high, gap, low], axis=0)
    total = lax.dot_general(left, right, NT, preferred_element_type=F32)
    total = total[:size] + total[size:]
    total = total[:, :size] + total[:, size + gap.shape[0] :]
    if folds(ntrain):
        half = ntrain // 2
        out_ref[:half, :] = jnp.concatenate([total[:half, :ntrain], total[half:ntrain, :ntrain]], axis=1)
        rest = [total[start : start + nquery, ntrain:] for start in range(0, size, nquery)]
        rest.append(jnp.zeros((nquery, 2 * ntrain - size), F32))
        out_ref[half:, :] = jnp.concatenate(rest, axis=1)
    else:
        out_ref[...] = total


def folds(ntrain):
    return 2 * ntrain <= 128


def solve_kernel(ntrain, feat, share, low_ref, one_ref, two_ref, out_ref, columns):
    nquery = out_ref.shape[1]
    whole = one_ref[...] + two_ref[...]
    if folds(ntrain):
        half = ntrain // 2
        gram = jnp.concatenate([whole[:half, :ntrain], whole[:half, ntrain:]], axis=0)
        rest = whole[half:]
        cross = [rest[:, start : start + nquery] for start in range(0, ntrain, nquery)]
        cross = jnp.concatenate(cross, axis=0)
        square = rest[:, ntrain : ntrain + nquery]
    else:
        gram = whole[:ntrain, :ntrain]
        cross = whole[:ntrain, ntrain:]
        square = whole[ntrain:, ntrain:]

    def colsum(v):
        return jnp.sum(v, axis=0, keepdims=True)

    def diagonal(v):
        rows = lax.broadcasted_iota(jnp.int32, v.shape, 0)
        cols = lax.broadcasted_iota(jnp.int32, v.shape, 1)
        return jnp.where(rows == cols, v, 0.0)

    norm = colsum(diagonal(square))
    trace = jnp.sum(colsum(diagonal(gram)), axis=1, keepdims=True) / ntrain
    scale = 1.0 / (ntrain * (DAMP * trace / feat))

    def thirds(value):
        high, rest = halves(value)
        low = value - high.astype(F32) - rest.astype(F32)
        return high, rest, low.astype(jnp.bfloat16)

    gram_parts = jnp.concatenate(thirds(gram), axis=0)

    def times_gram(value):
        out = sum(
            jnp.dot(gram_parts, part, preferred_element_type=F32) for part in thirds(value)[::-1]
        )
        return out[2 * ntrain :] + out[ntrain : 2 * ntrain] + out[:ntrain]

    res_a, res_x, res_p = jnp.ones_like(norm), jnp.zeros_like(cross), cross
    dir_a, dir_x, dir_p = res_a, res_x, res_p
    solved = jnp.zeros_like(cross)
    now = norm
    for step in range(ITERS):
        inner = dir_p * dir_p * scale
        if step:
            inner = inner + dir_x * (dir_a * cross + dir_p)
        alpha = now / (dir_a * dir_a * norm + colsum(inner))
        solved = solved + alpha * dir_p
        if step == ITERS - 1:
            break
        res_a = res_a - alpha * dir_a
        res_x = res_x - alpha * (dir_x + dir_p * scale)
        res_p = res_a * cross + times_gram(res_x)
        fresh = res_a * res_a * norm + colsum(res_x * (res_a * cross + res_p))
        beta = fresh / now
        dir_a = res_a + beta * dir_a
        dir_x = res_x + beta * dir_x
        dir_p = res_p + beta * dir_p
        now = fresh
    columns[...] = solved
    out_ref[...] = columns[pl.ds(low_ref[0] * share, share), :]


def per_device(
    mesh, train_hidden, train_grads, train_ids, query_hidden, query_grads, query_ids, proj_in, proj_out
):
    parts = lax.axis_size("tensor")
    groups = lax.axis_size("dp")
    at = lax.axis_index("tensor").astype(jnp.int32).reshape(1)
    group = lax.axis_index("dp").astype(jnp.int32)
    low = (group & 3).reshape(1)
    steady = group
    for bit in range(1, (groups - 1).bit_length()):
        steady = steady ^ (group >> bit)
    quarter = ((steady & 1) * 2 + (low >> 1)).reshape(1)
    nseq, seq_len, ff = train_hidden.shape
    width = train_grads.shape[2]
    rank = proj_in.shape[1]
    nquery, qtok, _ = query_hidden.shape
    ntrain = nseq * groups
    share = nseq // parts
    qshare = nquery // parts
    half = rank // 8

    arrays = (
        train_hidden.reshape(nseq * seq_len, ff),
        train_grads.reshape(nseq * seq_len, width),
        query_hidden.reshape(nquery * qtok, ff),
        query_grads.reshape(nquery * qtok, width),
        proj_in.T,
        proj_out.T,
    )
    pieces = {}
    turn = at
    for hops in ((3,), (2, 1), (0,)):
        values = project(mesh, turn, arrays, parts, hops)
        turn, *values = lax.optimization_barrier((turn, *values))
        for hop, value in zip(hops, values):
            pieces[hop] = swap(value, 0, hop) if hop else value

    early = pieces[3] + pieces[0]
    rows = share + qshare + 1
    keep, send = call(
        functools.partial(outer_kernel, share, qshare),
        [jax.ShapeDtypeStruct((2, rows, half, 2 * rank), F32)] * 2,
        "outer",
        in_specs=[SMEM_SPEC] * 2 + [VMEM_SPEC] * 5,
        scratch_shapes=[pltpu.VMEM((4, rows, half, 2 * rank), F32)],
    )(at, quarter, train_ids, query_ids, early, pieces[2], pieces[1])

    def ordered(bit, mine, other):
        nex = mine.shape[-3] - qshare - 1
        first = jnp.where(bit == 0, mine, other)[..., :nex, :, :]
        second = jnp.where(bit == 0, other, mine)[..., :nex, :, :]
        return jnp.concatenate([first, second, (mine + other)[..., nex:, :, :]], axis=-3)

    both = ordered(low[0] & 1, keep, swap(send, 1, 0))
    block = ordered(low[0] >> 1, both[0], swap(both[1], 3, 0))
    flip = 4
    while 2 * flip < groups:
        block = ordered(0, block, swap(block, flip | 1, 0))
        flip *= 2
    nex = block.shape[0] - qshare - 1
    own = block[:nex]
    other = swap(block, flip | 1, 0)
    ahead = {hop: swap(own, 0, hop) for hop in (2, 1)}
    rest = (block + other)[nex:]
    after = jnp.concatenate([other[:nex], rest[:qshare] / rest[qshare, :qshare, None, :]], axis=0)
    whole = jnp.concatenate([own, after], axis=0)

    far = swap(whole, 0, 3)
    behind = {
        2: swap(lax.optimization_barrier((after, ahead[2], ahead[1]))[0], 0, 2),
        1: swap(after, 0, 1),
    }
    first = call(
        functools.partial(rows_kernel, qshare),
        jax.ShapeDtypeStruct((4 * nex, half * 2 * rank), F32),
        "rows",
    )(whole, ahead[1], ahead[2])
    blocks = [whole, behind[1], far, behind[2]]
    hops = (0, 1, 3, 2)
    size = ntrain + nquery
    shape = (ntrain // 2 + nquery, 2 * ntrain) if folds(ntrain) else (size, size)
    gram = call(
        functools.partial(gram_kernel, qshare, hops),
        jax.ShapeDtypeStruct(shape, F32),
        "gram",
        in_specs=[SMEM_SPEC] + [VMEM_SPEC] * (1 + len(blocks)),
        scratch_shapes=[pltpu.VMEM((nquery, half, 2 * rank), F32)],
    )(at, first, *blocks)
    gram = gram + swap(gram, 3, 0)
    return call(
        functools.partial(solve_kernel, ntrain, rank * rank, share),
        jax.ShapeDtypeStruct((share, nquery), F32),
        "solve",
        in_specs=[SMEM_SPEC] + [VMEM_SPEC] * 2,
        scratch_shapes=[pltpu.VMEM((ntrain, nquery), F32)],
    )(low, gram, swap(gram, 1, 0)).T


def solution(mesh):
    return jax.shard_map(
        functools.partial(per_device, mesh),
        mesh=mesh,
        in_specs=(
            P("dp", None, "tensor"),
            P("dp", None, "tensor"),
            P("dp", None),
            P(None, "dp", "tensor"),
            P(None, "dp", "tensor"),
            P(None, "dp"),
            P("tensor", None),
            P("tensor", None),
        ),
        out_specs=P(None, ("dp", "tensor")),
        check_vma=False,
    )
```

```python
import functools

import jax
import jax.numpy as jnp
from jax import lax
from jax.experimental import pallas as pl
from jax.experimental.pallas import tpu as pltpu
from jax.sharding import PartitionSpec as P

ITERS = 3
PAD_ID = 128004
DAMP = 0.1
HIGHEST = lax.Precision.HIGHEST
F32 = jnp.float32
VMEM_LIMIT = 32 * 1024 * 1024
NT = (((1,), (1,)), ((), ()))
SMEM_SPEC = pl.BlockSpec(memory_space=pltpu.SMEM)
VMEM_SPEC = pl.BlockSpec(memory_space=pltpu.VMEM)
HBM_SPEC = pl.BlockSpec(memory_space=pltpu.HBM)


def call(kernel, out_shape, name, **kwargs):
    return pl.pallas_call(
        kernel,
        out_shape=out_shape,
        name=name,
        compiler_params=pltpu.CompilerParams(vmem_limit_bytes=VMEM_LIMIT),
        **kwargs,
    )


def swap(value, dp_flip, tensor_flip):
    groups, parts = lax.axis_size("dp"), lax.axis_size("tensor")
    flip = dp_flip * parts + tensor_flip
    return lax.ppermute(value, ("dp", "tensor"), [(i, i ^ flip) for i in range(groups * parts)])


def project_kernel(mesh, parts, hops, tile, at_ref, th_ref, tg_ref, qh_ref, qg_ref, pin_ref, pout_ref, *refs):
    out_refs = refs[: len(hops)]
    hid, grad, pin, pout, sems = refs[len(hops) :]
    at = at_ref[0]
    trows = th_ref.shape[0] // parts
    qrows = qh_ref.shape[0] // parts
    rows = trows + qrows
    rank = pin_ref.shape[0]
    sides = ((th_ref, qh_ref, hid, pin_ref, pin), (tg_ref, qg_ref, grad, pout_ref, pout))
    chunks = []
    started = 0
    for side in (1, 0):
        train, query, buf, weight, held = sides[side]
        wide = buf.shape[1]
        first = wide if side else 4 * tile
        second = (wide - first + tile) // (2 * tile) * tile
        for start, size in ((0, first), (first, second), (first + second, wide - first - second)):
            if not size:
                continue
            cols = pl.ds(start, size)
            pairs = [] if start else [(weight, held)]
            for slot, hop in enumerate(hops):
                to = at ^ hop
                tsrc = pl.ds(pl.multiple_of(to * trows, trows), trows)
                pairs.append((train.at[tsrc, cols], buf.at[pl.ds(slot * rows, trows), cols]))
            for slot, hop in enumerate(() if start else hops):
                to = at ^ hop
                qsrc = pl.ds(pl.multiple_of(to * qrows, qrows), qrows)
                pairs.append((query.at[qsrc, :], buf.at[pl.ds(slot * rows + trows, qrows), :]))
            copies = []
            for src, dst in pairs:
                copies.append(pltpu.make_async_copy(src, dst, sems.at[started]))
                copies[-1].start()
                started += 1
            chunks.append((side, start, size, copies))

    by_rows = len(hops) > 1
    held_rows = hid.shape[0] // 2 if by_rows else hid.shape[0]

    def multiply(*sums):
        count = 0
        for side, start, size, copies in chunks:
            _, _, buf, _, held = sides[side]
            for copy in copies:
                copy.wait()
            for col in range(start, start + size, tile):
                weight = [held[:, col : col + tile]]
                if side:
                    weight.insert(0, jnp.zeros((side * rank, tile), held.dtype))
                weight.append(jnp.zeros((tile - (side + 1) * rank, tile), held.dtype))
                weight = jnp.concatenate(weight, axis=0)
                units = range(len(sums)) if by_rows else (count % len(sums),)
                turn = (count if by_rows else count // len(sums)) % 2
                count += 1
                for unit in units:
                    first = unit * held_rows if by_rows else 0
                    pltpu.matmul_push_rhs(weight, turn, unit, transpose=True)
                    tokens = buf[first : first + held_rows, col : col + tile]
                    pltpu.matmul_acc_lhs(sums[unit], tokens, load_staged_rhs=turn)
        total = [pltpu.matmul_pop(acc)[:, : 2 * rank] for acc in sums]
        total = jnp.concatenate(total, axis=0) if by_rows else sum(total)
        for slot, ref in enumerate(out_refs):
            ref[...] = total[slot * rows : (slot + 1) * rows]

    with jax.sharding.use_abstract_mesh(mesh.abstract_mesh):
        sums = [pltpu.ACC(unit)((held_rows, tile), F32) for unit in range(2)]
        pl.run_scoped(multiply, *sums)


def project(mesh, at, arrays, parts, hops):
    train, _, query, _, pin, pout = arrays
    rank, ff = pin.shape
    width = pout.shape[1]
    rows = (train.shape[0] + query.shape[0]) // parts
    held = rows * len(hops)
    bf16 = jnp.bfloat16
    tile = 256
    return call(
        functools.partial(project_kernel, mesh, parts, hops, tile),
        [jax.ShapeDtypeStruct((rows, 2 * rank), F32)] * len(hops),
        "project_" + "_".join(str(hop) for hop in hops),
        in_specs=[SMEM_SPEC] + [HBM_SPEC] * 6,
        out_specs=[VMEM_SPEC] * len(hops),
        scratch_shapes=[
            pltpu.VMEM((held, ff), bf16),
            pltpu.VMEM((held, width), bf16),
            pltpu.VMEM((rank, ff), bf16),
            pltpu.VMEM((rank, width), bf16),
            pltpu.SemaphoreType.DMA((2 + 6 * len(hops),)),
        ],
        cost_estimate=pl.CostEstimate(
            flops=2 * held * (ff + width) * rank,
            bytes_accessed=2 * (held + rank) * (ff + width),
            transcendentals=0,
        ),
    )(at, *[pltpu.with_memory_space_constraint(array, pltpu.HBM) for array in arrays])


def halves(value):
    high = value.astype(jnp.bfloat16)
    return high, (value - high.astype(F32)).astype(jnp.bfloat16)


def outer_kernel(share, qshare, at_ref, quarter_ref, ids_ref, qids_ref, *refs):
    tok_refs, (keep_ref, send_ref, scratch) = refs[:-3], refs[-3:]
    at, mine = at_ref[0], quarter_ref[0]
    seq_len = ids_ref.shape[1]
    rank = tok_refs[0].shape[1] // 2
    qtok = qids_ref.shape[1]
    half = rank // 8

    def total(start, rows):
        value = tok_refs[0][start : start + rows, :]
        for ref in tok_refs[1:]:
            value = value + ref[start : start + rows, :]
        return value

    def product(lefts, tokens):
        left = jnp.concatenate([part for value in lefts for part in halves(value)], axis=0)
        right = jnp.concatenate(halves(tokens), axis=1)
        out = jnp.dot(left, right, preferred_element_type=F32)
        out = out[:, : 2 * rank] + out[:, 2 * rank :]
        sums = []
        for index in range(len(lefts)):
            start = 2 * rank * index
            sums.append(out[start : start + rank] + out[start + rank : start + 2 * rank])
        return sums

    def store(slot, outer):
        for quarter in range(4):
            start = quarter * 2 * half
            scratch[quarter, slot] = jnp.concatenate(
                [outer[start : start + half, rank:], outer[start + half : start + 2 * half, rank:]],
                axis=1,
            )

    for seq in range(share):
        tokens = total(seq * seq_len, seq_len)
        mask = (ids_ref[pl.ds(at * share + seq, 1), :] != PAD_ID).astype(F32)
        (outer,) = product([tokens.T[:rank] * mask], tokens)
        store(seq, outer / jnp.sum(mask, axis=1, keepdims=True))

    for quarter in range(4):
        scratch[quarter, share + qshare] = jnp.ones((half, 2 * rank), F32)
    tokens = total(share * seq_len, qshare * qtok)
    left = tokens.T[:rank]
    owner = lax.broadcasted_iota(jnp.int32, (1, qshare * qtok), 1) // qtok
    lefts = []
    for query in range(qshare):
        mask = (qids_ref[pl.ds(at * qshare + query, 1), :] != PAD_ID).astype(F32)
        lefts.append(left * jnp.where(owner == query, jnp.concatenate([mask] * qshare, axis=1), 0.0))
        count = jnp.broadcast_to(jnp.sum(mask, axis=1, keepdims=True), (1, 2 * rank))
        for quarter in range(4):
            scratch[quarter, share + qshare, query : query + 1, :] = count
    for query, outer in enumerate(product(lefts, tokens)):
        store(share + query, outer)
    for flip in range(2):
        keep_ref[flip] = scratch[mine ^ flip]
        send_ref[flip] = scratch[mine ^ 2 ^ flip]


def as_rows(values):
    half = values[0].shape[1]
    return jnp.concatenate(
        [
            jnp.concatenate([value[:, row, :] for value in values], axis=0) for row in range(half)
        ],
        axis=1,
    )


def rows_kernel(qshare, whole_ref, *refs):
    own = whole_ref.at[: whole_ref.shape[0] - qshare]
    refs[-1][...] = as_rows([own, *refs[:-1]])


def gram_kernel(qshare, hops, at_ref, first_ref, *refs):
    piece_refs, (out_ref, scratch) = refs[:-2], refs[-2:]
    nquery = scratch.shape[0]
    examples = []
    for hop, ref in zip(hops, piece_refs):
        nex = ref.shape[0] - qshare
        if hop:
            examples.append(ref.at[:nex])
        scratch[pl.ds((at_ref[0] ^ hop) * qshare, qshare)] = ref[nex:]
    both = jnp.concatenate([first_ref[...], as_rows([*examples, scratch])], axis=0)
    ntrain = both.shape[0] - nquery
    size = ntrain + nquery
    high, low = halves(both)
    gap = jnp.zeros((-size % 128, both.shape[1]), high.dtype)
    left = jnp.concatenate([high, low], axis=0)
    right = jnp.concatenate([high, gap, low], axis=0)
    total = lax.dot_general(left, right, NT, preferred_element_type=F32)
    total = total[:size] + total[size:]
    total = total[:, :size] + total[:, size + gap.shape[0] :]
    if folds(ntrain):
        half = ntrain // 2
        out_ref[:half, :] = jnp.concatenate([total[:half, :ntrain], total[half:ntrain, :ntrain]], axis=1)
        rest = [total[start : start + nquery, ntrain:] for start in range(0, size, nquery)]
        rest.append(jnp.zeros((nquery, 2 * ntrain - size), F32))
        out_ref[half:, :] = jnp.concatenate(rest, axis=1)
    else:
        out_ref[...] = total


def folds(ntrain):
    return 2 * ntrain <= 128


def solve_kernel(ntrain, feat, share, low_ref, one_ref, two_ref, out_ref, columns):
    nquery = out_ref.shape[1]
    whole = one_ref[...] + two_ref[...]
    if folds(ntrain):
        half = ntrain // 2
        gram = jnp.concatenate([whole[:half, :ntrain], whole[:half, ntrain:]], axis=0)
        rest = whole[half:]
        cross = [rest[:, start : start + nquery] for start in range(0, ntrain, nquery)]
        cross = jnp.concatenate(cross, axis=0)
        square = rest[:, ntrain : ntrain + nquery]
    else:
        gram = whole[:ntrain, :ntrain]
        cross = whole[:ntrain, ntrain:]
        square = whole[ntrain:, ntrain:]

    def colsum(v):
        return jnp.sum(v, axis=0, keepdims=True)

    def diagonal(v):
        rows = lax.broadcasted_iota(jnp.int32, v.shape, 0)
        cols = lax.broadcasted_iota(jnp.int32, v.shape, 1)
        return jnp.where(rows == cols, v, 0.0)

    norm = colsum(diagonal(square))
    trace = jnp.sum(colsum(diagonal(gram)), axis=1, keepdims=True) / ntrain
    scale = 1.0 / (ntrain * (DAMP * trace / feat))

    def thirds(value):
        high, rest = halves(value)
        low = value - high.astype(F32) - rest.astype(F32)
        return high, rest, low.astype(jnp.bfloat16)

    gram_parts = jnp.concatenate(thirds(gram), axis=0)

    def times_gram(value):
        out = sum(
            jnp.dot(gram_parts, part, preferred_element_type=F32) for part in thirds(value)[::-1]
        )
        return out[2 * ntrain :] + out[ntrain : 2 * ntrain] + out[:ntrain]

    res_a, res_x, res_p = jnp.ones_like(norm), jnp.zeros_like(cross), cross
    dir_a, dir_x, dir_p = res_a, res_x, res_p
    solved = jnp.zeros_like(cross)
    now = norm
    for step in range(ITERS):
        inner = dir_p * dir_p * scale
        if step:
            inner = inner + dir_x * (dir_a * cross + dir_p)
        alpha = now / (dir_a * dir_a * norm + colsum(inner))
        solved = solved + alpha * dir_p
        if step == ITERS - 1:
            break
        res_a = res_a - alpha * dir_a
        res_x = res_x - alpha * (dir_x + dir_p * scale)
        res_p = res_a * cross + times_gram(res_x)
        fresh = res_a * res_a * norm + colsum(res_x * (res_a * cross + res_p))
        beta = fresh / now
        dir_a = res_a + beta * dir_a
        dir_x = res_x + beta * dir_x
        dir_p = res_p + beta * dir_p
        now = fresh
    columns[...] = solved
    out_ref[...] = columns[pl.ds(low_ref[0] * share, share), :]


def per_device(
    mesh, train_hidden, train_grads, train_ids, query_hidden, query_grads, query_ids, proj_in, proj_out
):
    parts = lax.axis_size("tensor")
    groups = lax.axis_size("dp")
    at = lax.axis_index("tensor").astype(jnp.int32).reshape(1)
    group = lax.axis_index("dp").astype(jnp.int32)
    low = (group & 3).reshape(1)
    steady = group
    for bit in range(1, (groups - 1).bit_length()):
        steady = steady ^ (group >> bit)
    quarter = ((steady & 1) * 2 + (low >> 1)).reshape(1)
    nseq, seq_len, ff = train_hidden.shape
    width = train_grads.shape[2]
    rank = proj_in.shape[1]
    nquery, qtok, _ = query_hidden.shape
    ntrain = nseq * groups
    share = nseq // parts
    qshare = nquery // parts
    half = rank // 8

    arrays = (
        train_hidden.reshape(nseq * seq_len, ff),
        train_grads.reshape(nseq * seq_len, width),
        query_hidden.reshape(nquery * qtok, ff),
        query_grads.reshape(nquery * qtok, width),
        proj_in.T,
        proj_out.T,
    )
    pieces = {}
    turn = at
    for hops in ((3,), (2, 1), (0,)):
        values = project(mesh, turn, arrays, parts, hops)
        turn, *values = lax.optimization_barrier((turn, *values))
        for hop, value in zip(hops, values):
            pieces[hop] = swap(value, 0, hop) if hop else value

    early = pieces[3] + pieces[0]
    rows = share + qshare + 1
    keep, send = call(
        functools.partial(outer_kernel, share, qshare),
        [jax.ShapeDtypeStruct((2, rows, half, 2 * rank), F32)] * 2,
        "outer",
        in_specs=[SMEM_SPEC] * 2 + [VMEM_SPEC] * 5,
        scratch_shapes=[pltpu.VMEM((4, rows, half, 2 * rank), F32)],
    )(at, quarter, train_ids, query_ids, early, pieces[2], pieces[1])

    def ordered(bit, mine, other):
        nex = mine.shape[-3] - qshare - 1
        first = jnp.where(bit == 0, mine, other)[..., :nex, :, :]
        second = jnp.where(bit == 0, other, mine)[..., :nex, :, :]
        return jnp.concatenate([first, second, (mine + other)[..., nex:, :, :]], axis=-3)

    both = ordered(low[0] & 1, keep, swap(send, 1, 0))
    block = ordered(low[0] >> 1, both[0], swap(both[1], 3, 0))
    flip = 4
    while 2 * flip < groups:
        block = ordered(0, block, swap(block, flip | 1, 0))
        flip *= 2
    nex = block.shape[0] - qshare - 1
    own = block[:nex]
    other = swap(block, flip | 1, 0)
    ahead = {hop: swap(own, 0, hop) for hop in (2, 1)}
    rest = (block + other)[nex:]
    after = jnp.concatenate([other[:nex], rest[:qshare] / rest[qshare, :qshare, None, :]], axis=0)
    whole = jnp.concatenate([own, after], axis=0)

    far = swap(whole, 0, 3)
    behind = {
        2: swap(lax.optimization_barrier((after, ahead[2], ahead[1]))[0], 0, 2),
        1: swap(after, 0, 1),
    }
    first = call(
        functools.partial(rows_kernel, qshare),
        jax.ShapeDtypeStruct((4 * nex, half * 2 * rank), F32),
        "rows",
    )(whole, ahead[1], ahead[2])
    blocks = [whole, behind[1], far, behind[2]]
    hops = (0, 1, 3, 2)
    size = ntrain + nquery
    shape = (ntrain // 2 + nquery, 2 * ntrain) if folds(ntrain) else (size, size)
    gram = call(
        functools.partial(gram_kernel, qshare, hops),
        jax.ShapeDtypeStruct(shape, F32),
        "gram",
        in_specs=[SMEM_SPEC] + [VMEM_SPEC] * (1 + len(blocks)),
        scratch_shapes=[pltpu.VMEM((nquery, half, 2 * rank), F32)],
    )(at, first, *blocks)
    gram = gram + swap(gram, 3, 0)
    return call(
        functools.partial(solve_kernel, ntrain, rank * rank, share),
        jax.ShapeDtypeStruct((share, nquery), F32),
        "solve",
        in_specs=[SMEM_SPEC] + [VMEM_SPEC] * 2,
        scratch_shapes=[pltpu.VMEM((ntrain, nquery), F32)],
    )(low, gram, swap(gram, 1, 0)).T


def solution(mesh):
    return jax.shard_map(
        functools.partial(per_device, mesh),
        mesh=mesh,
        in_specs=(
            P("dp", None, "tensor"),
            P("dp", None, "tensor"),
            P("dp", None),
            P(None, "dp", "tensor"),
            P(None, "dp", "tensor"),
            P(None, "dp"),
            P("tensor", None),
            P("tensor", None),
        ),
        out_specs=P(None, ("dp", "tensor")),
        check_vma=False,
    )
```

```python
import functools

import jax
import jax.numpy as jnp
from jax import lax
from jax.experimental import pallas as pl
from jax.experimental.pallas import tpu as pltpu
from jax.sharding import PartitionSpec as P

ITERS = 3
PAD_ID = 128004
DAMP = 0.1
HIGHEST = lax.Precision.HIGHEST
F32 = jnp.float32
VMEM_LIMIT = 32 * 1024 * 1024
NT = (((1,), (1,)), ((), ()))
SMEM_SPEC = pl.BlockSpec(memory_space=pltpu.SMEM)
VMEM_SPEC = pl.BlockSpec(memory_space=pltpu.VMEM)
HBM_SPEC = pl.BlockSpec(memory_space=pltpu.HBM)


def call(kernel, out_shape, name, **kwargs):
    return pl.pallas_call(
        kernel,
        out_shape=out_shape,
        name=name,
        compiler_params=pltpu.CompilerParams(vmem_limit_bytes=VMEM_LIMIT),
        **kwargs,
    )


def swap(value, dp_flip, tensor_flip):
    groups, parts = lax.axis_size("dp"), lax.axis_size("tensor")
    flip = dp_flip * parts + tensor_flip
    return lax.ppermute(value, ("dp", "tensor"), [(i, i ^ flip) for i in range(groups * parts)])


def project_kernel(mesh, parts, hops, tile, at_ref, th_ref, tg_ref, qh_ref, qg_ref, pin_ref, pout_ref, *refs):
    out_refs = refs[: len(hops)]
    hid, grad, pin, pout, sems = refs[len(hops) :]
    at = at_ref[0]
    trows = th_ref.shape[0] // parts
    qrows = qh_ref.shape[0] // parts
    rows = trows + qrows
    rank = pin_ref.shape[0]
    sides = ((th_ref, qh_ref, hid, pin_ref, pin), (tg_ref, qg_ref, grad, pout_ref, pout))
    chunks = []
    started = 0
    for side in (1, 0):
        train, query, buf, weight, held = sides[side]
        wide = buf.shape[1]
        first = wide if side else 4 * tile
        second = (wide - first + tile) // (2 * tile) * tile
        for start, size in ((0, first), (first, second), (first + second, wide - first - second)):
            if not size:
                continue
            cols = pl.ds(start, size)
            pairs = [] if start else [(weight, held)]
            for slot, hop in enumerate(hops):
                to = at ^ hop
                tsrc = pl.ds(pl.multiple_of(to * trows, trows), trows)
                pairs.append((train.at[tsrc, cols], buf.at[pl.ds(slot * rows, trows), cols]))
            for slot, hop in enumerate(() if start else hops):
                to = at ^ hop
                qsrc = pl.ds(pl.multiple_of(to * qrows, qrows), qrows)
                pairs.append((query.at[qsrc, :], buf.at[pl.ds(slot * rows + trows, qrows), :]))
            copies = []
            for src, dst in pairs:
                copies.append(pltpu.make_async_copy(src, dst, sems.at[started]))
                copies[-1].start()
                started += 1
            chunks.append((side, start, size, copies))

    by_rows = len(hops) > 1
    held_rows = hid.shape[0] // 2 if by_rows else hid.shape[0]

    def multiply(*sums):
        used = [0] * len(sums)
        for side in (1, 0):
            _, _, buf, _, held = sides[side]
            mine = [chunk for chunk in chunks if chunk[0] == side]
            tiles = range(0, buf.shape[1], tile)
            turns = [
                list(tiles) if by_rows else list(tiles)[unit :: len(sums)]
                for unit in range(len(sums))
            ]

            def push(unit, place):
                if place >= len(turns[unit]):
                    return
                col = turns[unit][place]
                weight = [held[:, col : col + tile]]
                if side:
                    weight.insert(0, jnp.zeros((side * rank, tile), held.dtype))
                weight.append(jnp.zeros((tile - (side + 1) * rank, tile), held.dtype))
                weight = jnp.concatenate(weight, axis=0)
                pltpu.matmul_push_rhs(weight, (used[unit] + place) % 2, unit, transpose=True)

            mine[0][3][0].wait()
            for place in range(2):
                for unit in range(len(sums)):
                    push(unit, place)
            for _, start, size, copies in mine:
                for copy in copies[0 if start else 1 :]:
                    copy.wait()
                for col in range(start, start + size, tile):
                    for unit, acc in enumerate(sums):
                        if col not in turns[unit]:
                            continue
                        place = turns[unit].index(col)
                        first = unit * held_rows if by_rows else 0
                        tokens = buf[first : first + held_rows, col : col + tile]
                        pltpu.matmul_acc_lhs(
                            acc, tokens, load_staged_rhs=(used[unit] + place) % 2
                        )
                        push(unit, place + 2)
            for unit in range(len(sums)):
                used[unit] += len(turns[unit])
        total = [pltpu.matmul_pop(acc)[:, : 2 * rank] for acc in sums]
        total = jnp.concatenate(total, axis=0) if by_rows else sum(total)
        for slot, ref in enumerate(out_refs):
            ref[...] = total[slot * rows : (slot + 1) * rows]

    with jax.sharding.use_abstract_mesh(mesh.abstract_mesh):
        sums = [pltpu.ACC(unit)((held_rows, tile), F32) for unit in range(2)]
        pl.run_scoped(multiply, *sums)


def project(mesh, at, arrays, parts, hops):
    train, _, query, _, pin, pout = arrays
    rank, ff = pin.shape
    width = pout.shape[1]
    rows = (train.shape[0] + query.shape[0]) // parts
    held = rows * len(hops)
    bf16 = jnp.bfloat16
    tile = 256
    return call(
        functools.partial(project_kernel, mesh, parts, hops, tile),
        [jax.ShapeDtypeStruct((rows, 2 * rank), F32)] * len(hops),
        "project_" + "_".join(str(hop) for hop in hops),
        in_specs=[SMEM_SPEC] + [HBM_SPEC] * 6,
        out_specs=[VMEM_SPEC] * len(hops),
        scratch_shapes=[
            pltpu.VMEM((held, ff), bf16),
            pltpu.VMEM((held, width), bf16),
            pltpu.VMEM((rank, ff), bf16),
            pltpu.VMEM((rank, width), bf16),
            pltpu.SemaphoreType.DMA((2 + 6 * len(hops),)),
        ],
        cost_estimate=pl.CostEstimate(
            flops=2 * held * (ff + width) * rank,
            bytes_accessed=2 * (held + rank) * (ff + width),
            transcendentals=0,
        ),
    )(at, *[pltpu.with_memory_space_constraint(array, pltpu.HBM) for array in arrays])


def halves(value):
    high = value.astype(jnp.bfloat16)
    return high, (value - high.astype(F32)).astype(jnp.bfloat16)


def outer_kernel(share, qshare, at_ref, quarter_ref, ids_ref, qids_ref, *refs):
    tok_refs, (keep_ref, send_ref, scratch) = refs[:-3], refs[-3:]
    at, mine = at_ref[0], quarter_ref[0]
    seq_len = ids_ref.shape[1]
    rank = tok_refs[0].shape[1] // 2
    qtok = qids_ref.shape[1]
    half = rank // 8

    def total(start, rows):
        value = tok_refs[0][start : start + rows, :]
        for ref in tok_refs[1:]:
            value = value + ref[start : start + rows, :]
        return value

    def product(lefts, tokens):
        left = jnp.concatenate([part for value in lefts for part in halves(value)], axis=0)
        right = jnp.concatenate(halves(tokens), axis=1)
        out = jnp.dot(left, right, preferred_element_type=F32)
        out = out[:, : 2 * rank] + out[:, 2 * rank :]
        sums = []
        for index in range(len(lefts)):
            start = 2 * rank * index
            sums.append(out[start : start + rank] + out[start + rank : start + 2 * rank])
        return sums

    def store(slot, outer):
        for quarter in range(4):
            start = quarter * 2 * half
            scratch[quarter, slot] = jnp.concatenate(
                [outer[start : start + half, rank:], outer[start + half : start + 2 * half, rank:]],
                axis=1,
            )

    for seq in range(share):
        tokens = total(seq * seq_len, seq_len)
        mask = (ids_ref[pl.ds(at * share + seq, 1), :] != PAD_ID).astype(F32)
        (outer,) = product([tokens.T[:rank] * mask], tokens)
        store(seq, outer / jnp.sum(mask, axis=1, keepdims=True))

    for quarter in range(4):
        scratch[quarter, share + qshare] = jnp.ones((half, 2 * rank), F32)
    tokens = total(share * seq_len, qshare * qtok)
    left = tokens.T[:rank]
    owner = lax.broadcasted_iota(jnp.int32, (1, qshare * qtok), 1) // qtok
    lefts = []
    for query in range(qshare):
        mask = (qids_ref[pl.ds(at * qshare + query, 1), :] != PAD_ID).astype(F32)
        lefts.append(left * jnp.where(owner == query, jnp.concatenate([mask] * qshare, axis=1), 0.0))
        count = jnp.broadcast_to(jnp.sum(mask, axis=1, keepdims=True), (1, 2 * rank))
        for quarter in range(4):
            scratch[quarter, share + qshare, query : query + 1, :] = count
    for query, outer in enumerate(product(lefts, tokens)):
        store(share + query, outer)
    for flip in range(2):
        keep_ref[flip] = scratch[mine ^ flip]
        send_ref[flip] = scratch[mine ^ 2 ^ flip]


def as_rows(values):
    half = values[0].shape[1]
    return jnp.concatenate(
        [
            jnp.concatenate([value[:, row, :] for value in values], axis=0) for row in range(half)
        ],
        axis=1,
    )


def rows_kernel(qshare, whole_ref, *refs):
    own = whole_ref.at[: whole_ref.shape[0] - qshare]
    refs[-1][...] = as_rows([own, *refs[:-1]])


def gram_kernel(qshare, hops, at_ref, first_ref, *refs):
    piece_refs, (out_ref, scratch) = refs[:-2], refs[-2:]
    nquery = scratch.shape[0]
    examples = []
    for hop, ref in zip(hops, piece_refs):
        nex = ref.shape[0] - qshare
        if hop:
            examples.append(ref.at[:nex])
        scratch[pl.ds((at_ref[0] ^ hop) * qshare, qshare)] = ref[nex:]
    both = jnp.concatenate([first_ref[...], as_rows([*examples, scratch])], axis=0)
    ntrain = both.shape[0] - nquery
    size = ntrain + nquery
    high, low = halves(both)
    gap = jnp.zeros((-size % 128, both.shape[1]), high.dtype)
    left = jnp.concatenate([high, low], axis=0)
    right = jnp.concatenate([high, gap, low], axis=0)
    total = lax.dot_general(left, right, NT, preferred_element_type=F32)
    total = total[:size] + total[size:]
    total = total[:, :size] + total[:, size + gap.shape[0] :]
    if folds(ntrain):
        half = ntrain // 2
        out_ref[:half, :] = jnp.concatenate([total[:half, :ntrain], total[half:ntrain, :ntrain]], axis=1)
        rest = [total[start : start + nquery, ntrain:] for start in range(0, size, nquery)]
        rest.append(jnp.zeros((nquery, 2 * ntrain - size), F32))
        out_ref[half:, :] = jnp.concatenate(rest, axis=1)
    else:
        out_ref[...] = total


def folds(ntrain):
    return 2 * ntrain <= 128


def solve_kernel(ntrain, feat, share, low_ref, one_ref, two_ref, out_ref, columns):
    nquery = out_ref.shape[1]
    whole = one_ref[...] + two_ref[...]
    if folds(ntrain):
        half = ntrain // 2
        gram = jnp.concatenate([whole[:half, :ntrain], whole[:half, ntrain:]], axis=0)
        rest = whole[half:]
        cross = [rest[:, start : start + nquery] for start in range(0, ntrain, nquery)]
        cross = jnp.concatenate(cross, axis=0)
        square = rest[:, ntrain : ntrain + nquery]
    else:
        gram = whole[:ntrain, :ntrain]
        cross = whole[:ntrain, ntrain:]
        square = whole[ntrain:, ntrain:]

    def colsum(v):
        return jnp.sum(v, axis=0, keepdims=True)

    def diagonal(v):
        rows = lax.broadcasted_iota(jnp.int32, v.shape, 0)
        cols = lax.broadcasted_iota(jnp.int32, v.shape, 1)
        return jnp.where(rows == cols, v, 0.0)

    norm = colsum(diagonal(square))
    trace = jnp.sum(colsum(diagonal(gram)), axis=1, keepdims=True) / ntrain
    scale = 1.0 / (ntrain * (DAMP * trace / feat))

    def thirds(value):
        high, rest = halves(value)
        low = value - high.astype(F32) - rest.astype(F32)
        return high, rest, low.astype(jnp.bfloat16)

    gram_parts = jnp.concatenate(thirds(gram), axis=0)

    def times_gram(value):
        out = sum(
            jnp.dot(gram_parts, part, preferred_element_type=F32) for part in thirds(value)[::-1]
        )
        return out[2 * ntrain :] + out[ntrain : 2 * ntrain] + out[:ntrain]

    res_a, res_x, res_p = jnp.ones_like(norm), jnp.zeros_like(cross), cross
    dir_a, dir_x, dir_p = res_a, res_x, res_p
    solved = jnp.zeros_like(cross)
    now = norm
    for step in range(ITERS):
        inner = dir_p * dir_p * scale
        if step:
            inner = inner + dir_x * (dir_a * cross + dir_p)
        alpha = now / (dir_a * dir_a * norm + colsum(inner))
        solved = solved + alpha * dir_p
        if step == ITERS - 1:
            break
        res_a = res_a - alpha * dir_a
        res_x = res_x - alpha * (dir_x + dir_p * scale)
        res_p = res_a * cross + times_gram(res_x)
        fresh = res_a * res_a * norm + colsum(res_x * (res_a * cross + res_p))
        beta = fresh / now
        dir_a = res_a + beta * dir_a
        dir_x = res_x + beta * dir_x
        dir_p = res_p + beta * dir_p
        now = fresh
    columns[...] = solved
    out_ref[...] = columns[pl.ds(low_ref[0] * share, share), :]


def per_device(
    mesh, train_hidden, train_grads, train_ids, query_hidden, query_grads, query_ids, proj_in, proj_out
):
    parts = lax.axis_size("tensor")
    groups = lax.axis_size("dp")
    at = lax.axis_index("tensor").astype(jnp.int32).reshape(1)
    group = lax.axis_index("dp").astype(jnp.int32)
    low = (group & 3).reshape(1)
    steady = group
    for bit in range(1, (groups - 1).bit_length()):
        steady = steady ^ (group >> bit)
    quarter = ((steady & 1) * 2 + (low >> 1)).reshape(1)
    nseq, seq_len, ff = train_hidden.shape
    width = train_grads.shape[2]
    rank = proj_in.shape[1]
    nquery, qtok, _ = query_hidden.shape
    ntrain = nseq * groups
    share = nseq // parts
    qshare = nquery // parts
    half = rank // 8

    arrays = (
        train_hidden.reshape(nseq * seq_len, ff),
        train_grads.reshape(nseq * seq_len, width),
        query_hidden.reshape(nquery * qtok, ff),
        query_grads.reshape(nquery * qtok, width),
        proj_in.T,
        proj_out.T,
    )
    pieces = {}
    turn = at
    for hops in ((3,), (2, 1), (0,)):
        values = project(mesh, turn, arrays, parts, hops)
        turn, *values = lax.optimization_barrier((turn, *values))
        for hop, value in zip(hops, values):
            pieces[hop] = swap(value, 0, hop) if hop else value

    early = pieces[3] + pieces[0]
    rows = share + qshare + 1
    keep, send = call(
        functools.partial(outer_kernel, share, qshare),
        [jax.ShapeDtypeStruct((2, rows, half, 2 * rank), F32)] * 2,
        "outer",
        in_specs=[SMEM_SPEC] * 2 + [VMEM_SPEC] * 5,
        scratch_shapes=[pltpu.VMEM((4, rows, half, 2 * rank), F32)],
    )(at, quarter, train_ids, query_ids, early, pieces[2], pieces[1])

    def ordered(bit, mine, other):
        nex = mine.shape[-3] - qshare - 1
        first = jnp.where(bit == 0, mine, other)[..., :nex, :, :]
        second = jnp.where(bit == 0, other, mine)[..., :nex, :, :]
        return jnp.concatenate([first, second, (mine + other)[..., nex:, :, :]], axis=-3)

    both = ordered(low[0] & 1, keep, swap(send, 1, 0))
    block = ordered(low[0] >> 1, both[0], swap(both[1], 3, 0))
    flip = 4
    while 2 * flip < groups:
        block = ordered(0, block, swap(block, flip | 1, 0))
        flip *= 2
    nex = block.shape[0] - qshare - 1
    own = block[:nex]
    other = swap(block, flip | 1, 0)
    ahead = {hop: swap(own, 0, hop) for hop in (2, 1)}
    rest = (block + other)[nex:]
    after = jnp.concatenate([other[:nex], rest[:qshare] / rest[qshare, :qshare, None, :]], axis=0)
    whole = jnp.concatenate([own, after], axis=0)

    far = swap(whole, 0, 3)
    behind = {
        2: swap(lax.optimization_barrier((after, ahead[2], ahead[1]))[0], 0, 2),
        1: swap(after, 0, 1),
    }
    first = call(
        functools.partial(rows_kernel, qshare),
        jax.ShapeDtypeStruct((4 * nex, half * 2 * rank), F32),
        "rows",
    )(whole, ahead[1], ahead[2])
    blocks = [whole, behind[1], far, behind[2]]
    hops = (0, 1, 3, 2)
    size = ntrain + nquery
    shape = (ntrain // 2 + nquery, 2 * ntrain) if folds(ntrain) else (size, size)
    gram = call(
        functools.partial(gram_kernel, qshare, hops),
        jax.ShapeDtypeStruct(shape, F32),
        "gram",
        in_specs=[SMEM_SPEC] + [VMEM_SPEC] * (1 + len(blocks)),
        scratch_shapes=[pltpu.VMEM((nquery, half, 2 * rank), F32)],
    )(at, first, *blocks)
    gram = gram + swap(gram, 3, 0)
    return call(
        functools.partial(solve_kernel, ntrain, rank * rank, share),
        jax.ShapeDtypeStruct((share, nquery), F32),
        "solve",
        in_specs=[SMEM_SPEC] + [VMEM_SPEC] * 2,
        scratch_shapes=[pltpu.VMEM((ntrain, nquery), F32)],
    )(low, gram, swap(gram, 1, 0)).T


def solution(mesh):
    return jax.shard_map(
        functools.partial(per_device, mesh),
        mesh=mesh,
        in_specs=(
            P("dp", None, "tensor"),
            P("dp", None, "tensor"),
            P("dp", None),
            P(None, "dp", "tensor"),
            P(None, "dp", "tensor"),
            P(None, "dp"),
            P("tensor", None),
            P("tensor", None),
        ),
        out_specs=P(None, ("dp", "tensor")),
        check_vma=False,
    )
```

```python
import functools

import jax
import jax.numpy as jnp
from jax import lax
from jax.experimental import pallas as pl
from jax.experimental.pallas import tpu as pltpu
from jax.sharding import PartitionSpec as P

ITERS = 3
PAD_ID = 128004
DAMP = 0.1
HIGHEST = lax.Precision.HIGHEST
F32 = jnp.float32
VMEM_LIMIT = 32 * 1024 * 1024
NT = (((1,), (1,)), ((), ()))
SMEM_SPEC = pl.BlockSpec(memory_space=pltpu.SMEM)
VMEM_SPEC = pl.BlockSpec(memory_space=pltpu.VMEM)
HBM_SPEC = pl.BlockSpec(memory_space=pltpu.HBM)


def call(kernel, out_shape, name, **kwargs):
    return pl.pallas_call(
        kernel,
        out_shape=out_shape,
        name=name,
        compiler_params=pltpu.CompilerParams(vmem_limit_bytes=VMEM_LIMIT),
        **kwargs,
    )


def swap(value, dp_flip, tensor_flip):
    groups, parts = lax.axis_size("dp"), lax.axis_size("tensor")
    flip = dp_flip * parts + tensor_flip
    return lax.ppermute(value, ("dp", "tensor"), [(i, i ^ flip) for i in range(groups * parts)])


def project_kernel(mesh, parts, hops, tile, at_ref, th_ref, tg_ref, qh_ref, qg_ref, pin_ref, pout_ref, *refs):
    out_refs = refs[: len(hops)]
    hid, grad, pin, pout, sems = refs[len(hops) :]
    at = at_ref[0]
    trows = th_ref.shape[0] // parts
    qrows = qh_ref.shape[0] // parts
    rows = trows + qrows
    rank = pin_ref.shape[0]
    sides = ((th_ref, qh_ref, hid, pin_ref, pin), (tg_ref, qg_ref, grad, pout_ref, pout))
    chunks = []
    started = 0
    for side in (1, 0):
        train, query, buf, weight, held = sides[side]
        wide = buf.shape[1]
        for start, size in ((0, wide),):
            cols = pl.ds(start, size)
            pairs = [] if start else [(weight, held)]
            for slot, hop in enumerate(hops):
                to = at ^ hop
                tsrc = pl.ds(pl.multiple_of(to * trows, trows), trows)
                pairs.append((train.at[tsrc, cols], buf.at[pl.ds(slot * rows, trows), cols]))
            for slot, hop in enumerate(() if start else hops):
                to = at ^ hop
                qsrc = pl.ds(pl.multiple_of(to * qrows, qrows), qrows)
                pairs.append((query.at[qsrc, :], buf.at[pl.ds(slot * rows + trows, qrows), :]))
            copies = []
            for src, dst in pairs:
                copies.append(pltpu.make_async_copy(src, dst, sems.at[started]))
                copies[-1].start()
                started += 1
            chunks.append((side, start, size, copies))

    by_rows = len(hops) > 1
    held_rows = hid.shape[0] // 2 if by_rows else hid.shape[0]

    def multiply(*sums):
        used = [0] * len(sums)
        for side in (1, 0):
            _, _, buf, _, held = sides[side]
            mine = [chunk for chunk in chunks if chunk[0] == side]
            tiles = range(0, buf.shape[1], tile)
            turns = [
                list(tiles) if by_rows else list(tiles)[unit :: len(sums)]
                for unit in range(len(sums))
            ]

            def push(unit, place):
                if place >= len(turns[unit]):
                    return
                col = turns[unit][place]
                weight = [held[:, col : col + tile]]
                if side:
                    weight.insert(0, jnp.zeros((side * rank, tile), held.dtype))
                weight.append(jnp.zeros((tile - (side + 1) * rank, tile), held.dtype))
                weight = jnp.concatenate(weight, axis=0)
                pltpu.matmul_push_rhs(weight, (used[unit] + place) % 2, unit, transpose=True)

            mine[0][3][0].wait()
            for place in range(2):
                for unit in range(len(sums)):
                    push(unit, place)
            for _, start, size, copies in mine:
                for copy in copies[0 if start else 1 :]:
                    copy.wait()
                for col in range(start, start + size, tile):
                    for unit, acc in enumerate(sums):
                        if col not in turns[unit]:
                            continue
                        place = turns[unit].index(col)
                        first = unit * held_rows if by_rows else 0
                        tokens = buf[first : first + held_rows, col : col + tile]
                        pltpu.matmul_acc_lhs(
                            acc, tokens, load_staged_rhs=(used[unit] + place) % 2
                        )
                        push(unit, place + 2)
            for unit in range(len(sums)):
                used[unit] += len(turns[unit])
        total = [pltpu.matmul_pop(acc)[:, : 2 * rank] for acc in sums]
        total = jnp.concatenate(total, axis=0) if by_rows else sum(total)
        for slot, ref in enumerate(out_refs):
            ref[...] = total[slot * rows : (slot + 1) * rows]

    with jax.sharding.use_abstract_mesh(mesh.abstract_mesh):
        sums = [pltpu.ACC(unit)((held_rows, tile), F32) for unit in range(2)]
        pl.run_scoped(multiply, *sums)


def project(mesh, at, arrays, parts, hops):
    train, _, query, _, pin, pout = arrays
    rank, ff = pin.shape
    width = pout.shape[1]
    rows = (train.shape[0] + query.shape[0]) // parts
    held = rows * len(hops)
    bf16 = jnp.bfloat16
    tile = 256
    return call(
        functools.partial(project_kernel, mesh, parts, hops, tile),
        [jax.ShapeDtypeStruct((rows, 2 * rank), F32)] * len(hops),
        "project_" + "_".join(str(hop) for hop in hops),
        in_specs=[SMEM_SPEC] + [HBM_SPEC] * 6,
        out_specs=[VMEM_SPEC] * len(hops),
        scratch_shapes=[
            pltpu.VMEM((held, ff), bf16),
            pltpu.VMEM((held, width), bf16),
            pltpu.VMEM((rank, ff), bf16),
            pltpu.VMEM((rank, width), bf16),
            pltpu.SemaphoreType.DMA((2 + 6 * len(hops),)),
        ],
        cost_estimate=pl.CostEstimate(
            flops=2 * held * (ff + width) * rank,
            bytes_accessed=2 * (held + rank) * (ff + width),
            transcendentals=0,
        ),
    )(at, *[pltpu.with_memory_space_constraint(array, pltpu.HBM) for array in arrays])


def halves(value):
    high = value.astype(jnp.bfloat16)
    return high, (value - high.astype(F32)).astype(jnp.bfloat16)


def outer_kernel(share, qshare, at_ref, quarter_ref, ids_ref, qids_ref, *refs):
    tok_refs, (keep_ref, send_ref, scratch) = refs[:-3], refs[-3:]
    at, mine = at_ref[0], quarter_ref[0]
    seq_len = ids_ref.shape[1]
    rank = tok_refs[0].shape[1] // 2
    qtok = qids_ref.shape[1]
    half = rank // 8

    def total(start, rows):
        value = tok_refs[0][start : start + rows, :]
        for ref in tok_refs[1:]:
            value = value + ref[start : start + rows, :]
        return value

    def product(lefts, tokens):
        left = jnp.concatenate([part for value in lefts for part in halves(value)], axis=0)
        right = jnp.concatenate(halves(tokens), axis=1)
        out = jnp.dot(left, right, preferred_element_type=F32)
        out = out[:, : 2 * rank] + out[:, 2 * rank :]
        sums = []
        for index in range(len(lefts)):
            start = 2 * rank * index
            sums.append(out[start : start + rank] + out[start + rank : start + 2 * rank])
        return sums

    def store(slot, outer):
        for quarter in range(4):
            start = quarter * 2 * half
            scratch[quarter, slot] = jnp.concatenate(
                [outer[start : start + half, rank:], outer[start + half : start + 2 * half, rank:]],
                axis=1,
            )

    for seq in range(share):
        tokens = total(seq * seq_len, seq_len)
        mask = (ids_ref[pl.ds(at * share + seq, 1), :] != PAD_ID).astype(F32)
        (outer,) = product([tokens.T[:rank] * mask], tokens)
        store(seq, outer / jnp.sum(mask, axis=1, keepdims=True))

    for quarter in range(4):
        scratch[quarter, share + qshare] = jnp.ones((half, 2 * rank), F32)
    tokens = total(share * seq_len, qshare * qtok)
    left = tokens.T[:rank]
    owner = lax.broadcasted_iota(jnp.int32, (1, qshare * qtok), 1) // qtok
    lefts = []
    for query in range(qshare):
        mask = (qids_ref[pl.ds(at * qshare + query, 1), :] != PAD_ID).astype(F32)
        lefts.append(left * jnp.where(owner == query, jnp.concatenate([mask] * qshare, axis=1), 0.0))
        count = jnp.broadcast_to(jnp.sum(mask, axis=1, keepdims=True), (1, 2 * rank))
        for quarter in range(4):
            scratch[quarter, share + qshare, query : query + 1, :] = count
    for query, outer in enumerate(product(lefts, tokens)):
        store(share + query, outer)
    for flip in range(2):
        keep_ref[flip] = scratch[mine ^ flip]
        send_ref[flip] = scratch[mine ^ 2 ^ flip]


def as_rows(values):
    half = values[0].shape[1]
    return jnp.concatenate(
        [
            jnp.concatenate([value[:, row, :] for value in values], axis=0) for row in range(half)
        ],
        axis=1,
    )


def rows_kernel(qshare, whole_ref, *refs):
    own = whole_ref.at[: whole_ref.shape[0] - qshare]
    refs[-1][...] = as_rows([own, *refs[:-1]])


def gram_kernel(qshare, hops, at_ref, first_ref, *refs):
    piece_refs, (out_ref, scratch) = refs[:-2], refs[-2:]
    nquery = scratch.shape[0]
    examples = []
    for hop, ref in zip(hops, piece_refs):
        nex = ref.shape[0] - qshare
        if hop:
            examples.append(ref.at[:nex])
        scratch[pl.ds((at_ref[0] ^ hop) * qshare, qshare)] = ref[nex:]
    both = jnp.concatenate([first_ref[...], as_rows([*examples, scratch])], axis=0)
    ntrain = both.shape[0] - nquery
    size = ntrain + nquery
    high, low = halves(both)
    gap = jnp.zeros((-size % 128, both.shape[1]), high.dtype)
    left = jnp.concatenate([high, low], axis=0)
    right = jnp.concatenate([high, gap, low], axis=0)
    total = lax.dot_general(left, right, NT, preferred_element_type=F32)
    total = total[:size] + total[size:]
    total = total[:, :size] + total[:, size + gap.shape[0] :]
    if folds(ntrain):
        half = ntrain // 2
        out_ref[:half, :] = jnp.concatenate([total[:half, :ntrain], total[half:ntrain, :ntrain]], axis=1)
        rest = [total[start : start + nquery, ntrain:] for start in range(0, size, nquery)]
        rest.append(jnp.zeros((nquery, 2 * ntrain - size), F32))
        out_ref[half:, :] = jnp.concatenate(rest, axis=1)
    else:
        out_ref[...] = total


def folds(ntrain):
    return 2 * ntrain <= 128


def solve_kernel(ntrain, feat, share, low_ref, one_ref, two_ref, out_ref, columns):
    nquery = out_ref.shape[1]
    whole = one_ref[...] + two_ref[...]
    if folds(ntrain):
        half = ntrain // 2
        gram = jnp.concatenate([whole[:half, :ntrain], whole[:half, ntrain:]], axis=0)
        rest = whole[half:]
        cross = [rest[:, start : start + nquery] for start in range(0, ntrain, nquery)]
        cross = jnp.concatenate(cross, axis=0)
        square = rest[:, ntrain : ntrain + nquery]
    else:
        gram = whole[:ntrain, :ntrain]
        cross = whole[:ntrain, ntrain:]
        square = whole[ntrain:, ntrain:]

    def colsum(v):
        return jnp.sum(v, axis=0, keepdims=True)

    def diagonal(v):
        rows = lax.broadcasted_iota(jnp.int32, v.shape, 0)
        cols = lax.broadcasted_iota(jnp.int32, v.shape, 1)
        return jnp.where(rows == cols, v, 0.0)

    norm = colsum(diagonal(square))
    trace = jnp.sum(colsum(diagonal(gram)), axis=1, keepdims=True) / ntrain
    scale = 1.0 / (ntrain * (DAMP * trace / feat))

    def thirds(value):
        high, rest = halves(value)
        low = value - high.astype(F32) - rest.astype(F32)
        return high, rest, low.astype(jnp.bfloat16)

    gram_parts = jnp.concatenate(thirds(gram), axis=0)

    def times_gram(value):
        out = sum(
            jnp.dot(gram_parts, part, preferred_element_type=F32) for part in thirds(value)[::-1]
        )
        return out[2 * ntrain :] + out[ntrain : 2 * ntrain] + out[:ntrain]

    res_a, res_x, res_p = jnp.ones_like(norm), jnp.zeros_like(cross), cross
    dir_a, dir_x, dir_p = res_a, res_x, res_p
    solved = jnp.zeros_like(cross)
    now = norm
    for step in range(ITERS):
        inner = dir_p * dir_p * scale
        if step:
            inner = inner + dir_x * (dir_a * cross + dir_p)
        alpha = now / (dir_a * dir_a * norm + colsum(inner))
        solved = solved + alpha * dir_p
        if step == ITERS - 1:
            break
        res_a = res_a - alpha * dir_a
        res_x = res_x - alpha * (dir_x + dir_p * scale)
        res_p = res_a * cross + times_gram(res_x)
        fresh = res_a * res_a * norm + colsum(res_x * (res_a * cross + res_p))
        beta = fresh / now
        dir_a = res_a + beta * dir_a
        dir_x = res_x + beta * dir_x
        dir_p = res_p + beta * dir_p
        now = fresh
    columns[...] = solved
    out_ref[...] = columns[pl.ds(low_ref[0] * share, share), :]


def per_device(
    mesh, train_hidden, train_grads, train_ids, query_hidden, query_grads, query_ids, proj_in, proj_out
):
    parts = lax.axis_size("tensor")
    groups = lax.axis_size("dp")
    at = lax.axis_index("tensor").astype(jnp.int32).reshape(1)
    group = lax.axis_index("dp").astype(jnp.int32)
    low = (group & 3).reshape(1)
    steady = group
    for bit in range(1, (groups - 1).bit_length()):
        steady = steady ^ (group >> bit)
    quarter = ((steady & 1) * 2 + (low >> 1)).reshape(1)
    nseq, seq_len, ff = train_hidden.shape
    width = train_grads.shape[2]
    rank = proj_in.shape[1]
    nquery, qtok, _ = query_hidden.shape
    ntrain = nseq * groups
    share = nseq // parts
    qshare = nquery // parts
    half = rank // 8

    arrays = (
        train_hidden.reshape(nseq * seq_len, ff),
        train_grads.reshape(nseq * seq_len, width),
        query_hidden.reshape(nquery * qtok, ff),
        query_grads.reshape(nquery * qtok, width),
        proj_in.T,
        proj_out.T,
    )
    pieces = {}
    turn = at
    for hops in ((3,), (2, 1), (0,)):
        values = project(mesh, turn, arrays, parts, hops)
        turn, *values = lax.optimization_barrier((turn, *values))
        for hop, value in zip(hops, values):
            pieces[hop] = swap(value, 0, hop) if hop else value

    early = pieces[3] + pieces[0]
    rows = share + qshare + 1
    keep, send = call(
        functools.partial(outer_kernel, share, qshare),
        [jax.ShapeDtypeStruct((2, rows, half, 2 * rank), F32)] * 2,
        "outer",
        in_specs=[SMEM_SPEC] * 2 + [VMEM_SPEC] * 5,
        scratch_shapes=[pltpu.VMEM((4, rows, half, 2 * rank), F32)],
    )(at, quarter, train_ids, query_ids, early, pieces[2], pieces[1])

    def ordered(bit, mine, other):
        nex = mine.shape[-3] - qshare - 1
        first = jnp.where(bit == 0, mine, other)[..., :nex, :, :]
        second = jnp.where(bit == 0, other, mine)[..., :nex, :, :]
        return jnp.concatenate([first, second, (mine + other)[..., nex:, :, :]], axis=-3)

    both = ordered(low[0] & 1, keep, swap(send, 1, 0))
    block = ordered(low[0] >> 1, both[0], swap(both[1], 3, 0))
    flip = 4
    while 2 * flip < groups:
        block = ordered(0, block, swap(block, flip | 1, 0))
        flip *= 2
    nex = block.shape[0] - qshare - 1
    own = block[:nex]
    other = swap(block, flip | 1, 0)
    ahead = {hop: swap(own, 0, hop) for hop in (2, 1)}
    rest = (block + other)[nex:]
    after = jnp.concatenate([other[:nex], rest[:qshare] / rest[qshare, :qshare, None, :]], axis=0)
    whole = jnp.concatenate([own, after], axis=0)

    far = swap(whole, 0, 3)
    behind = {
        2: swap(lax.optimization_barrier((after, ahead[2], ahead[1]))[0], 0, 2),
        1: swap(after, 0, 1),
    }
    first = call(
        functools.partial(rows_kernel, qshare),
        jax.ShapeDtypeStruct((4 * nex, half * 2 * rank), F32),
        "rows",
    )(whole, ahead[1], ahead[2])
    blocks = [whole, behind[1], far, behind[2]]
    hops = (0, 1, 3, 2)
    size = ntrain + nquery
    shape = (ntrain // 2 + nquery, 2 * ntrain) if folds(ntrain) else (size, size)
    gram = call(
        functools.partial(gram_kernel, qshare, hops),
        jax.ShapeDtypeStruct(shape, F32),
        "gram",
        in_specs=[SMEM_SPEC] + [VMEM_SPEC] * (1 + len(blocks)),
        scratch_shapes=[pltpu.VMEM((nquery, half, 2 * rank), F32)],
    )(at, first, *blocks)
    gram = gram + swap(gram, 3, 0)
    return call(
        functools.partial(solve_kernel, ntrain, rank * rank, share),
        jax.ShapeDtypeStruct((share, nquery), F32),
        "solve",
        in_specs=[SMEM_SPEC] + [VMEM_SPEC] * 2,
        scratch_shapes=[pltpu.VMEM((ntrain, nquery), F32)],
    )(low, gram, swap(gram, 1, 0)).T


def solution(mesh):
    return jax.shard_map(
        functools.partial(per_device, mesh),
        mesh=mesh,
        in_specs=(
            P("dp", None, "tensor"),
            P("dp", None, "tensor"),
            P("dp", None),
            P(None, "dp", "tensor"),
            P(None, "dp", "tensor"),
            P(None, "dp"),
            P("tensor", None),
            P("tensor", None),
        ),
        out_specs=P(None, ("dp", "tensor")),
        check_vma=False,
    )
```

```python
import functools

import jax
import jax.numpy as jnp
from jax import lax
from jax.experimental import pallas as pl
from jax.experimental.pallas import tpu as pltpu
from jax.sharding import PartitionSpec as P

ITERS = 3
PAD_ID = 128004
DAMP = 0.1
HIGHEST = lax.Precision.HIGHEST
F32 = jnp.float32
VMEM_LIMIT = 32 * 1024 * 1024
NT = (((1,), (1,)), ((), ()))
SMEM_SPEC = pl.BlockSpec(memory_space=pltpu.SMEM)
VMEM_SPEC = pl.BlockSpec(memory_space=pltpu.VMEM)
HBM_SPEC = pl.BlockSpec(memory_space=pltpu.HBM)


def call(kernel, out_shape, name, **kwargs):
    return pl.pallas_call(
        kernel,
        out_shape=out_shape,
        name=name,
        compiler_params=pltpu.CompilerParams(vmem_limit_bytes=VMEM_LIMIT),
        **kwargs,
    )


def swap(value, dp_flip, tensor_flip):
    groups, parts = lax.axis_size("dp"), lax.axis_size("tensor")
    flip = dp_flip * parts + tensor_flip
    return lax.ppermute(value, ("dp", "tensor"), [(i, i ^ flip) for i in range(groups * parts)])


def project_kernel(mesh, parts, hops, tile, at_ref, th_ref, tg_ref, qh_ref, qg_ref, pin_ref, pout_ref, *refs):
    out_refs = refs[: len(hops)]
    hid, grad, pin, pout, sems = refs[len(hops) :]
    at = at_ref[0]
    trows = th_ref.shape[0] // parts
    qrows = qh_ref.shape[0] // parts
    rows = trows + qrows
    rank = pin_ref.shape[0]
    sides = ((th_ref, qh_ref, hid, pin_ref, pin), (tg_ref, qg_ref, grad, pout_ref, pout))
    chunks = []
    started = 0
    for side in (1, 0):
        train, query, buf, weight, held = sides[side]
        wide = buf.shape[1]
        first = wide if side else 6 * tile
        second = (wide - first + tile) // (2 * tile) * tile
        for start, size in ((0, first), (first, second), (first + second, wide - first - second)):
            if not size:
                continue
            cols = pl.ds(start, size)
            pairs = [] if start else [(weight, held)]
            for slot, hop in enumerate(hops):
                to = at ^ hop
                tsrc = pl.ds(pl.multiple_of(to * trows, trows), trows)
                pairs.append((train.at[tsrc, cols], buf.at[pl.ds(slot * rows, trows), cols]))
            for slot, hop in enumerate(() if start else hops):
                to = at ^ hop
                qsrc = pl.ds(pl.multiple_of(to * qrows, qrows), qrows)
                pairs.append((query.at[qsrc, :], buf.at[pl.ds(slot * rows + trows, qrows), :]))
            copies = []
            for src, dst in pairs:
                copies.append(pltpu.make_async_copy(src, dst, sems.at[started]))
                copies[-1].start()
                started += 1
            chunks.append((side, start, size, copies))

    by_rows = len(hops) > 1
    held_rows = hid.shape[0] // 2 if by_rows else hid.shape[0]

    def multiply(*sums):
        used = [0] * len(sums)
        for side in (1, 0):
            _, _, buf, _, held = sides[side]
            mine = [chunk for chunk in chunks if chunk[0] == side]
            tiles = range(0, buf.shape[1], tile)
            turns = [
                list(tiles) if by_rows else list(tiles)[unit :: len(sums)]
                for unit in range(len(sums))
            ]

            def push(unit, place):
                if place >= len(turns[unit]):
                    return
                col = turns[unit][place]
                weight = [held[:, col : col + tile]]
                if side:
                    weight.insert(0, jnp.zeros((side * rank, tile), held.dtype))
                weight.append(jnp.zeros((tile - (side + 1) * rank, tile), held.dtype))
                weight = jnp.concatenate(weight, axis=0)
                pltpu.matmul_push_rhs(weight, (used[unit] + place) % 2, unit, transpose=True)

            mine[0][3][0].wait()
            for place in range(2):
                for unit in range(len(sums)):
                    push(unit, place)
            for _, start, size, copies in mine:
                for copy in copies[0 if start else 1 :]:
                    copy.wait()
                for col in range(start, start + size, tile):
                    for unit, acc in enumerate(sums):
                        if col not in turns[unit]:
                            continue
                        place = turns[unit].index(col)
                        first = unit * held_rows if by_rows else 0
                        tokens = buf[first : first + held_rows, col : col + tile]
                        pltpu.matmul_acc_lhs(
                            acc, tokens, load_staged_rhs=(used[unit] + place) % 2
                        )
                        push(unit, place + 2)
            for unit in range(len(sums)):
                used[unit] += len(turns[unit])
        total = [pltpu.matmul_pop(acc)[:, : 2 * rank] for acc in sums]
        total = jnp.concatenate(total, axis=0) if by_rows else sum(total)
        for slot, ref in enumerate(out_refs):
            ref[...] = total[slot * rows : (slot + 1) * rows]

    with jax.sharding.use_abstract_mesh(mesh.abstract_mesh):
        sums = [pltpu.ACC(unit)((held_rows, tile), F32) for unit in range(2)]
        pl.run_scoped(multiply, *sums)


def project(mesh, at, arrays, parts, hops):
    train, _, query, _, pin, pout = arrays
    rank, ff = pin.shape
    width = pout.shape[1]
    rows = (train.shape[0] + query.shape[0]) // parts
    held = rows * len(hops)
    bf16 = jnp.bfloat16
    tile = 256
    return call(
        functools.partial(project_kernel, mesh, parts, hops, tile),
        [jax.ShapeDtypeStruct((rows, 2 * rank), F32)] * len(hops),
        "project_" + "_".join(str(hop) for hop in hops),
        in_specs=[SMEM_SPEC] + [HBM_SPEC] * 6,
        out_specs=[VMEM_SPEC] * len(hops),
        scratch_shapes=[
            pltpu.VMEM((held, ff), bf16),
            pltpu.VMEM((held, width), bf16),
            pltpu.VMEM((rank, ff), bf16),
            pltpu.VMEM((rank, width), bf16),
            pltpu.SemaphoreType.DMA((2 + 6 * len(hops),)),
        ],
        cost_estimate=pl.CostEstimate(
            flops=2 * held * (ff + width) * rank,
            bytes_accessed=2 * (held + rank) * (ff + width),
            transcendentals=0,
        ),
    )(at, *[pltpu.with_memory_space_constraint(array, pltpu.HBM) for array in arrays])


def halves(value):
    high = value.astype(jnp.bfloat16)
    return high, (value - high.astype(F32)).astype(jnp.bfloat16)


def outer_kernel(share, qshare, at_ref, quarter_ref, ids_ref, qids_ref, *refs):
    tok_refs, (keep_ref, send_ref, scratch) = refs[:-3], refs[-3:]
    at, mine = at_ref[0], quarter_ref[0]
    seq_len = ids_ref.shape[1]
    rank = tok_refs[0].shape[1] // 2
    qtok = qids_ref.shape[1]
    half = rank // 8

    def total(start, rows):
        value = tok_refs[0][start : start + rows, :]
        for ref in tok_refs[1:]:
            value = value + ref[start : start + rows, :]
        return value

    def product(lefts, tokens):
        left = jnp.concatenate([part for value in lefts for part in halves(value)], axis=0)
        right = jnp.concatenate(halves(tokens), axis=1)
        out = jnp.dot(left, right, preferred_element_type=F32)
        out = out[:, : 2 * rank] + out[:, 2 * rank :]
        sums = []
        for index in range(len(lefts)):
            start = 2 * rank * index
            sums.append(out[start : start + rank] + out[start + rank : start + 2 * rank])
        return sums

    def store(slot, outer):
        for quarter in range(4):
            start = quarter * 2 * half
            scratch[quarter, slot] = jnp.concatenate(
                [outer[start : start + half, rank:], outer[start + half : start + 2 * half, rank:]],
                axis=1,
            )

    for seq in range(share):
        tokens = total(seq * seq_len, seq_len)
        mask = (ids_ref[pl.ds(at * share + seq, 1), :] != PAD_ID).astype(F32)
        (outer,) = product([tokens.T[:rank] * mask], tokens)
        store(seq, outer / jnp.sum(mask, axis=1, keepdims=True))

    for quarter in range(4):
        scratch[quarter, share + qshare] = jnp.ones((half, 2 * rank), F32)
    tokens = total(share * seq_len, qshare * qtok)
    left = tokens.T[:rank]
    owner = lax.broadcasted_iota(jnp.int32, (1, qshare * qtok), 1) // qtok
    lefts = []
    for query in range(qshare):
        mask = (qids_ref[pl.ds(at * qshare + query, 1), :] != PAD_ID).astype(F32)
        lefts.append(left * jnp.where(owner == query, jnp.concatenate([mask] * qshare, axis=1), 0.0))
        count = jnp.broadcast_to(jnp.sum(mask, axis=1, keepdims=True), (1, 2 * rank))
        for quarter in range(4):
            scratch[quarter, share + qshare, query : query + 1, :] = count
    for query, outer in enumerate(product(lefts, tokens)):
        store(share + query, outer)
    for flip in range(2):
        keep_ref[flip] = scratch[mine ^ flip]
        send_ref[flip] = scratch[mine ^ 2 ^ flip]


def as_rows(values):
    half = values[0].shape[1]
    return jnp.concatenate(
        [
            jnp.concatenate([value[:, row, :] for value in values], axis=0) for row in range(half)
        ],
        axis=1,
    )


def rows_kernel(qshare, whole_ref, *refs):
    own = whole_ref.at[: whole_ref.shape[0] - qshare]
    refs[-1][...] = as_rows([own, *refs[:-1]])


def gram_kernel(qshare, hops, at_ref, first_ref, *refs):
    piece_refs, (out_ref, scratch) = refs[:-2], refs[-2:]
    nquery = scratch.shape[0]
    examples = []
    for hop, ref in zip(hops, piece_refs):
        nex = ref.shape[0] - qshare
        if hop:
            examples.append(ref.at[:nex])
        scratch[pl.ds((at_ref[0] ^ hop) * qshare, qshare)] = ref[nex:]
    both = jnp.concatenate([first_ref[...], as_rows([*examples, scratch])], axis=0)
    ntrain = both.shape[0] - nquery
    size = ntrain + nquery
    high, low = halves(both)
    gap = jnp.zeros((-size % 128, both.shape[1]), high.dtype)
    left = jnp.concatenate([high, low], axis=0)
    right = jnp.concatenate([high, gap, low], axis=0)
    total = lax.dot_general(left, right, NT, preferred_element_type=F32)
    total = total[:size] + total[size:]
    total = total[:, :size] + total[:, size + gap.shape[0] :]
    if folds(ntrain):
        half = ntrain // 2
        out_ref[:half, :] = jnp.concatenate([total[:half, :ntrain], total[half:ntrain, :ntrain]], axis=1)
        rest = [total[start : start + nquery, ntrain:] for start in range(0, size, nquery)]
        rest.append(jnp.zeros((nquery, 2 * ntrain - size), F32))
        out_ref[half:, :] = jnp.concatenate(rest, axis=1)
    else:
        out_ref[...] = total


def folds(ntrain):
    return 2 * ntrain <= 128


def solve_kernel(ntrain, feat, share, low_ref, one_ref, two_ref, out_ref, columns):
    nquery = out_ref.shape[1]
    whole = one_ref[...] + two_ref[...]
    if folds(ntrain):
        half = ntrain // 2
        gram = jnp.concatenate([whole[:half, :ntrain], whole[:half, ntrain:]], axis=0)
        rest = whole[half:]
        cross = [rest[:, start : start + nquery] for start in range(0, ntrain, nquery)]
        cross = jnp.concatenate(cross, axis=0)
        square = rest[:, ntrain : ntrain + nquery]
    else:
        gram = whole[:ntrain, :ntrain]
        cross = whole[:ntrain, ntrain:]
        square = whole[ntrain:, ntrain:]

    def colsum(v):
        return jnp.sum(v, axis=0, keepdims=True)

    def diagonal(v):
        rows = lax.broadcasted_iota(jnp.int32, v.shape, 0)
        cols = lax.broadcasted_iota(jnp.int32, v.shape, 1)
        return jnp.where(rows == cols, v, 0.0)

    norm = colsum(diagonal(square))
    trace = jnp.sum(colsum(diagonal(gram)), axis=1, keepdims=True) / ntrain
    scale = 1.0 / (ntrain * (DAMP * trace / feat))

    def thirds(value):
        high, rest = halves(value)
        low = value - high.astype(F32) - rest.astype(F32)
        return high, rest, low.astype(jnp.bfloat16)

    gram_parts = jnp.concatenate(thirds(gram), axis=0)

    def times_gram(value):
        out = sum(
            jnp.dot(gram_parts, part, preferred_element_type=F32) for part in thirds(value)[::-1]
        )
        return out[2 * ntrain :] + out[ntrain : 2 * ntrain] + out[:ntrain]

    res_a, res_x, res_p = jnp.ones_like(norm), jnp.zeros_like(cross), cross
    dir_a, dir_x, dir_p = res_a, res_x, res_p
    solved = jnp.zeros_like(cross)
    now = norm
    for step in range(ITERS):
        inner = dir_p * dir_p * scale
        if step:
            inner = inner + dir_x * (dir_a * cross + dir_p)
        alpha = now / (dir_a * dir_a * norm + colsum(inner))
        solved = solved + alpha * dir_p
        if step == ITERS - 1:
            break
        res_a = res_a - alpha * dir_a
        res_x = res_x - alpha * (dir_x + dir_p * scale)
        res_p = res_a * cross + times_gram(res_x)
        fresh = res_a * res_a * norm + colsum(res_x * (res_a * cross + res_p))
        beta = fresh / now
        dir_a = res_a + beta * dir_a
        dir_x = res_x + beta * dir_x
        dir_p = res_p + beta * dir_p
        now = fresh
    columns[...] = solved
    out_ref[...] = columns[pl.ds(low_ref[0] * share, share), :]


def per_device(
    mesh, train_hidden, train_grads, train_ids, query_hidden, query_grads, query_ids, proj_in, proj_out
):
    parts = lax.axis_size("tensor")
    groups = lax.axis_size("dp")
    at = lax.axis_index("tensor").astype(jnp.int32).reshape(1)
    group = lax.axis_index("dp").astype(jnp.int32)
    low = (group & 3).reshape(1)
    steady = group
    for bit in range(1, (groups - 1).bit_length()):
        steady = steady ^ (group >> bit)
    quarter = ((steady & 1) * 2 + (low >> 1)).reshape(1)
    nseq, seq_len, ff = train_hidden.shape
    width = train_grads.shape[2]
    rank = proj_in.shape[1]
    nquery, qtok, _ = query_hidden.shape
    ntrain = nseq * groups
    share = nseq // parts
    qshare = nquery // parts
    half = rank // 8

    arrays = (
        train_hidden.reshape(nseq * seq_len, ff),
        train_grads.reshape(nseq * seq_len, width),
        query_hidden.reshape(nquery * qtok, ff),
        query_grads.reshape(nquery * qtok, width),
        proj_in.T,
        proj_out.T,
    )
    pieces = {}
    turn = at
    for hops in ((3,), (2, 1), (0,)):
        values = project(mesh, turn, arrays, parts, hops)
        turn, *values = lax.optimization_barrier((turn, *values))
        for hop, value in zip(hops, values):
            pieces[hop] = swap(value, 0, hop) if hop else value

    early = pieces[3] + pieces[0]
    rows = share + qshare + 1
    keep, send = call(
        functools.partial(outer_kernel, share, qshare),
        [jax.ShapeDtypeStruct((2, rows, half, 2 * rank), F32)] * 2,
        "outer",
        in_specs=[SMEM_SPEC] * 2 + [VMEM_SPEC] * 5,
        scratch_shapes=[pltpu.VMEM((4, rows, half, 2 * rank), F32)],
    )(at, quarter, train_ids, query_ids, early, pieces[2], pieces[1])

    def ordered(bit, mine, other):
        nex = mine.shape[-3] - qshare - 1
        first = jnp.where(bit == 0, mine, other)[..., :nex, :, :]
        second = jnp.where(bit == 0, other, mine)[..., :nex, :, :]
        return jnp.concatenate([first, second, (mine + other)[..., nex:, :, :]], axis=-3)

    both = ordered(low[0] & 1, keep, swap(send, 1, 0))
    block = ordered(low[0] >> 1, both[0], swap(both[1], 3, 0))
    flip = 4
    while 2 * flip < groups:
        block = ordered(0, block, swap(block, flip | 1, 0))
        flip *= 2
    nex = block.shape[0] - qshare - 1
    own = block[:nex]
    other = swap(block, flip | 1, 0)
    ahead = {hop: swap(own, 0, hop) for hop in (2, 1)}
    rest = (block + other)[nex:]
    after = jnp.concatenate([other[:nex], rest[:qshare] / rest[qshare, :qshare, None, :]], axis=0)
    whole = jnp.concatenate([own, after], axis=0)

    far = swap(whole, 0, 3)
    behind = {
        2: swap(lax.optimization_barrier((after, ahead[2], ahead[1]))[0], 0, 2),
        1: swap(after, 0, 1),
    }
    first = call(
        functools.partial(rows_kernel, qshare),
        jax.ShapeDtypeStruct((4 * nex, half * 2 * rank), F32),
        "rows",
    )(whole, ahead[1], ahead[2])
    blocks = [whole, behind[1], far, behind[2]]
    hops = (0, 1, 3, 2)
    size = ntrain + nquery
    shape = (ntrain // 2 + nquery, 2 * ntrain) if folds(ntrain) else (size, size)
    gram = call(
        functools.partial(gram_kernel, qshare, hops),
        jax.ShapeDtypeStruct(shape, F32),
        "gram",
        in_specs=[SMEM_SPEC] + [VMEM_SPEC] * (1 + len(blocks)),
        scratch_shapes=[pltpu.VMEM((nquery, half, 2 * rank), F32)],
    )(at, first, *blocks)
    gram = gram + swap(gram, 3, 0)
    return call(
        functools.partial(solve_kernel, ntrain, rank * rank, share),
        jax.ShapeDtypeStruct((share, nquery), F32),
        "solve",
        in_specs=[SMEM_SPEC] + [VMEM_SPEC] * 2,
        scratch_shapes=[pltpu.VMEM((ntrain, nquery), F32)],
    )(low, gram, swap(gram, 1, 0)).T


def solution(mesh):
    return jax.shard_map(
        functools.partial(per_device, mesh),
        mesh=mesh,
        in_specs=(
            P("dp", None, "tensor"),
            P("dp", None, "tensor"),
            P("dp", None),
            P(None, "dp", "tensor"),
            P(None, "dp", "tensor"),
            P(None, "dp"),
            P("tensor", None),
            P("tensor", None),
        ),
        out_specs=P(None, ("dp", "tensor")),
        check_vma=False,
    )
```
